128 devices in a mesh: seq: 32 (over x, y, core), tp: 4 (over z).
Axes of the slice: x: 4, y: 4, z: 4, core: 2. Of those that a mesh axis runs over, the one named last changes fastest.
Arguments:
- tokens: bfloat16 [12288, 2560], P('seq', 'tp'), may hold values from -6 to 6
- w_query: bfloat16 [2560, 2560], P(None, 'tp'), may hold values from -0.125 to 0.125
- w_key: bfloat16 [2560, 2560], P(None, 'tp'), may hold values from -0.125 to 0.125
- w_value: bfloat16 [2560, 2560], P(None, 'tp'), may hold values from -0.125 to 0.125
- w_out: bfloat16 [2560, 2560], P('tp'), may hold values from -0.125 to 0.125
- shift_filter: float32 [64, 2560], P(None, 'tp'), may hold values from -0.75 to 0.75
- log_decay: float32 [64, 2560], P(None, 'tp'), may hold values from 8.138021e-05 to 0.03
- readout: float32 [64, 2560], P(None, 'tp'), may hold values from -3 to 3
- skip_gain: float32 [2560], P('tp'), may hold values from 0.5 to 1.5
- init_state: float32 [64, 2560], P(None, 'tp'), may hold values from -6 to 6
- cotangent: bfloat16 [12288, 2560], P('seq', 'tp'), may hold values from -6 to 6
Outputs:
- mixed: bfloat16 [12288, 2560], P('seq', 'tp')
- grad_input: bfloat16 [12288, 2560], P('seq', 'tp')
- grad_query: float32 [2560, 2560], P('seq', 'tp')
- grad_key: float32 [2560, 2560], P('seq', 'tp')
- grad_value: float32 [2560, 2560], P('seq', 'tp')
- grad_out: float32 [2560, 2560], P('tp', 'seq')
- grad_filter: float32 [64, 2560], P(None, 'tp')
- grad_init: float32 [64, 2560], P(None, 'tp')
The draws below stay inside these ranges and needn't reach their ends.
All inputs are finite; a program needn't handle non-finite values.
Results may differ from the reference program's by a relative error of at most 0.025.
Values may be sent and summed in bfloat16 or wider, within the bound.
No kernel may reach another device: no remote copies, remote signals or barrier semaphores. Data moves between devices by JAX's collectives and lax.ppermute only.
A program may use at most 192 MiB of HBM per device.

```python
import math
import jax
import jax.numpy as jnp
from jax import lax

D = 2560
NS = 64
TAPS = 64
BLK = 64
TOKENS = 12288


def shard_levels(stream_key, dims, shards, least, largest):
    factor_of = 1.0
    for axis_at, shards_of in shards:
        heights = jax.random.uniform(jax.random.fold_in(jax.random.fold_in(stream_key, 6), axis_at), (shards_of,), jnp.float32, least / len(shards), largest / len(shards))
        factor_of = factor_of * jnp.repeat(jnp.exp(heights), dims[axis_at] // shards_of).reshape((-1,) + (1,) * (len(dims) - 1 - axis_at))
    return factor_of


def bell_draw(stream_key, extent, scale, most, split=(), held_as=jnp.bfloat16):
    entries = jax.random.normal(stream_key, extent, jnp.float32) * scale
    if len(split) > 0:
        entries = shard_levels(stream_key, extent, split, -0.22, 0.18) * entries
    return jnp.clip(entries, min=-most, max=most).astype(held_as)


def setup_inputs(seed: int = 0) -> dict:
    streams_of = jax.random.split(jax.random.key(seed), 12)
    return {
        "tokens": bell_draw(streams_of[0], (TOKENS, D), 1.0, 6.0, ((0, 32), (1, 4))),
        "w_query": bell_draw(streams_of[1], (D, D), D ** -0.5, 0.125, ((1, 4),)),
        "w_key": bell_draw(streams_of[2], (D, D), D ** -0.5, 0.125, ((1, 4),)),
        "w_value": bell_draw(streams_of[3], (D, D), D ** -0.5, 0.125, ((1, 4),)),
        "w_out": bell_draw(streams_of[4], (D, D), D ** -0.5, 0.125, ((0, 4),)),
        "shift_filter": bell_draw(streams_of[5], (TAPS, D), 0.125, 0.75, ((1, 4),), jnp.float32),
        "log_decay": jnp.clip(jnp.exp(math.log(0.03) - 5.9098205 * jax.random.uniform(streams_of[6], (NS, D), jnp.float32) ** shard_levels(streams_of[6], (NS, D), ((1, 4),), -0.2, 0.2)), 8.138021075865254e-05, 0.03),
        "readout": bell_draw(streams_of[7], (NS, D), 0.5, 3.0, ((1, 4),), jnp.float32),
        "skip_gain": jnp.clip(1.0 + 0.1 * jax.random.normal(streams_of[8], (D,), jnp.float32), 0.5, 1.5),
        "init_state": bell_draw(streams_of[9], (NS, D), 1.0, 6.0, ((1, 4),), jnp.float32),
        "cotangent": bell_draw(streams_of[10], (TOKENS, D), 1.0, 6.0, ((0, 32), (1, 4))),
    }


EXACT = lax.Precision.HIGHEST


def tables(log_decay, readout, block_len):
    row_steps = jnp.arange(block_len).astype(jnp.float32)[:, None, None]
    step_decay = jnp.exp(-log_decay)
    inflow = 1.0 - step_decay
    reading = jnp.exp(-log_decay[None] * (row_steps + 1.0))
    feeding = jnp.exp(-log_decay[None] * (block_len - 1.0 - row_steps)) * inflow[None]
    kernel = jnp.sum(readout[None] * inflow[None] * jnp.exp(-log_decay[None] * row_steps), axis=1)
    offset = (jnp.arange(block_len)[:, None] - jnp.arange(block_len)[None, :]).astype(jnp.int32)
    picked = kernel[jnp.clip(offset, 0, block_len - 1)]
    toeplitz = jnp.where((offset >= 0)[:, :, None], picked, jnp.zeros_like(picked))
    return reading, feeding, toeplitz


def reference(tokens, w_query, w_key, w_value, w_out, shift_filter, log_decay, readout, skip_gain, init_state, cotangent):
    token_count = tokens.shape[0]
    channels = tokens.shape[1]
    query_rows = jnp.dot(tokens, w_query, preferred_element_type=jnp.float32).astype(jnp.bfloat16)
    key_rows = jnp.dot(tokens, w_key, preferred_element_type=jnp.float32).astype(jnp.bfloat16)
    value_rows = jnp.dot(tokens, w_value, preferred_element_type=jnp.float32).astype(jnp.bfloat16)
    extended = jnp.concatenate([jnp.zeros((TAPS - 1, channels), jnp.float32), key_rows.astype(jnp.float32)], 0)

    def tap_step(tap_index, running):
        return running + shift_filter[tap_index][None, :] * lax.dynamic_slice_in_dim(extended, TAPS - 1 - tap_index, token_count, 0)

    shifted = lax.fori_loop(0, TAPS, tap_step, jnp.zeros((token_count, channels), jnp.float32))
    value_wide = value_rows.astype(jnp.float32)
    drive_rows = shifted * value_wide
    reading, feeding, toeplitz = tables(log_decay, readout, BLK)
    block_decay = jnp.exp(-log_decay * BLK)

    def forward_step(state_carry, drive_block):
        local_part = jnp.einsum("ijc,jc->ic", toeplitz, drive_block, precision=EXACT)
        entering = jnp.einsum("inc,nc->ic", reading, readout * state_carry, precision=EXACT)
        result = local_part + entering + skip_gain[None, :] * drive_block
        state_carry = block_decay * state_carry + jnp.einsum("jnc,jc->nc", feeding, drive_block, precision=EXACT)
        return state_carry, result

    _, response = lax.scan(forward_step, init_state, drive_rows.reshape(-1, BLK, channels))
    response = response.reshape(token_count, channels)
    gated_rows = (query_rows.astype(jnp.float32) * response).astype(jnp.bfloat16)
    mixed = jnp.dot(gated_rows, w_out, preferred_element_type=jnp.float32).astype(jnp.bfloat16)
    grad_out = jnp.dot(gated_rows.T, cotangent, preferred_element_type=jnp.float32)
    grad_gated = jnp.dot(cotangent, w_out.T, preferred_element_type=jnp.float32).astype(jnp.bfloat16)
    gated_wide = grad_gated.astype(jnp.float32)
    grad_response = gated_wide * query_rows.astype(jnp.float32)
    back_query = (gated_wide * response).astype(jnp.bfloat16)

    def backward_step(state_carry, grad_block):
        local_part = jnp.einsum("jic,jc->ic", toeplitz, grad_block, precision=EXACT)
        entering = jnp.einsum("inc,nc->ic", feeding, state_carry, precision=EXACT)
        result = local_part + entering + skip_gain[None, :] * grad_block
        state_carry = block_decay * state_carry + readout * jnp.einsum("jnc,jc->nc", reading, grad_block, precision=EXACT)
        return state_carry, result

    grad_init, back_drive = lax.scan(backward_step, jnp.zeros_like(init_state), grad_response.reshape(-1, BLK, channels), reverse=True)
    back_drive = back_drive.reshape(token_count, channels)
    back_value = (back_drive * shifted).astype(jnp.bfloat16)
    back_shifted = back_drive * value_wide
    trailing = jnp.concatenate([back_shifted, jnp.zeros((TAPS - 1, channels), jnp.float32)], 0)

    def back_tap(tap_index, running):
        return running + shift_filter[tap_index][None, :] * lax.dynamic_slice_in_dim(trailing, tap_index, token_count, 0)

    back_key = lax.fori_loop(0, TAPS, back_tap, jnp.zeros((token_count, channels), jnp.float32)).astype(jnp.bfloat16)

    def filter_row(tap_index):
        return jnp.sum(back_shifted * lax.dynamic_slice_in_dim(extended, TAPS - 1 - tap_index, token_count, 0), axis=0)

    grad_filter = lax.map(filter_row, jnp.arange(TAPS).astype(jnp.int32))
    grad_input = (jnp.dot(back_query, w_query.T, preferred_element_type=jnp.float32)
                  + jnp.dot(back_key, w_key.T, preferred_element_type=jnp.float32)
                  + jnp.dot(back_value, w_value.T, preferred_element_type=jnp.float32)).astype(jnp.bfloat16)
    grad_query = jnp.dot(tokens.T, back_query, preferred_element_type=jnp.float32)
    grad_key = jnp.dot(tokens.T, back_key, preferred_element_type=jnp.float32)
    grad_value = jnp.dot(tokens.T, back_value, preferred_element_type=jnp.float32)
    return (mixed, grad_input, grad_query, grad_key, grad_value, grad_out, grad_filter, grad_init)
```

```python
import functools

import jax
import jax.numpy as jnp
from jax import lax
from jax.experimental import pallas as pl
from jax.experimental.pallas import tpu as pltpu
from jax.sharding import PartitionSpec as P

LANE = 128
F32 = jnp.float32
BF16 = jnp.bfloat16


def dot_nn(left, right):
    return lax.dot_general(left, right, (((1,), (0,)), ((), ())), preferred_element_type=F32)


def dot_nt(left, right):
    return lax.dot_general(left, right, (((1,), (1,)), ((), ())), preferred_element_type=F32)


def dot_tn(left, right):
    return lax.dot_general(left, right, (((0,), (0,)), ((), ())), preferred_element_type=F32)


def dot_tt(left, right):
    return lax.dot_general(left, right, (((0,), (1,)), ((), ())), preferred_element_type=F32)


def split_pair(value):
    high = value.astype(BF16)
    return high, (value - high.astype(F32)).astype(BF16)


SIDE = 4
MIB = 1024 * 1024


def call_cost(flops, bytes_accessed, transcendentals=0):
    return pl.CostEstimate(
        flops=flops, bytes_accessed=bytes_accessed, transcendentals=transcendentals
    )


def params(mebibytes):
    return pltpu.CompilerParams(vmem_limit_bytes=mebibytes * MIB)


def in_vmem(count):
    return [pl.BlockSpec(memory_space=pltpu.VMEM)] * count


def in_smem(count):
    return [pl.BlockSpec(memory_space=pltpu.SMEM)] * count


def anywhere(count):
    return [pl.BlockSpec(memory_space=pl.ANY)] * count


def padded(rows):
    return -(-rows // 8) * 8


def later(value, steps, source_at):
    at = source_at[:, : value.shape[1]]
    return jnp.where(at >= steps, pltpu.roll(value, steps, 0), 0.0)


def earlier(value, steps, source_at):
    sources = value.shape[0]
    at = source_at[:, : value.shape[1]]
    return jnp.where(at < sources - steps, pltpu.roll(value, sources - steps, 0), 0.0)


def circulant(row):
    return pltpu.roll(jnp.broadcast_to(row, (LANE, LANE)), 0, 1, stride=1, stride_axis=0)


def iotas(sources):
    lane_at = lax.broadcasted_iota(jnp.int32, (LANE, LANE), 1)
    row_at = lax.broadcasted_iota(jnp.int32, (LANE, LANE), 0)
    source_at = lax.broadcasted_iota(jnp.int32, (sources, LANE), 0)
    return lane_at, row_at, source_at


def decay_tables(cols_ref, channel, lane_at):
    rate = cols_ref[0, channel]
    read = cols_ref[1, channel]
    lanes = lane_at[: rate.shape[0]].astype(F32)
    step_decay = jnp.exp(-rate)
    inflow = 1.0 - step_decay
    rising = jnp.exp(-rate * lanes)
    falling = jnp.exp(-rate * (LANE - 1.0 - lanes))
    reading = (read * step_decay) * rising
    feeding = inflow * falling
    weight = read * inflow
    kernel_row = jnp.sum(weight * rising, axis=0, keepdims=True)
    wrapped = jnp.where(lanes > 0.0, step_decay * falling, 1.0)
    kernel_turned = jnp.sum(weight * wrapped, axis=0, keepdims=True)
    return reading.astype(BF16), feeding.astype(BF16), kernel_row, kernel_turned


def part_rows(value, sources):
    return [value[at : at + sources] for at in range(0, value.shape[0], sources)]


def load_rows(ref, row, sources, pad, parts):
    return [
        ref[pl.ds(row + part * sources * pad, sources, stride=pad), :] for part in range(parts)
    ]


def store_rows(ref, row, sources, pad, value):
    for part, piece in enumerate(part_rows(value, sources)):
        ref[pl.ds(row + part * sources * pad, sources, stride=pad), :] = piece


def spread(block_ref, rows_ref, pad):
    sources, count, width = block_ref.shape
    for part in range(width // LANE):
        for source in range(sources):
            row = (part * sources + source) * pad
            rows_ref[row : row + count] = block_ref[
                source, :, LANE * part : LANE * (part + 1)
            ].astype(F32)


def forward_channel(
    channel, sources, parts, group, at, kv_rows, out_rows, rows_ref, cols_ref, taps_ref, skip_ref,
    shifted_ref, value_ref, pair_ref,
):
    lane_at, row_at, source_at = at
    kv_pad, out_pad = padded(2 * group), padded(group)
    key = load_rows(kv_rows, channel, sources, kv_pad, parts)
    value = jnp.concatenate(load_rows(kv_rows, channel + group, sources, kv_pad, parts), 0)
    rate_row = rows_ref[0, pl.ds(channel, 1), :]
    start_row = rows_ref[1, pl.ds(channel, 1), :]
    states = rate_row.shape[1]
    reading, feeding, kernel_row, _ = decay_tables(cols_ref, channel, lane_at)
    ahead = lane_at >= row_at
    local = jnp.where(ahead, circulant(kernel_row), 0.0).astype(BF16)
    taps = circulant(taps_ref[0, pl.ds(channel, 1), :])
    taps_forward = jnp.concatenate(
        [jnp.where(ahead, 0.0, taps), jnp.where(ahead, taps, 0.0)], 0
    ).astype(BF16)
    part_decay = jnp.exp(-rate_row * LANE)
    row_decay = jnp.exp(-rate_row * (LANE * parts))

    key_now = jnp.concatenate(key, 0)
    key_before = jnp.concatenate([later(key[-1], 1, source_at)] + key[:-1], 0)
    key_pair = jnp.concatenate([key_before, key_now], 1).astype(BF16)
    shifted = dot_nn(key_pair, taps_forward)
    drive = shifted * value
    drive_short = drive.astype(BF16)
    shifted_ref[channel] = shifted
    value_ref[channel] = value
    pair_ref[channel] = key_pair

    fed = part_rows(dot_nt(drive_short, feeding), sources)
    whole = fed[0]
    for part in range(1, parts):
        whole = part_decay * whole + fed[part]
    scan = jnp.where(source_at[:, :states] >= 1, pltpu.roll(whole, 1, 0), start_row)
    step, decay = 1, row_decay
    while step < sources:
        scan = scan + decay * later(scan, step, source_at)
        step, decay = 2 * step, decay * decay
    entering = [scan]
    for part in range(1, parts):
        entering.append(part_decay * entering[-1] + fed[part - 1])
    state_high, state_low = split_pair(jnp.concatenate(entering, 0))
    response = (
        dot_nn(
            jnp.concatenate([drive_short, state_high, state_low], 1),
            jnp.concatenate([local, reading, reading], 0),
        )
        + skip_ref[channel] * drive
    )
    store_rows(out_rows, channel, sources, out_pad, response)


def backward_channel(
    channel, sources, parts, group, at, grad_rows, out_rows, small_rows, rows_ref, cols_ref,
    taps_ref, skip_ref, shifted_ref, value_ref, pair_ref,
):
    lane_at, row_at, source_at = at
    grad_pad, out_pad = padded(group), padded(2 * group)
    grads = jnp.concatenate(load_rows(grad_rows, channel, sources, grad_pad, parts), 0)
    shifted, value, key_pair = shifted_ref[channel], value_ref[channel], pair_ref[channel]
    rate_row = rows_ref[0, pl.ds(channel, 1), :]
    states = rate_row.shape[1]
    reading, feeding, _, kernel_turned = decay_tables(cols_ref, channel, lane_at)
    behind = lane_at <= row_at
    local_turned = jnp.where(behind, circulant(kernel_turned), 0.0).astype(BF16)
    taps_turned = circulant(taps_ref[1, pl.ds(channel, 1), :])
    taps_back = jnp.concatenate(
        [jnp.where(behind, taps_turned, 0.0), jnp.where(behind, 0.0, taps_turned)], 0
    ).astype(BF16)
    part_decay = jnp.exp(-rate_row * LANE)
    row_decay = jnp.exp(-rate_row * (LANE * parts))

    grad_short = grads.astype(BF16)
    read = part_rows(dot_nt(grad_short, reading), sources)
    whole = read[-1]
    for part in range(parts - 2, -1, -1):
        whole = part_decay * whole + read[part]
    scan = earlier(whole, 1, source_at)
    step, decay = 1, row_decay
    while step < sources:
        scan = scan + decay * earlier(scan, step, source_at)
        step, decay = 2 * step, decay * decay
    leaving = [scan]
    for part in range(parts - 1, 0, -1):
        leaving.insert(0, part_decay * leaving[0] + read[part])
    start_grad = (part_decay * leaving[0] + read[0])[0:1]
    carry_high, carry_low = split_pair(jnp.concatenate(leaving, 0))
    back_drive = (
        dot_nn(
            jnp.concatenate([grad_short, carry_high, carry_low], 1),
            jnp.concatenate([local_turned, feeding, feeding], 0),
        )
        + skip_ref[channel] * grads
    )
    back_value = back_drive * shifted
    back_shifted = back_drive * value
    pieces = part_rows(back_shifted, sources)
    back_after = jnp.concatenate(pieces[1:] + [earlier(pieces[0], 1, source_at)], 0)
    back_short = back_shifted.astype(BF16)
    back_pair = jnp.concatenate([back_short, back_after.astype(BF16)], 1)
    back_key = dot_nn(back_pair, taps_back)

    gram = dot_tn(key_pair, back_short)
    gram = jnp.where(lane_at >= row_at, gram[LANE:], gram[:LANE])
    aligned = gram[:8]
    for first in range(8, LANE, 8):
        aligned = aligned + pltpu.roll(gram[first : first + 8], LANE - first, 1)
    for bit in (1, 2, 4):
        aligned = jnp.where((row_at[:8] & bit) > 0, pltpu.roll(aligned, LANE - bit, 1), aligned)
    filter_grad = jnp.sum(aligned, axis=0, keepdims=True)[:, : LANE - states]
    small_rows[pl.ds(channel, 1), :] = jnp.concatenate([filter_grad, start_grad], 1)
    store_rows(out_rows, channel, sources, out_pad, back_value)
    store_rows(out_rows, channel + group, sources, out_pad, back_key)


UNROLL = 4


def each_channel(group, body):
    def step(index, carry):
        for inner in range(UNROLL):
            body(index * UNROLL + inner)
        return carry

    lax.fori_loop(0, group // UNROLL, step, 0)


def forward_kernel(
    group, after_ref, kv_ref, rows_ref, cols_ref, taps_ref, skip_ref, out_ref, shifted_ref,
    value_ref, pair_ref, kv_rows, out_rows,
):
    sources, _, width = kv_ref.shape
    parts = width // LANE
    spread(kv_ref, kv_rows, padded(2 * group))
    at = iotas(sources)
    each_channel(
        group,
        lambda channel: forward_channel(
            channel, sources, parts, group, at, kv_rows, out_rows, rows_ref, cols_ref, taps_ref,
            skip_ref, shifted_ref, value_ref, pair_ref,
        ),
    )
    out_pad = padded(group)
    for part in range(parts):
        for source in range(sources):
            row = (part * sources + source) * out_pad
            out_ref[source, :, LANE * part : LANE * (part + 1)] = out_rows[
                row : row + group
            ].astype(BF16)


def forward_part(after, kv, rows, cols, taps, skip):
    sources, double, width = kv.shape
    group = double // 2
    lines = sources * width // LANE
    return pl.pallas_call(
        functools.partial(forward_kernel, group),
        out_shape=(
            jax.ShapeDtypeStruct((sources, group, width), BF16),
            jax.ShapeDtypeStruct((group, lines, LANE), F32),
            jax.ShapeDtypeStruct((group, lines, LANE), F32),
            jax.ShapeDtypeStruct((group, lines, 2 * LANE), BF16),
        ),
        in_specs=anywhere(1) + in_vmem(4) + in_smem(1),
        out_specs=tuple(in_vmem(4)),
        scratch_shapes=[
            pltpu.VMEM((lines * padded(2 * group), LANE), F32),
            pltpu.VMEM((lines * padded(group), LANE), F32),
        ],
        compiler_params=params(16),
        cost_estimate=call_cost(9_000_000_000, 5_000_000),
    )(after, kv, rows, cols, taps, skip)


def backward_kernel(
    group, grad_ref, shifted_ref, value_ref, pair_ref, rows_ref, cols_ref, taps_ref, skip_ref,
    out_ref, grad_rows, out_rows, small_rows,
):
    sources, _, width = grad_ref.shape
    parts = width // LANE
    spread(grad_ref, grad_rows, padded(group))
    small_rows[...] = jnp.zeros_like(small_rows)
    at = iotas(sources)
    each_channel(
        group,
        lambda channel: backward_channel(
            channel, sources, parts, group, at, grad_rows, out_rows, small_rows, rows_ref,
            cols_ref, taps_ref, skip_ref, shifted_ref, value_ref, pair_ref,
        ),
    )
    out_pad = padded(2 * group)
    extra = out_ref.shape[1] - 2 * group
    for part in range(parts):
        small = small_rows[extra * part : extra * (part + 1)].astype(BF16)
        for source in range(sources):
            row = (part * sources + source) * out_pad
            columns = slice(LANE * part, LANE * (part + 1))
            out_ref[source, : 2 * group, columns] = out_rows[row : row + 2 * group].astype(BF16)
            out_ref[source, 2 * group :, columns] = small


def backward_part(grads, shifted, value, pair, rows, cols, taps, skip):
    sources, group, width = grads.shape
    parts = width // LANE
    lines = sources * parts
    extra = -(-group // parts)
    return pl.pallas_call(
        functools.partial(backward_kernel, group),
        out_shape=jax.ShapeDtypeStruct((sources, 2 * group + extra, width), BF16),
        in_specs=in_vmem(7) + in_smem(1),
        out_specs=in_vmem(1)[0],
        scratch_shapes=[
            pltpu.VMEM((lines * padded(group), LANE), F32),
            pltpu.VMEM((lines * padded(2 * group), LANE), F32),
            pltpu.VMEM((padded(extra * parts), LANE), F32),
        ],
        compiler_params=params(18),
        cost_estimate=call_cost(12_000_000_000, 5_000_000),
    )(grads, shifted, value, pair, rows, cols, taps, skip)


def projected(shards_ref, ids_ref, weight_ref, total_ref):
    count, _, depth = shards_ref.shape
    for tile in range(count):
        first = pl.multiple_of(ids_ref[tile] * depth, depth)
        part = dot_nn(shards_ref[tile], weight_ref[pl.ds(first, depth), :])
        if tile == 0:
            total_ref[...] = part
        else:
            total_ref[...] += part


def key_value_kernel(
    group, shards_ref, key_ref, value_ref, ids_ref, kv_ref, turned_ref, total, across, packed,
):
    pad = padded(2 * group)
    owners = kv_ref.shape[0]
    for index, weight_ref in enumerate((key_ref, value_ref)):
        projected(shards_ref, ids_ref, weight_ref, total)
        across[...] = total[...].T
        for owner in range(owners):
            first = owner * pad + index * group
            packed[first : first + group] = across[owner * group : (owner + 1) * group]
    for owner in range(owners):
        kv_ref[owner] = packed[owner * pad : owner * pad + 2 * group].astype(BF16)
    for tile in range(shards_ref.shape[0]):
        turned_ref[tile] = shards_ref[tile].T


def key_value_part(shards, ids, w_key, w_value, owners):
    count, rows, depth = shards.shape
    channels = w_key.shape[1]
    group = channels // owners
    return pl.pallas_call(
        functools.partial(key_value_kernel, group),
        in_specs=in_vmem(3) + in_smem(1),
        out_specs=tuple(in_vmem(2)),
        out_shape=(
            jax.ShapeDtypeStruct((owners, 2 * group, rows), BF16),
            jax.ShapeDtypeStruct((count, depth, rows), BF16),
        ),
        scratch_shapes=[
            pltpu.VMEM((rows, channels), F32),
            pltpu.VMEM((channels, rows), F32),
            pltpu.VMEM((owners * padded(2 * group), rows), F32),
        ],
        compiler_params=params(24),
        cost_estimate=call_cost(4 * count * rows * depth * channels, 12_000_000),
    )(shards, w_key, w_value, ids)


def query_kernel(after_ref, shards_ref, weight_ref, ids_ref, query_ref, total):
    projected(shards_ref, ids_ref, weight_ref, total)
    query_ref[...] = total[...].astype(BF16)


def query_part(after, shards, ids, w_query):
    count, rows, depth = shards.shape
    channels = w_query.shape[1]
    return pl.pallas_call(
        query_kernel,
        in_specs=anywhere(1) + in_vmem(2) + in_smem(1),
        out_specs=in_vmem(1)[0],
        out_shape=jax.ShapeDtypeStruct((rows, channels), BF16),
        scratch_shapes=[pltpu.VMEM((rows, channels), F32)],
        compiler_params=params(14),
        cost_estimate=call_cost(2 * count * rows * depth * channels, 6_000_000),
    )(after, shards, w_query, ids)


def gated_grad_kernel(
    group, after_ref, shards_ref, weight_ref, query_ref, gated_ref, grouped_ref, turned_ref,
    total, across,
):
    count, _, depth = shards_ref.shape
    for tile in range(count):
        part = dot_nt(shards_ref[tile], weight_ref[:, tile * depth : (tile + 1) * depth])
        if tile == 0:
            total[...] = part
        else:
            total[...] += part
    gated = total[...].astype(BF16)
    gated_ref[...] = gated
    across[...] = (gated.astype(F32) * query_ref[...].astype(F32)).T
    for owner in range(grouped_ref.shape[0]):
        grouped_ref[owner] = across[owner * group : (owner + 1) * group].astype(BF16)
    for tile in range(count):
        turned_ref[tile] = shards_ref[tile].T


def gated_grad_part(after, shards, w_out, query, owners):
    count, rows, depth = shards.shape
    channels = w_out.shape[0]
    group = channels // owners
    return pl.pallas_call(
        functools.partial(gated_grad_kernel, group),
        in_specs=anywhere(1) + in_vmem(3),
        out_specs=tuple(in_vmem(3)),
        out_shape=(
            jax.ShapeDtypeStruct((rows, channels), BF16),
            jax.ShapeDtypeStruct((owners, group, rows), BF16),
            jax.ShapeDtypeStruct((count, depth, rows), BF16),
        ),
        scratch_shapes=[pltpu.VMEM((rows, channels), F32), pltpu.VMEM((channels, rows), F32)],
        compiler_params=params(18),
        cost_estimate=call_cost(2 * count * rows * depth * channels, 9_000_000),
    )(after, shards, w_out, query)


def response_kernel(
    group, returned_ref, query_ref, gated_ref, forward_ref, query_grad_ref, across
):
    for owner in range(returned_ref.shape[0]):
        across[owner * group : (owner + 1) * group] = returned_ref[owner].astype(F32)
    response = across[...].T
    forward_ref[...] = (query_ref[...].astype(F32) * response).astype(BF16)
    query_grad_ref[...] = (gated_ref[...].astype(F32) * response).astype(BF16)


def response_part(returned, query, gated):
    rows, channels = query.shape
    return pl.pallas_call(
        functools.partial(response_kernel, returned.shape[1]),
        in_specs=in_vmem(3),
        out_specs=tuple(in_vmem(2)),
        out_shape=(jax.ShapeDtypeStruct((rows, channels), BF16),) * 2,
        scratch_shapes=[pltpu.VMEM((channels, rows), F32)],
        compiler_params=params(8),
        cost_estimate=call_cost(4 * rows * channels, 3_000_000),
    )(returned, query, gated)


def back_kernel(group, returned_ref, value_ref, key_ref, value_rows, key_rows):
    for owner in range(returned_ref.shape[0]):
        piece = returned_ref[owner].astype(F32)
        value_rows[owner * group : (owner + 1) * group] = piece[:group]
        key_rows[owner * group : (owner + 1) * group] = piece[group : 2 * group]
    value_ref[...] = value_rows[...].T.astype(BF16)
    key_ref[...] = key_rows[...].T.astype(BF16)


def back_part(returned, channels):
    owners, _, rows = returned.shape
    return pl.pallas_call(
        functools.partial(back_kernel, channels // owners),
        in_specs=in_vmem(1),
        out_specs=tuple(in_vmem(2)),
        out_shape=(jax.ShapeDtypeStruct((rows, channels), BF16),) * 2,
        scratch_shapes=[pltpu.VMEM((channels, rows), F32)] * 2,
        compiler_params=params(8),
        cost_estimate=call_cost(4 * rows * channels, 3_000_000),
    )(returned)


def weight_kernel(rows, after_ref, wide_ref, narrow_ref, ids_ref, core_ref, keep_ref, send_ref):
    tiles = wide_ref.shape[0]
    held = keep_ref.shape[0] // tiles
    for tile in range(tiles):
        result = dot_nn(wide_ref[tile], narrow_ref[...]).astype(BF16)
        first = ids_ref[tile] * held
        for core in range(2):

            @pl.when(core_ref[0] == core)
            def _():
                for chip in range(held):
                    at = (2 * chip + core) * rows
                    other = (2 * chip + 1 - core) * rows
                    keep_ref[first + chip] = result[at : at + rows]
                    send_ref[first + chip] = result[other : other + rows]


def weight_partial(after, wide, ids, narrow, core, chips):
    tiles, height, depth = wide.shape
    width = narrow.shape[1]
    total = tiles * height
    rows = total // (2 * chips)
    return pl.pallas_call(
        functools.partial(weight_kernel, rows),
        in_specs=anywhere(1) + in_vmem(2) + in_smem(2),
        out_specs=tuple(in_vmem(2)),
        out_shape=(jax.ShapeDtypeStruct((chips, rows, width), BF16),) * 2,
        compiler_params=params(14),
        cost_estimate=call_cost(2 * total * depth * width, 6_000_000),
    )(after, wide, narrow, ids, core)


def mixed_kernel(after_ref, gated_ref, weight_ref, out_ref):
    count, _, width = out_ref.shape
    for tile in range(count):
        out_ref[tile] = dot_nn(
            gated_ref[...], weight_ref[:, tile * width : (tile + 1) * width]
        ).astype(BF16)


def mixed_part(after, gated, w_out, count):
    rows, depth = gated.shape
    width = w_out.shape[1] // count
    return pl.pallas_call(
        mixed_kernel,
        in_specs=anywhere(1) + in_vmem(2),
        out_specs=in_vmem(1)[0],
        out_shape=jax.ShapeDtypeStruct((count, rows, width), BF16),
        compiler_params=params(12),
        cost_estimate=call_cost(2 * rows * depth * width * count, 6_000_000),
    )(after, gated, w_out)


def input_kernel(after_ref, *refs):
    out_ref = refs[-1]
    half = (len(refs) - 1) // 2
    count, _, width = out_ref.shape
    for tile in range(count):
        at = slice(tile * width, (tile + 1) * width)
        total = dot_nt(refs[0][...], refs[half][at])
        for index in range(1, half):
            total += dot_nt(refs[index][...], refs[half + index][at])
        out_ref[tile] = total.astype(BF16)


def input_part(after, backs, weights, count):
    rows, depth = backs[0].shape
    width = weights[0].shape[0] // count
    return pl.pallas_call(
        input_kernel,
        in_specs=anywhere(1) + in_vmem(len(backs) + len(weights)),
        out_specs=in_vmem(1)[0],
        out_shape=jax.ShapeDtypeStruct((count, rows, width), BF16),
        compiler_params=params(20),
        cost_estimate=call_cost(6 * rows * depth * width * count, 14_000_000),
    )(after, *backs, *weights)


def moved(value, axis, steps):
    by_core = steps if isinstance(steps, tuple) else (steps, steps)
    pairs = []
    for x in range(SIDE):
        for y in range(SIDE):
            for core in range(2):
                for z in range(SIDE):
                    goal = [x, y, core, z]
                    if axis == "core":
                        goal[2] = 1 - core
                    else:
                        at = {"x": 0, "y": 1, "z": 3}[axis]
                        goal[at] = (goal[at] + by_core[core]) % SIDE
                    pairs.append(
                        tuple(
                            ((a * SIDE + b) * 2 + c) * SIDE + d
                            for a, b, c, d in ((x, y, core, z), goal)
                        )
                    )
    return lax.ppermute(value, ("seq", "tp"), pairs)


def first_kernel(along_x, keep_ref, came_ref, place_ref, up_ref, down_ref, mine_ref, near_ref):
    place = place_ref[0]
    half = SIDE // 2

    def block(chip, row):
        at = chip * SIDE + row if along_x else row * SIDE + chip
        return keep_ref[at].astype(F32) + came_ref[at].astype(F32)

    above, below, far = (lax.rem(place + step, SIDE) for step in (1, 3, 2))
    for row in range(half):
        up_ref[row] = block(far, row).astype(BF16)
        up_ref[half + row] = block(above, half + row).astype(BF16)
        down_ref[row] = block(below, row).astype(BF16)
        down_ref[half + row] = block(far, half + row).astype(BF16)
        near_ref[row] = block(above, row)
        near_ref[half + row] = block(below, half + row)
        mine_ref[row] = block(place, row)
        mine_ref[half + row] = block(place, half + row)


def first_part(keep, came, place, along_x):
    _, rows, width = keep.shape
    short = jax.ShapeDtypeStruct((SIDE, rows, width), BF16)
    wide = jax.ShapeDtypeStruct((SIDE, rows, width), F32)
    return pl.pallas_call(
        functools.partial(first_kernel, along_x),
        in_specs=in_vmem(2) + in_smem(1),
        out_specs=tuple(in_vmem(4)),
        out_shape=(short, short, wide, wide),
        compiler_params=params(12),
        cost_estimate=call_cost(2 * SIDE * SIDE * rows * width, 6_000_000),
    )(keep, came, place.reshape(1))


def second_kernel(near_ref, up_ref, down_ref, up_out, down_out):
    half = SIDE // 2
    for row in range(half):
        up_out[row] = (near_ref[row] + up_ref[row].astype(F32)).astype(BF16)
        down_out[row] = (near_ref[half + row] + down_ref[half + row].astype(F32)).astype(BF16)


def second_part(near, came_up, came_down):
    _, rows, width = near.shape
    out = jax.ShapeDtypeStruct((SIDE // 2, rows, width), BF16)
    return pl.pallas_call(
        second_kernel,
        in_specs=in_vmem(3),
        out_specs=tuple(in_vmem(2)),
        out_shape=(out, out),
        compiler_params=params(8),
        cost_estimate=call_cost(SIDE * rows * width, 2_000_000),
    )(near, came_up, came_down)


def third_kernel(
    mine_ref, up_ref, down_ref, up_more, down_more, place_ref, own_out, above_out, below_out,
    far_out, sums,
):
    half = SIDE // 2
    for row in range(half):
        sums[row] = mine_ref[row] + down_ref[row].astype(F32) + up_more[row].astype(F32)
        sums[half + row] = (
            mine_ref[half + row] + up_ref[half + row].astype(F32) + down_more[row].astype(F32)
        )
    place = place_ref[0]
    own_out[...] = sums[place]
    above_out[...] = sums[lax.rem(place + 1, SIDE)].astype(BF16)
    below_out[...] = sums[lax.rem(place + 3, SIDE)].astype(BF16)
    far_out[...] = sums[lax.rem(place + 2, SIDE)].astype(BF16)


def third_part(mine, came_up, came_down, more_up, more_down, place):
    _, rows, width = mine.shape
    short = jax.ShapeDtypeStruct((rows, width), BF16)
    return pl.pallas_call(
        third_kernel,
        in_specs=in_vmem(5) + in_smem(1),
        out_specs=tuple(in_vmem(4)),
        out_shape=(jax.ShapeDtypeStruct((rows, width), F32), short, short, short),
        scratch_shapes=[pltpu.VMEM((SIDE, rows, width), F32)],
        compiler_params=params(8),
        cost_estimate=call_cost(2 * SIDE * rows * width, 3_000_000),
    )(mine, came_up, came_down, more_up, more_down, place.reshape(1))


def summed_over_seq(keep, send, first, places):
    second = "y" if first == "x" else "x"
    came = moved(send, "core", 1)
    up, down, mine, near = first_part(keep, came, places[first], first == "x")
    came_up, came_down = moved(up, first, 1), moved(down, first, -1)
    more_up, more_down = second_part(near, came_up, came_down)
    more_up, more_down = moved(more_up, first, 1), moved(more_down, first, -1)
    own, above, below, far = third_part(
        mine, came_up, came_down, more_up, more_down, places[second]
    )
    return (
        own
        + moved(above, second, 1).astype(F32)
        + moved(below, second, -1).astype(F32)
        + moved(far, second, (2, -2)).astype(F32)
    )


def per_device(
    tokens,
    w_query,
    w_key,
    w_value,
    w_out,
    shift_filter,
    log_decay,
    readout,
    skip_gain,
    init_state,
    cotangent,
):
    row_count = tokens.shape[0]
    channels = w_query.shape[1]
    tap_count = shift_filter.shape[0]
    seq_count = lax.axis_size("seq")
    group = channels // seq_count
    position = lax.axis_index("seq")
    core = position % 2
    chip_z = lax.axis_index("tp")
    places = {"x": position // (2 * SIDE), "y": (position // 2) % SIDE}
    core_word = core.reshape(1)

    from_below, from_above = moved(tokens, "z", 1), moved(tokens, "z", -1)
    passed_on = jnp.where(core == 0, from_below, from_above)
    cotangent, passed_on = lax.optimization_barrier((cotangent, passed_on))
    from_far = moved(passed_on, "z", (1, -1))
    grad_shards = lax.all_gather(cotangent, "tp", axis=0, tiled=False)
    shards = jnp.stack([tokens, from_below, from_above, from_far])
    in_order = jnp.arange(SIDE, dtype=jnp.int32)
    ids = (chip_z + jnp.array([0, SIDE - 1, 1, 2], jnp.int32)) % SIDE

    def own(value):
        return lax.dynamic_slice_in_dim(value, position * group, group, value.ndim - 1)

    own_rate, own_read, own_init, own_taps = (
        own(value).T for value in (log_decay, readout, init_state, shift_filter)
    )
    own_taps = jnp.pad(own_taps, ((0, 0), (0, LANE - tap_count)))
    taps = jnp.stack([own_taps, jnp.roll(own_taps[:, ::-1], 1, axis=1)])
    rows = jnp.stack([own_rate, own_init])
    cols = jnp.stack([own_rate, own_read])[..., None]
    skip = own(skip_gain)

    def exchanged(value):
        return lax.all_to_all(value, "seq", 0, 0, tiled=True)

    kv, shards_turned = key_value_part(shards, ids, w_key, w_value, seq_count)
    query = query_part(kv, shards, ids, w_query)
    kv = exchanged(kv)
    gated_grad, grads, grad_turned = gated_grad_part(kv, grad_shards, w_out, query, seq_count)
    response, shifted, value, pair = forward_part(grads, kv, rows, cols, taps, skip)
    grads = exchanged(grads)
    response = exchanged(response)
    backs = backward_part(grads, shifted, value, pair, rows, cols, taps, skip)
    backs = exchanged(backs)

    gated, back_query = response_part(response, query, gated_grad)
    chips = SIDE * SIDE

    def weight(after, wide, order, narrow):
        return weight_partial(after, wide, order, narrow, core_word, chips)

    out_keep, out_send = weight(gated, grad_turned, in_order, gated)
    query_keep, query_send = weight(out_send, shards_turned, ids, back_query)
    partial_mixed = mixed_part(query_send, gated, w_out, SIDE)
    mixed = lax.psum_scatter(partial_mixed, "tp", scatter_dimension=0, tiled=True)[0]

    back_value, back_key = back_part(backs, channels)
    key_keep, key_send = weight(partial_mixed, shards_turned, ids, back_key)
    value_keep, value_send = weight(key_send, shards_turned, ids, back_value)
    partial_input = input_part(
        value_send, (back_query, back_key, back_value), (w_query, w_key, w_value), SIDE
    )
    grad_input = lax.psum_scatter(partial_input, "tp", scatter_dimension=0, tiled=True)[0]

    small = backs[:, 2 * group :].reshape(seq_count, -1, row_count // LANE, LANE)
    small = small.transpose(0, 2, 1, 3).reshape(seq_count, -1, LANE)[:, :group]
    small = small.reshape(channels, LANE).T.astype(F32)
    grad_filter, grad_init = small[:tap_count], small[tap_count:]

    grad_out = summed_over_seq(out_keep, out_send, "x", places).T
    grad_query = summed_over_seq(query_keep, query_send, "y", places)
    grad_key = summed_over_seq(key_keep, key_send, "x", places)
    grad_value = summed_over_seq(value_keep, value_send, "y", places)
    return (mixed, grad_input, grad_query, grad_key, grad_value, grad_out, grad_filter, grad_init)


def solution(mesh):
    return jax.shard_map(
        per_device,
        mesh=mesh,
        in_specs=(
            P("seq", "tp"),
            P(None, "tp"),
            P(None, "tp"),
            P(None, "tp"),
            P("tp", None),
            P(None, "tp"),
            P(None, "tp"),
            P(None, "tp"),
            P("tp"),
            P(None, "tp"),
            P("seq", "tp"),
        ),
        out_specs=(
            P("seq", "tp"),
            P("seq", "tp"),
            P("seq", "tp"),
            P("seq", "tp"),
            P("seq", "tp"),
            P("tp", "seq"),
            P(None, "tp"),
            P(None, "tp"),
        ),
        check_vma=False,
    )
```

```python
import functools

import jax
import jax.numpy as jnp
from jax import lax
from jax.experimental import pallas as pl
from jax.experimental.pallas import tpu as pltpu
from jax.sharding import PartitionSpec as P

LANE = 128
F32 = jnp.float32
BF16 = jnp.bfloat16


def dot_nn(left, right):
    return lax.dot_general(left, right, (((1,), (0,)), ((), ())), preferred_element_type=F32)


def dot_nt(left, right):
    return lax.dot_general(left, right, (((1,), (1,)), ((), ())), preferred_element_type=F32)


def dot_tn(left, right):
    return lax.dot_general(left, right, (((0,), (0,)), ((), ())), preferred_element_type=F32)


def dot_tt(left, right):
    return lax.dot_general(left, right, (((0,), (1,)), ((), ())), preferred_element_type=F32)


def split_pair(value):
    high = value.astype(BF16)
    return high, (value - high.astype(F32)).astype(BF16)


SIDE = 4
MIB = 1024 * 1024


def call_cost(flops, bytes_accessed, transcendentals=0):
    return pl.CostEstimate(
        flops=flops, bytes_accessed=bytes_accessed, transcendentals=transcendentals
    )


def params(mebibytes):
    return pltpu.CompilerParams(vmem_limit_bytes=mebibytes * MIB)


def in_vmem(count):
    return [pl.BlockSpec(memory_space=pltpu.VMEM)] * count


def in_smem(count):
    return [pl.BlockSpec(memory_space=pltpu.SMEM)] * count


def anywhere(count):
    return [pl.BlockSpec(memory_space=pl.ANY)] * count


def padded(rows):
    return -(-rows // 8) * 8


def later(value, steps, source_at):
    at = source_at[:, : value.shape[1]]
    return jnp.where(at >= steps, pltpu.roll(value, steps, 0), 0.0)


def earlier(value, steps, source_at):
    sources = value.shape[0]
    at = source_at[:, : value.shape[1]]
    return jnp.where(at < sources - steps, pltpu.roll(value, sources - steps, 0), 0.0)


def circulant(row):
    return pltpu.roll(jnp.broadcast_to(row, (LANE, LANE)), 0, 1, stride=1, stride_axis=0)


def iotas(sources):
    lane_at = lax.broadcasted_iota(jnp.int32, (LANE, LANE), 1)
    row_at = lax.broadcasted_iota(jnp.int32, (LANE, LANE), 0)
    source_at = lax.broadcasted_iota(jnp.int32, (sources, LANE), 0)
    return lane_at, row_at, source_at


def decay_tables(cols_ref, channel, lane_at):
    rate = cols_ref[0, channel]
    read = cols_ref[1, channel]
    lanes = lane_at[: rate.shape[0]].astype(F32)
    step_decay = jnp.exp(-rate)
    inflow = 1.0 - step_decay
    rising = jnp.exp(-rate * lanes)
    falling = jnp.exp(-rate * (LANE - 1.0 - lanes))
    reading = (read * step_decay) * rising
    feeding = inflow * falling
    weight = read * inflow
    kernel_row = jnp.sum(weight * rising, axis=0, keepdims=True)
    wrapped = jnp.where(lanes > 0.0, step_decay * falling, 1.0)
    kernel_turned = jnp.sum(weight * wrapped, axis=0, keepdims=True)
    return reading.astype(BF16), feeding.astype(BF16), kernel_row, kernel_turned


def part_rows(value, sources):
    return [value[at : at + sources] for at in range(0, value.shape[0], sources)]


def load_rows(ref, row, sources, pad, parts):
    return [
        ref[pl.ds(row + part * sources * pad, sources, stride=pad), :] for part in range(parts)
    ]


def store_rows(ref, row, sources, pad, value):
    for part, piece in enumerate(part_rows(value, sources)):
        ref[pl.ds(row + part * sources * pad, sources, stride=pad), :] = piece


def spread(block_ref, rows_ref, pad):
    sources, count, width = block_ref.shape
    for part in range(width // LANE):
        for source in range(sources):
            row = (part * sources + source) * pad
            rows_ref[row : row + count] = block_ref[
                source, :, LANE * part : LANE * (part + 1)
            ].astype(F32)


def forward_channel(
    channel, sources, parts, group, at, kv_rows, out_rows, rows_ref, cols_ref, taps_ref, skip_ref,
    shifted_ref, value_ref, pair_ref,
):
    lane_at, row_at, source_at = at
    kv_pad, out_pad = padded(2 * group), padded(group)
    key = load_rows(kv_rows, channel, sources, kv_pad, parts)
    value = jnp.concatenate(load_rows(kv_rows, channel + group, sources, kv_pad, parts), 0)
    rate_row = rows_ref[0, pl.ds(channel, 1), :]
    start_row = rows_ref[1, pl.ds(channel, 1), :]
    states = rate_row.shape[1]
    reading, feeding, kernel_row, _ = decay_tables(cols_ref, channel, lane_at)
    ahead = lane_at >= row_at
    local = jnp.where(ahead, circulant(kernel_row), 0.0).astype(BF16)
    taps = circulant(taps_ref[0, pl.ds(channel, 1), :])
    taps_forward = jnp.concatenate(
        [jnp.where(ahead, 0.0, taps), jnp.where(ahead, taps, 0.0)], 0
    ).astype(BF16)
    part_decay = jnp.exp(-rate_row * LANE)
    row_decay = jnp.exp(-rate_row * (LANE * parts))

    key_now = jnp.concatenate(key, 0)
    key_before = jnp.concatenate([later(key[-1], 1, source_at)] + key[:-1], 0)
    key_pair = jnp.concatenate([key_before, key_now], 1).astype(BF16)
    shifted = dot_nn(key_pair, taps_forward)
    drive = shifted * value
    drive_short = drive.astype(BF16)
    shifted_ref[channel] = shifted
    value_ref[channel] = value
    pair_ref[channel] = key_pair

    fed = part_rows(dot_nt(drive_short, feeding), sources)
    whole = fed[0]
    for part in range(1, parts):
        whole = part_decay * whole + fed[part]
    scan = jnp.where(source_at[:, :states] >= 1, pltpu.roll(whole, 1, 0), start_row)
    step, decay = 1, row_decay
    while step < sources:
        scan = scan + decay * later(scan, step, source_at)
        step, decay = 2 * step, decay * decay
    entering = [scan]
    for part in range(1, parts):
        entering.append(part_decay * entering[-1] + fed[part - 1])
    state_high, state_low = split_pair(jnp.concatenate(entering, 0))
    response = (
        dot_nn(
            jnp.concatenate([drive_short, state_high, state_low], 1),
            jnp.concatenate([local, reading, reading], 0),
        )
        + skip_ref[channel] * drive
    )
    store_rows(out_rows, channel, sources, out_pad, response)


def backward_channel(
    channel, sources, parts, group, at, grad_rows, out_rows, small_rows, rows_ref, cols_ref,
    taps_ref, skip_ref, shifted_ref, value_ref, pair_ref,
):
    lane_at, row_at, source_at = at
    grad_pad, out_pad = padded(group), padded(2 * group)
    grads = jnp.concatenate(load_rows(grad_rows, channel, sources, grad_pad, parts), 0)
    shifted, value, key_pair = shifted_ref[channel], value_ref[channel], pair_ref[channel]
    rate_row = rows_ref[0, pl.ds(channel, 1), :]
    states = rate_row.shape[1]
    reading, feeding, _, kernel_turned = decay_tables(cols_ref, channel, lane_at)
    behind = lane_at <= row_at
    local_turned = jnp.where(behind, circulant(kernel_turned), 0.0).astype(BF16)
    taps_turned = circulant(taps_ref[1, pl.ds(channel, 1), :])
    taps_back = jnp.concatenate(
        [jnp.where(behind, taps_turned, 0.0), jnp.where(behind, 0.0, taps_turned)], 0
    ).astype(BF16)
    part_decay = jnp.exp(-rate_row * LANE)
    row_decay = jnp.exp(-rate_row * (LANE * parts))

    grad_short = grads.astype(BF16)
    read = part_rows(dot_nt(grad_short, reading), sources)
    whole = read[-1]
    for part in range(parts - 2, -1, -1):
        whole = part_decay * whole + read[part]
    scan = earlier(whole, 1, source_at)
    step, decay = 1, row_decay
    while step < sources:
        scan = scan + decay * earlier(scan, step, source_at)
        step, decay = 2 * step, decay * decay
    leaving = [scan]
    for part in range(parts - 1, 0, -1):
        leaving.insert(0, part_decay * leaving[0] + read[part])
    start_grad = (part_decay * leaving[0] + read[0])[0:1]
    carry_high, carry_low = split_pair(jnp.concatenate(leaving, 0))
    back_drive = (
        dot_nn(
            jnp.concatenate([grad_short, carry_high, carry_low], 1),
            jnp.concatenate([local_turned, feeding, feeding], 0),
        )
        + skip_ref[channel] * grads
    )
    back_value = back_drive * shifted
    back_shifted = back_drive * value
    pieces = part_rows(back_shifted, sources)
    back_after = jnp.concatenate(pieces[1:] + [earlier(pieces[0], 1, source_at)], 0)
    back_short = back_shifted.astype(BF16)
    back_pair = jnp.concatenate([back_short, back_after.astype(BF16)], 1)
    back_key = dot_nn(back_pair, taps_back)

    gram = dot_tn(key_pair, back_short)
    gram = jnp.where(lane_at >= row_at, gram[LANE:], gram[:LANE])
    aligned = gram[:8]
    for first in range(8, LANE, 8):
        aligned = aligned + pltpu.roll(gram[first : first + 8], LANE - first, 1)
    for bit in (1, 2, 4):
        aligned = jnp.where((row_at[:8] & bit) > 0, pltpu.roll(aligned, LANE - bit, 1), aligned)
    filter_grad = jnp.sum(aligned, axis=0, keepdims=True)[:, : LANE - states]
    small_rows[pl.ds(channel, 1), :] = jnp.concatenate([filter_grad, start_grad], 1)
    store_rows(out_rows, channel, sources, out_pad, back_value)
    store_rows(out_rows, channel + group, sources, out_pad, back_key)


UNROLL = 4


def each_channel(group, body):
    def step(index, carry):
        for inner in range(UNROLL):
            body(index * UNROLL + inner)
        return carry

    lax.fori_loop(0, group // UNROLL, step, 0)


def fetched(pairs, sems):
    copies = [
        pltpu.make_async_copy(source, target, sems.at[index])
        for index, (source, target) in enumerate(pairs)
    ]
    for copy in copies:
        copy.start()
    return copies


def wait_all(copies):
    for copy in copies:
        copy.wait()


def shape_of(*dims, kind=BF16):
    return jax.ShapeDtypeStruct(dims, kind)


def forward_kernel(
    group, after_ref, kv_ref, rows_ref, cols_ref, taps_ref, skip_ref, out_ref, shifted_out,
    value_out, pair_out, kv_rows, out_rows, shifted_ref, value_ref, pair_ref, sems,
):
    sources, _, width = kv_ref.shape
    parts = width // LANE
    spread(kv_ref, kv_rows, padded(2 * group))
    at = iotas(sources)
    each_channel(
        group,
        lambda channel: forward_channel(
            channel, sources, parts, group, at, kv_rows, out_rows, rows_ref, cols_ref, taps_ref,
            skip_ref, shifted_ref, value_ref, pair_ref,
        ),
    )
    copies = fetched(
        [(shifted_ref, shifted_out), (value_ref, value_out), (pair_ref, pair_out)], sems
    )
    out_pad = padded(group)
    for part in range(parts):
        for source in range(sources):
            row = (part * sources + source) * out_pad
            out_ref[source, :, LANE * part : LANE * (part + 1)] = out_rows[
                row : row + group
            ].astype(BF16)
    wait_all(copies)


def forward_part(after, kv, rows, cols, taps, skip):
    sources, double, width = kv.shape
    group = double // 2
    lines = sources * width // LANE
    kept = (
        shape_of(group, lines, LANE, kind=F32),
        shape_of(group, lines, LANE, kind=F32),
        shape_of(group, lines, 2 * LANE),
    )
    return pl.pallas_call(
        functools.partial(forward_kernel, group),
        out_shape=(shape_of(sources, group, width),) + kept,
        in_specs=anywhere(1) + in_vmem(4) + in_smem(1),
        out_specs=tuple(in_vmem(1) + anywhere(3)),
        scratch_shapes=[
            pltpu.VMEM((lines * padded(2 * group), LANE), F32),
            pltpu.VMEM((lines * padded(group), LANE), F32),
        ]
        + [pltpu.VMEM(one.shape, one.dtype) for one in kept]
        + [pltpu.SemaphoreType.DMA((3,))],
        compiler_params=params(40),
        cost_estimate=call_cost(9_000_000_000, 5_000_000),
    )(after, kv, rows, cols, taps, skip)


def backward_kernel(
    group, grad_ref, shifted_in, value_in, pair_in, rows_ref, cols_ref, taps_ref, skip_ref,
    out_ref, grad_rows, out_rows, small_rows, shifted_ref, value_ref, pair_ref, sems,
):
    copies = fetched(
        [(shifted_in, shifted_ref), (value_in, value_ref), (pair_in, pair_ref)], sems
    )
    sources, _, width = grad_ref.shape
    parts = width // LANE
    spread(grad_ref, grad_rows, padded(group))
    small_rows[...] = jnp.zeros_like(small_rows)
    at = iotas(sources)
    wait_all(copies)
    each_channel(
        group,
        lambda channel: backward_channel(
            channel, sources, parts, group, at, grad_rows, out_rows, small_rows, rows_ref,
            cols_ref, taps_ref, skip_ref, shifted_ref, value_ref, pair_ref,
        ),
    )
    out_pad = padded(2 * group)
    extra = out_ref.shape[1] - 2 * group
    for part in range(parts):
        small = small_rows[extra * part : extra * (part + 1)].astype(BF16)
        for source in range(sources):
            row = (part * sources + source) * out_pad
            columns = slice(LANE * part, LANE * (part + 1))
            out_ref[source, : 2 * group, columns] = out_rows[row : row + 2 * group].astype(BF16)
            out_ref[source, 2 * group :, columns] = small


def backward_part(grads, shifted, value, pair, rows, cols, taps, skip):
    sources, group, width = grads.shape
    parts = width // LANE
    lines = sources * parts
    extra = -(-group // parts)
    return pl.pallas_call(
        functools.partial(backward_kernel, group),
        out_shape=shape_of(sources, 2 * group + extra, width),
        in_specs=in_vmem(1) + anywhere(3) + in_vmem(3) + in_smem(1),
        out_specs=in_vmem(1)[0],
        scratch_shapes=[
            pltpu.VMEM((lines * padded(group), LANE), F32),
            pltpu.VMEM((lines * padded(2 * group), LANE), F32),
            pltpu.VMEM((padded(extra * parts), LANE), F32),
        ]
        + [pltpu.VMEM(one.shape, one.dtype) for one in (shifted, value, pair)]
        + [pltpu.SemaphoreType.DMA((3,))],
        compiler_params=params(40),
        cost_estimate=call_cost(12_000_000_000, 5_000_000),
    )(grads, shifted, value, pair, rows, cols, taps, skip)


def row_tile(ref, index, size):
    return ref.at[pl.ds(pl.multiple_of(index * size, size), size)]


def accumulate(total, part, tile):
    if tile == 0:
        total[...] = part
    else:
        total[...] += part


def key_value_kernel(
    group, shards_in, key_in, value_in, ids_ref, kv_ref, shards, keys, values, key_total,
    value_total, across, packed, shard_sems, key_sems, value_sems,
):
    count, _, depth = shards.shape
    copies = []
    for tile in range(count):
        copies.append(
            [
                pltpu.make_async_copy(shards_in.at[tile], shards.at[tile], shard_sems.at[tile]),
                pltpu.make_async_copy(
                    row_tile(key_in, ids_ref[tile], depth), keys.at[tile], key_sems.at[tile]
                ),
                pltpu.make_async_copy(
                    row_tile(value_in, ids_ref[tile], depth), values.at[tile], value_sems.at[tile]
                ),
            ]
        )
        for copy in copies[-1]:
            copy.start()
    for tile in range(count):
        wait_all(copies[tile])
        accumulate(key_total, dot_nn(shards[tile], keys[tile]), tile)
        accumulate(value_total, dot_nn(shards[tile], values[tile]), tile)
    pad = padded(2 * group)
    owners = kv_ref.shape[0]
    for index, total in enumerate((key_total, value_total)):
        across[...] = total[...].T
        for owner in range(owners):
            first = owner * pad + index * group
            packed[first : first + group] = across[owner * group : (owner + 1) * group]
    for owner in range(owners):
        kv_ref[owner] = packed[owner * pad : owner * pad + 2 * group].astype(BF16)


def key_value_part(shards, ids, w_key, w_value, owners):
    count, rows, depth = shards.shape
    channels = w_key.shape[1]
    group = channels // owners
    return pl.pallas_call(
        functools.partial(key_value_kernel, group),
        in_specs=anywhere(3) + in_smem(1),
        out_specs=in_vmem(1)[0],
        out_shape=shape_of(owners, 2 * group, rows),
        scratch_shapes=[
            pltpu.VMEM((count, rows, depth), BF16),
            pltpu.VMEM((count, depth, channels), BF16),
            pltpu.VMEM((count, depth, channels), BF16),
            pltpu.VMEM((rows, channels), F32),
            pltpu.VMEM((rows, channels), F32),
            pltpu.VMEM((channels, rows), F32),
            pltpu.VMEM((owners * padded(2 * group), rows), F32),
        ]
        + [pltpu.SemaphoreType.DMA((count,))] * 3,
        compiler_params=params(48),
        cost_estimate=call_cost(4 * count * rows * depth * channels, 12_000_000),
    )(shards, w_key, w_value, ids)


def query_kernel(
    after_ref, shards_in, weight_in, ids_ref, query_out, shards, weights, total, query,
    shard_sems, weight_sems, out_sem,
):
    count, _, depth = shards.shape
    copies = []
    for tile in range(count):
        copies.append(
            [
                pltpu.make_async_copy(shards_in.at[tile], shards.at[tile], shard_sems.at[tile]),
                pltpu.make_async_copy(
                    row_tile(weight_in, ids_ref[tile], depth), weights.at[tile],
                    weight_sems.at[tile],
                ),
            ]
        )
        for copy in copies[-1]:
            copy.start()
    for tile in range(count):
        wait_all(copies[tile])
        accumulate(total, dot_nn(shards[tile], weights[tile]), tile)
    query[...] = total[...].astype(BF16)
    wait_all(fetched([(query, query_out)], out_sem))


def query_part(after, shards, ids, w_query):
    count, rows, depth = shards.shape
    channels = w_query.shape[1]
    return pl.pallas_call(
        query_kernel,
        in_specs=anywhere(3) + in_smem(1),
        out_specs=anywhere(1)[0],
        out_shape=shape_of(rows, channels),
        scratch_shapes=[
            pltpu.VMEM((count, rows, depth), BF16),
            pltpu.VMEM((count, depth, channels), BF16),
            pltpu.VMEM((rows, channels), F32),
            pltpu.VMEM((rows, channels), BF16),
            pltpu.SemaphoreType.DMA((count,)),
            pltpu.SemaphoreType.DMA((count,)),
            pltpu.SemaphoreType.DMA((1,)),
        ],
        compiler_params=params(48),
        cost_estimate=call_cost(2 * count * rows * depth * channels, 6_000_000),
    )(after, shards, w_query, ids)


def gated_grad_kernel(
    group, after_ref, shards_in, weight_in, query_in, gated_out, grouped_ref, shards, weights,
    query, gated, total, across, shard_sems, weight_sems, sems,
):
    count, _, depth = shards.shape
    copies = []
    for tile in range(count):
        copies.append(
            [
                pltpu.make_async_copy(shards_in.at[tile], shards.at[tile], shard_sems.at[tile]),
                pltpu.make_async_copy(
                    weight_in.at[:, tile * depth : (tile + 1) * depth], weights.at[tile],
                    weight_sems.at[tile],
                ),
            ]
        )
        for copy in copies[-1]:
            copy.start()
    query_copy = pltpu.make_async_copy(query_in, query, sems.at[0])
    query_copy.start()
    for tile in range(count):
        wait_all(copies[tile])
        accumulate(total, dot_nt(shards[tile], weights[tile]), tile)
    gated[...] = total[...].astype(BF16)
    out_copy = pltpu.make_async_copy(gated, gated_out, sems.at[1])
    out_copy.start()
    query_copy.wait()
    across[...] = (gated[...].astype(F32) * query[...].astype(F32)).T
    for owner in range(grouped_ref.shape[0]):
        grouped_ref[owner] = across[owner * group : (owner + 1) * group].astype(BF16)
    out_copy.wait()


def gated_grad_part(after, shards, w_out, query, owners):
    count, rows, depth = shards.shape
    channels = w_out.shape[0]
    group = channels // owners
    return pl.pallas_call(
        functools.partial(gated_grad_kernel, group),
        in_specs=anywhere(4),
        out_specs=tuple(anywhere(1) + in_vmem(1)),
        out_shape=(shape_of(rows, channels), shape_of(owners, group, rows)),
        scratch_shapes=[
            pltpu.VMEM((count, rows, depth), BF16),
            pltpu.VMEM((count, channels, depth), BF16),
            pltpu.VMEM((rows, channels), BF16),
            pltpu.VMEM((rows, channels), BF16),
            pltpu.VMEM((rows, channels), F32),
            pltpu.VMEM((channels, rows), F32),
            pltpu.SemaphoreType.DMA((count,)),
            pltpu.SemaphoreType.DMA((count,)),
            pltpu.SemaphoreType.DMA((2,)),
        ],
        compiler_params=params(48),
        cost_estimate=call_cost(2 * count * rows * depth * channels, 9_000_000),
    )(after, shards, w_out, query)


def response_kernel(
    group, after_ref, returned_in, query_in, gated_in, forward_out, query_grad_out, returned,
    query, gated, forward, query_grad, across, sems, out_sems,
):
    copies = fetched([(returned_in, returned), (query_in, query), (gated_in, gated)], sems)
    copies[0].wait()
    for owner in range(returned.shape[0]):
        across[owner * group : (owner + 1) * group] = returned[owner].astype(F32)
    response = across[...].T
    wait_all(copies[1:])
    forward[...] = (query[...].astype(F32) * response).astype(BF16)
    query_grad[...] = (gated[...].astype(F32) * response).astype(BF16)
    wait_all(fetched([(forward, forward_out), (query_grad, query_grad_out)], out_sems))


def response_part(after, returned, query, gated):
    rows, channels = query.shape
    square = shape_of(rows, channels)
    return pl.pallas_call(
        functools.partial(response_kernel, returned.shape[1]),
        in_specs=anywhere(4),
        out_specs=tuple(anywhere(2)),
        out_shape=(square, square),
        scratch_shapes=[pltpu.VMEM(returned.shape, BF16)]
        + [pltpu.VMEM((rows, channels), BF16)] * 4
        + [pltpu.VMEM((channels, rows), F32)]
        + [pltpu.SemaphoreType.DMA((3,)), pltpu.SemaphoreType.DMA((2,))],
        compiler_params=params(48),
        cost_estimate=call_cost(4 * rows * channels, 3_000_000),
    )(after, returned, query, gated)


def back_kernel(
    group, after_ref, returned_in, value_out, key_out, returned, value, key, value_rows, key_rows,
    sems, out_sems,
):
    wait_all(fetched([(returned_in, returned)], sems))
    for owner in range(returned.shape[0]):
        piece = returned[owner].astype(F32)
        value_rows[owner * group : (owner + 1) * group] = piece[:group]
        key_rows[owner * group : (owner + 1) * group] = piece[group : 2 * group]
    value[...] = value_rows[...].T.astype(BF16)
    key[...] = key_rows[...].T.astype(BF16)
    wait_all(fetched([(value, value_out), (key, key_out)], out_sems))


def back_part(after, returned, channels):
    owners, _, rows = returned.shape
    square = shape_of(rows, channels)
    return pl.pallas_call(
        functools.partial(back_kernel, channels // owners),
        in_specs=anywhere(2),
        out_specs=tuple(anywhere(2)),
        out_shape=(square, square),
        scratch_shapes=[pltpu.VMEM(returned.shape, BF16)]
        + [pltpu.VMEM((rows, channels), BF16)] * 2
        + [pltpu.VMEM((channels, rows), F32)] * 2
        + [pltpu.SemaphoreType.DMA((1,)), pltpu.SemaphoreType.DMA((2,))],
        compiler_params=params(48),
        cost_estimate=call_cost(4 * rows * channels, 3_000_000),
    )(after, returned)


def weight_kernel(
    rows, after_ref, wide_in, narrow_in, ids_ref, core_ref, keep_out, send_out, wide, narrow, keep,
    send, wide_sems, narrow_sem, keep_sems, send_sems,
):
    tiles = wide.shape[0]
    held = keep.shape[1]
    narrow_copies = fetched([(narrow_in, narrow)], narrow_sem)
    copies = fetched([(wide_in.at[tile], wide.at[tile]) for tile in range(tiles)], wide_sems)
    wait_all(narrow_copies)
    sent = []
    for tile in range(tiles):
        copies[tile].wait()
        result = dot_tn(wide[tile], narrow[...]).astype(BF16)
        for core in range(2):

            @pl.when(core_ref[0] == core)
            def _():
                for chip in range(held):
                    at = (2 * chip + core) * rows
                    other = (2 * chip + 1 - core) * rows
                    keep[tile, chip] = result[at : at + rows]
                    send[tile, chip] = result[other : other + rows]

        first = pl.ds(ids_ref[tile] * held, held)
        sent.append(
            pltpu.make_async_copy(send.at[tile], send_out.at[first], send_sems.at[tile])
        )
        sent.append(
            pltpu.make_async_copy(keep.at[tile], keep_out.at[first], keep_sems.at[tile])
        )
        sent[-2].start()
        sent[-1].start()
    wait_all(sent)


def weight_partial(after, wide, ids, narrow, core, chips):
    tiles, depth, height = wide.shape
    width = narrow.shape[1]
    total = tiles * height
    rows = total // (2 * chips)
    out = shape_of(chips, rows, width)
    halves = pltpu.VMEM((tiles, chips // tiles, rows, width), BF16)
    return pl.pallas_call(
        functools.partial(weight_kernel, rows),
        in_specs=anywhere(3) + in_smem(2),
        out_specs=tuple(anywhere(2)),
        out_shape=(out, out),
        scratch_shapes=[
            pltpu.VMEM(wide.shape, BF16),
            pltpu.VMEM(narrow.shape, BF16),
            halves,
            halves,
            pltpu.SemaphoreType.DMA((tiles,)),
            pltpu.SemaphoreType.DMA((1,)),
            pltpu.SemaphoreType.DMA((tiles,)),
            pltpu.SemaphoreType.DMA((tiles,)),
        ],
        compiler_params=params(48),
        cost_estimate=call_cost(2 * total * depth * width, 6_000_000),
    )(after, wide, narrow, ids, core)


def mixed_kernel(
    after_ref, gated_in, weight_in, out_ref, gated, weights, result, gated_sem, weight_sems,
    out_sems,
):
    count, _, width = out_ref.shape
    gated_copies = fetched([(gated_in, gated)], gated_sem)
    copies = fetched(
        [
            (weight_in.at[:, tile * width : (tile + 1) * width], weights.at[tile])
            for tile in range(count)
        ],
        weight_sems,
    )
    wait_all(gated_copies)
    sent = []
    for tile in range(count):
        copies[tile].wait()
        result[tile] = dot_nn(gated[...], weights[tile]).astype(BF16)
        sent.append(pltpu.make_async_copy(result.at[tile], out_ref.at[tile], out_sems.at[tile]))
        sent[-1].start()
    wait_all(sent)


def mixed_part(after, gated, w_out, count):
    rows, depth = gated.shape
    width = w_out.shape[1] // count
    return pl.pallas_call(
        mixed_kernel,
        in_specs=anywhere(3),
        out_specs=anywhere(1)[0],
        out_shape=shape_of(count, rows, width),
        scratch_shapes=[
            pltpu.VMEM((rows, depth), BF16),
            pltpu.VMEM((count, depth, width), BF16),
            pltpu.VMEM((count, rows, width), BF16),
            pltpu.SemaphoreType.DMA((1,)),
            pltpu.SemaphoreType.DMA((count,)),
            pltpu.SemaphoreType.DMA((count,)),
        ],
        compiler_params=params(48),
        cost_estimate=call_cost(2 * rows * depth * width * count, 6_000_000),
    )(after, gated, w_out)


def input_kernel(unread, *refs):
    (
        first_in, second_in, third_in, first_weight, second_weight, third_weight, out_ref, backs,
        weights, result, back_sems, weight_sems, out_sems,
    ) = refs[unread:]
    count, _, width = out_ref.shape
    back_copies = fetched(
        [(ref, backs.at[index]) for index, ref in enumerate((first_in, second_in, third_in))],
        back_sems,
    )
    weight_refs = (first_weight, second_weight, third_weight)
    copies = fetched(
        [
            (ref.at[tile * width : (tile + 1) * width], weights.at[tile, index])
            for tile in range(count)
            for index, ref in enumerate(weight_refs)
        ],
        weight_sems,
    )
    wait_all(back_copies)
    sent = []
    for tile in range(count):
        wait_all(copies[3 * tile : 3 * tile + 3])
        total = dot_nt(backs[0], weights[tile, 0])
        total += dot_nt(backs[1], weights[tile, 1])
        total += dot_nt(backs[2], weights[tile, 2])
        result[tile] = total.astype(BF16)
        sent.append(pltpu.make_async_copy(result.at[tile], out_ref.at[tile], out_sems.at[tile]))
        sent[-1].start()
    wait_all(sent)


def input_part(after, backs, weights, count):
    rows, depth = backs[0].shape
    width = weights[0].shape[0] // count
    return pl.pallas_call(
        functools.partial(input_kernel, len(after)),
        in_specs=anywhere(6 + len(after)),
        out_specs=anywhere(1)[0],
        out_shape=shape_of(count, rows, width),
        scratch_shapes=[
            pltpu.VMEM((3, rows, depth), BF16),
            pltpu.VMEM((count, 3, width, depth), BF16),
            pltpu.VMEM((count, rows, width), BF16),
            pltpu.SemaphoreType.DMA((3,)),
            pltpu.SemaphoreType.DMA((3 * count,)),
            pltpu.SemaphoreType.DMA((count,)),
        ],
        compiler_params=params(48),
        cost_estimate=call_cost(6 * rows * depth * width * count, 14_000_000),
    )(*after, *backs, *weights)


def moved(value, axis, steps):
    by_core = steps if isinstance(steps, tuple) else (steps, steps)
    pairs = []
    for x in range(SIDE):
        for y in range(SIDE):
            for core in range(2):
                for z in range(SIDE):
                    goal = [x, y, core, z]
                    if axis == "core":
                        goal[2] = 1 - core
                    else:
                        at = {"x": 0, "y": 1, "z": 3}[axis]
                        goal[at] = (goal[at] + by_core[core]) % SIDE
                    pairs.append(
                        tuple(
                            ((a * SIDE + b) * 2 + c) * SIDE + d
                            for a, b, c, d in ((x, y, core, z), goal)
                        )
                    )
    return lax.ppermute(value, ("seq", "tp"), pairs)


def first_kernel(
    along_x, after_ref, keep_in, came_in, place_ref, up_out, down_out, mine_out, near_out, keep,
    came, results, in_sems, out_sems,
):
    place = place_ref[0]
    half = SIDE // 2
    above, below, far = (lax.rem(place + step, SIDE) for step in (1, 3, 2))
    order = (far, above, below, place)

    def chip_at(chip, row):
        return chip * SIDE + row if along_x else row * SIDE + chip

    copies = {}
    for index, chip in enumerate(order):
        for row in range(SIDE):
            at = index * SIDE + row
            copies[index, row] = (
                pltpu.make_async_copy(
                    keep_in.at[chip_at(chip, row)], keep.at[at], in_sems.at[2 * at]
                ),
                pltpu.make_async_copy(
                    came_in.at[chip_at(chip, row)], came.at[at], in_sems.at[2 * at + 1]
                ),
            )
            for copy in copies[index, row]:
                copy.start()

    def block(index, row):
        wait_all(copies[index, row])
        at = index * SIDE + row
        return (keep[at].astype(F32) + came[at].astype(F32)).astype(BF16)

    up, down, mine, near = range(4)
    for row in range(half):
        results[up, row] = block(0, row)
        results[down, half + row] = block(0, half + row)
        results[near, row] = block(1, row)
        results[up, half + row] = block(1, half + row)
        results[down, row] = block(2, row)
        results[near, half + row] = block(2, half + row)
    sent = [
        pltpu.make_async_copy(results.at[index], target, out_sems.at[index])
        for index, target in enumerate((up_out, down_out, mine_out, near_out))
    ]
    for index in (up, down, near):
        sent[index].start()
    for row in range(SIDE):
        results[mine, row] = block(3, row)
    sent[mine].start()
    wait_all(sent)


def first_part(after, keep, came, place, along_x):
    chips, rows, width = keep.shape
    short = shape_of(SIDE, rows, width)
    return pl.pallas_call(
        functools.partial(first_kernel, along_x),
        in_specs=anywhere(3) + in_smem(1),
        out_specs=tuple(anywhere(4)),
        out_shape=(short,) * 4,
        scratch_shapes=[
            pltpu.VMEM((chips, rows, width), BF16),
            pltpu.VMEM((chips, rows, width), BF16),
            pltpu.VMEM((4, SIDE, rows, width), BF16),
            pltpu.SemaphoreType.DMA((2 * chips,)),
            pltpu.SemaphoreType.DMA((4,)),
        ],
        compiler_params=params(48),
        cost_estimate=call_cost(2 * chips * rows * width, 6_000_000),
    )(after, keep, came, place.reshape(1))


def second_part(near, came_up, came_down):
    half = SIDE // 2
    return added(near[:half], came_up[:half]), added(near[half:], came_down[half:])


def added(left, right):
    return (left.astype(F32) + right.astype(F32)).astype(BF16)


def third_kernel(
    mine_in, up_in, down_in, up_more_in, down_more_in, place_ref, own_out, above_out, below_out,
    far_out, mine, up, down, up_more, down_more, sums, own, parts, in_sems, out_sems,
):
    half = SIDE // 2
    wait_all(
        fetched(
            [
                (mine_in, mine), (up_in.at[half:], up), (down_in.at[:half], down),
                (up_more_in, up_more), (down_more_in, down_more),
            ],
            in_sems,
        )
    )
    for row in range(half):
        sums[row] = (
            mine[row].astype(F32) + down[row].astype(F32) + up_more[row].astype(F32)
        )
        sums[half + row] = (
            mine[half + row].astype(F32) + up[row].astype(F32) + down_more[row].astype(F32)
        )
    place = place_ref[0]
    own[...] = sums[place]
    for index, step in enumerate((1, 3, 2)):
        parts[index] = sums[lax.rem(place + step, SIDE)].astype(BF16)
    wait_all(
        fetched(
            [
                (own, own_out), (parts.at[0], above_out), (parts.at[1], below_out),
                (parts.at[2], far_out),
            ],
            out_sems,
        )
    )


def third_part(mine, came_up, came_down, more_up, more_down, place):
    _, rows, width = mine.shape
    half = SIDE // 2
    short = shape_of(rows, width)
    return pl.pallas_call(
        third_kernel,
        in_specs=anywhere(5) + in_smem(1),
        out_specs=tuple(anywhere(4)),
        out_shape=(shape_of(rows, width, kind=F32), short, short, short),
        scratch_shapes=[pltpu.VMEM((SIDE, rows, width), BF16)]
        + [pltpu.VMEM((half, rows, width), BF16)] * 4
        + [
            pltpu.VMEM((SIDE, rows, width), F32),
            pltpu.VMEM((rows, width), F32),
            pltpu.VMEM((3, rows, width), BF16),
            pltpu.SemaphoreType.DMA((5,)),
            pltpu.SemaphoreType.DMA((4,)),
        ],
        compiler_params=params(48),
        cost_estimate=call_cost(2 * SIDE * rows * width, 3_000_000),
    )(mine, came_up, came_down, more_up, more_down, place.reshape(1))


def first_moves(pieces, first):
    up, down, mine, near = pieces
    return moved(up, first, 1), moved(down, first, -1), mine, near


def later_sums(pieces, first, places):
    second = "y" if first == "x" else "x"
    came_up, came_down, mine, near = pieces
    more_up, more_down = second_part(near, came_up, came_down)
    more_up, more_down = moved(more_up, first, 1), moved(more_down, first, -1)
    own, above, below, far = third_part(
        mine, came_up, came_down, more_up, more_down, places[second]
    )
    return (
        own
        + moved(above, second, 1).astype(F32)
        + moved(below, second, -1).astype(F32)
        + moved(far, second, (2, -2)).astype(F32)
    )


def per_device(
    tokens,
    w_query,
    w_key,
    w_value,
    w_out,
    shift_filter,
    log_decay,
    readout,
    skip_gain,
    init_state,
    cotangent,
):
    row_count = tokens.shape[0]
    channels = w_query.shape[1]
    tap_count = shift_filter.shape[0]
    seq_count = lax.axis_size("seq")
    group = channels // seq_count
    position = lax.axis_index("seq")
    core = position % 2
    chip_z = lax.axis_index("tp")
    places = {"x": position // (2 * SIDE), "y": (position // 2) % SIDE}
    core_word = core.reshape(1)

    from_below, from_above = moved(tokens, "z", 1), moved(tokens, "z", -1)
    passed_on = jnp.where(core == 0, from_below, from_above)
    cotangent, passed_on = lax.optimization_barrier((cotangent, passed_on))
    from_far = moved(passed_on, "z", (1, -1))
    grad_shards = lax.all_gather(cotangent, "tp", axis=0, tiled=False)
    shards = jnp.stack([tokens, from_below, from_above, from_far])
    in_order = jnp.arange(SIDE, dtype=jnp.int32)
    ids = (chip_z + jnp.array([0, SIDE - 1, 1, 2], jnp.int32)) % SIDE

    def own(value):
        return lax.dynamic_slice_in_dim(value, position * group, group, value.ndim - 1)

    own_rate, own_read, own_init, own_taps = (
        own(value).T for value in (log_decay, readout, init_state, shift_filter)
    )
    own_taps = jnp.pad(own_taps, ((0, 0), (0, LANE - tap_count)))
    taps = jnp.stack([own_taps, jnp.roll(own_taps[:, ::-1], 1, axis=1)])
    rows = jnp.stack([own_rate, own_init])
    cols = jnp.stack([own_rate, own_read])[..., None]
    skip = own(skip_gain)

    def exchanged(value):
        return lax.all_to_all(value, "seq", 0, 0, tiled=True)

    kv = key_value_part(shards, ids, w_key, w_value, seq_count)
    query = query_part(kv, shards, ids, w_query)
    kv = exchanged(kv)
    gated_grad, grads = gated_grad_part(kv, grad_shards, w_out, query, seq_count)
    response, shifted, value, pair = forward_part(grads, kv, rows, cols, taps, skip)
    grads = exchanged(grads)
    response, grads = lax.optimization_barrier((response, grads))
    response = exchanged(response)
    backs = backward_part(grads, shifted, value, pair, rows, cols, taps, skip)
    gated, back_query = response_part(backs, response, query, gated_grad)
    backs = exchanged(backs)
    chips = SIDE * SIDE

    def weight(after, wide, order, narrow):
        return weight_partial(after, wide, order, narrow, core_word, chips)

    out_keep, out_send = weight(gated, grad_shards, in_order, gated)
    query_keep, query_send = weight(out_send, shards, ids, back_query)
    partial_mixed = mixed_part(query_send, gated, w_out, SIDE)
    mixed = lax.psum_scatter(partial_mixed, "tp", scatter_dimension=0, tiled=True)[0]
    out_pieces = first_part(
        partial_mixed, out_keep, moved(out_send, "core", 1), places["x"], True
    )
    query_pieces = first_part(
        out_pieces[0], query_keep, moved(query_send, "core", 1), places["y"], False
    )

    back_value, back_key = back_part(query_pieces[0], backs, channels)
    out_moved, query_moved = first_moves(out_pieces, "x"), first_moves(query_pieces, "y")
    key_keep, key_send = weight(back_key, shards, ids, back_key)
    value_keep, value_send = weight(key_send, shards, ids, back_value)
    partial_input = input_part(
        (value_send, *out_moved[:2], *query_moved[:2]),
        (back_query, back_key, back_value),
        (w_query, w_key, w_value),
        SIDE,
    )
    grad_input = lax.psum_scatter(partial_input, "tp", scatter_dimension=0, tiled=True)[0]
    key_pieces = first_part(
        partial_input, key_keep, moved(key_send, "core", 1), places["x"], True
    )
    value_pieces = first_part(
        key_pieces[0], value_keep, moved(value_send, "core", 1), places["y"], False
    )

    small = backs[:, 2 * group :].reshape(seq_count, -1, row_count // LANE, LANE)
    small = small.transpose(0, 2, 1, 3).reshape(seq_count, -1, LANE)[:, :group]
    small = small.reshape(channels, LANE).T.astype(F32)
    grad_filter, grad_init = small[:tap_count], small[tap_count:]

    grad_out = later_sums(out_moved, "x", places).T
    grad_query = later_sums(query_moved, "y", places)
    grad_key = later_sums(first_moves(key_pieces, "x"), "x", places)
    grad_value = later_sums(first_moves(value_pieces, "y"), "y", places)
    return (mixed, grad_input, grad_query, grad_key, grad_value, grad_out, grad_filter, grad_init)


def solution(mesh):
    return jax.shard_map(
        per_device,
        mesh=mesh,
        in_specs=(
            P("seq", "tp"),
            P(None, "tp"),
            P(None, "tp"),
            P(None, "tp"),
            P("tp", None),
            P(None, "tp"),
            P(None, "tp"),
            P(None, "tp"),
            P("tp"),
            P(None, "tp"),
            P("seq", "tp"),
        ),
        out_specs=(
            P("seq", "tp"),
            P("seq", "tp"),
            P("seq", "tp"),
            P("seq", "tp"),
            P("seq", "tp"),
            P("tp", "seq"),
            P(None, "tp"),
            P(None, "tp"),
        ),
        check_vma=False,
    )
```

```python
import functools

import jax
import jax.numpy as jnp
from jax import lax
from jax.experimental import pallas as pl
from jax.experimental.pallas import tpu as pltpu
from jax.sharding import PartitionSpec as P

LANE = 128
F32 = jnp.float32
BF16 = jnp.bfloat16


def dot_nn(left, right):
    return lax.dot_general(left, right, (((1,), (0,)), ((), ())), preferred_element_type=F32)


def dot_nt(left, right):
    return lax.dot_general(left, right, (((1,), (1,)), ((), ())), preferred_element_type=F32)


def dot_tn(left, right):
    return lax.dot_general(left, right, (((0,), (0,)), ((), ())), preferred_element_type=F32)


def dot_tt(left, right):
    return lax.dot_general(left, right, (((0,), (1,)), ((), ())), preferred_element_type=F32)


def split_pair(value):
    high = value.astype(BF16)
    return high, (value - high.astype(F32)).astype(BF16)


SIDE = 4
MIB = 1024 * 1024


def call_cost(flops, bytes_accessed, transcendentals=0):
    return pl.CostEstimate(
        flops=flops, bytes_accessed=bytes_accessed, transcendentals=transcendentals
    )


def params(mebibytes):
    return pltpu.CompilerParams(vmem_limit_bytes=mebibytes * MIB)


def in_vmem(count):
    return [pl.BlockSpec(memory_space=pltpu.VMEM)] * count


def in_smem(count):
    return [pl.BlockSpec(memory_space=pltpu.SMEM)] * count


def anywhere(count):
    return [pl.BlockSpec(memory_space=pl.ANY)] * count


def padded(rows):
    return -(-rows // 8) * 8


def later(value, steps, source_at):
    at = source_at[:, : value.shape[1]]
    return jnp.where(at >= steps, pltpu.roll(value, steps, 0), 0.0)


def earlier(value, steps, source_at):
    sources = value.shape[0]
    at = source_at[:, : value.shape[1]]
    return jnp.where(at < sources - steps, pltpu.roll(value, sources - steps, 0), 0.0)


def circulant(row):
    return pltpu.roll(jnp.broadcast_to(row, (LANE, LANE)), 0, 1, stride=1, stride_axis=0)


def iotas(sources):
    lane_at = lax.broadcasted_iota(jnp.int32, (LANE, LANE), 1)
    row_at = lax.broadcasted_iota(jnp.int32, (LANE, LANE), 0)
    source_at = lax.broadcasted_iota(jnp.int32, (sources, LANE), 0)
    return lane_at, row_at, source_at


def decay_tables(cols_ref, channel, lane_at):
    rate = cols_ref[0, channel]
    read = cols_ref[1, channel]
    lanes = lane_at[: rate.shape[0]].astype(F32)
    step_decay = jnp.exp(-rate)
    inflow = 1.0 - step_decay
    rising = jnp.exp(-rate * lanes)
    falling = jnp.exp(-rate * (LANE - 1.0 - lanes))
    reading = (read * step_decay) * rising
    feeding = inflow * falling
    weight = read * inflow
    kernel_row = jnp.sum(weight * rising, axis=0, keepdims=True)
    wrapped = jnp.where(lanes > 0.0, step_decay * falling, 1.0)
    kernel_turned = jnp.sum(weight * wrapped, axis=0, keepdims=True)
    return reading.astype(BF16), feeding.astype(BF16), kernel_row, kernel_turned


def part_rows(value, sources):
    return [value[at : at + sources] for at in range(0, value.shape[0], sources)]


def load_rows(ref, row, sources, pad, parts):
    return [
        ref[pl.ds(row + part * sources * pad, sources, stride=pad), :] for part in range(parts)
    ]


def store_rows(ref, row, sources, pad, value):
    for part, piece in enumerate(part_rows(value, sources)):
        ref[pl.ds(row + part * sources * pad, sources, stride=pad), :] = piece


def spread(block_ref, rows_ref, pad):
    sources, count, width = block_ref.shape

    def step(source, carry):
        for part in range(width // LANE):
            row = pl.multiple_of((part * sources + source) * pad, 8)
            rows_ref[pl.ds(row, count), :] = block_ref[
                source, :, LANE * part : LANE * (part + 1)
            ].astype(F32)
        return carry

    lax.fori_loop(0, sources, step, 0)


def channel_body(
    channel, sources, parts, group, at, in_rows, out_rows, small_rows, rows_ref, cols_ref,
    taps_ref, skip_ref,
):
    lane_at, row_at, source_at = at
    in_pad, out_pad = padded(3 * group), padded(2 * group) + padded(group)
    key = load_rows(in_rows, channel, sources, in_pad, parts)
    value = jnp.concatenate(load_rows(in_rows, channel + group, sources, in_pad, parts), 0)
    grads = jnp.concatenate(load_rows(in_rows, channel + 2 * group, sources, in_pad, parts), 0)
    rate_row = rows_ref[0, pl.ds(channel, 1), :]
    start_row = rows_ref[1, pl.ds(channel, 1), :]
    states = rate_row.shape[1]
    reading, feeding, kernel_row, kernel_turned = decay_tables(cols_ref, channel, lane_at)
    ahead, behind = lane_at >= row_at, lane_at <= row_at
    local = jnp.where(ahead, circulant(kernel_row), 0.0).astype(BF16)
    local_turned = jnp.where(behind, circulant(kernel_turned), 0.0).astype(BF16)
    taps = circulant(taps_ref[0, pl.ds(channel, 1), :])
    taps_turned = circulant(taps_ref[1, pl.ds(channel, 1), :])
    taps_forward = jnp.concatenate(
        [jnp.where(ahead, 0.0, taps), jnp.where(ahead, taps, 0.0)], 0
    ).astype(BF16)
    taps_back = jnp.concatenate(
        [jnp.where(behind, taps_turned, 0.0), jnp.where(behind, 0.0, taps_turned)], 0
    ).astype(BF16)
    skip = skip_ref[channel]
    part_decay = jnp.exp(-rate_row * LANE)
    row_decay = jnp.exp(-rate_row * (LANE * parts))

    key_now = jnp.concatenate(key, 0)
    key_before = jnp.concatenate([later(key[-1], 1, source_at)] + key[:-1], 0)
    key_pair = jnp.concatenate([key_before, key_now], 1).astype(BF16)
    shifted = dot_nn(key_pair, taps_forward)
    drive = shifted * value
    drive_short = drive.astype(BF16)

    fed = part_rows(dot_nt(drive_short, feeding), sources)
    whole = fed[0]
    for part in range(1, parts):
        whole = part_decay * whole + fed[part]
    scan = jnp.where(source_at[:, :states] >= 1, pltpu.roll(whole, 1, 0), start_row)
    step, decay = 1, row_decay
    while step < sources:
        scan = scan + decay * later(scan, step, source_at)
        step, decay = 2 * step, decay * decay
    entering = [scan]
    for part in range(1, parts):
        entering.append(part_decay * entering[-1] + fed[part - 1])
    state_high, state_low = split_pair(jnp.concatenate(entering, 0))
    response = (
        dot_nn(
            jnp.concatenate([drive_short, state_high, state_low], 1),
            jnp.concatenate([local, reading, reading], 0),
        )
        + skip * drive
    )

    grad_short = grads.astype(BF16)
    read = part_rows(dot_nt(grad_short, reading), sources)
    whole = read[-1]
    for part in range(parts - 2, -1, -1):
        whole = part_decay * whole + read[part]
    scan = earlier(whole, 1, source_at)
    step, decay = 1, row_decay
    while step < sources:
        scan = scan + decay * earlier(scan, step, source_at)
        step, decay = 2 * step, decay * decay
    leaving = [scan]
    for part in range(parts - 1, 0, -1):
        leaving.insert(0, part_decay * leaving[0] + read[part])
    start_grad = (part_decay * leaving[0] + read[0])[0:1]
    carry_high, carry_low = split_pair(jnp.concatenate(leaving, 0))
    back_drive = (
        dot_nn(
            jnp.concatenate([grad_short, carry_high, carry_low], 1),
            jnp.concatenate([local_turned, feeding, feeding], 0),
        )
        + skip * grads
    )
    back_value = back_drive * shifted
    back_shifted = back_drive * value
    pieces = part_rows(back_shifted, sources)
    back_after = jnp.concatenate(pieces[1:] + [earlier(pieces[0], 1, source_at)], 0)
    back_short = back_shifted.astype(BF16)
    back_pair = jnp.concatenate([back_short, back_after.astype(BF16)], 1)
    back_key = dot_nn(back_pair, taps_back)

    gram = dot_tn(key_pair, back_short)
    gram = jnp.where(ahead, gram[LANE:], gram[:LANE])
    aligned = gram[:8]
    for first in range(8, LANE, 8):
        aligned = aligned + pltpu.roll(gram[first : first + 8], LANE - first, 1)
    for bit in (1, 2, 4):
        aligned = jnp.where((row_at[:8] & bit) > 0, pltpu.roll(aligned, LANE - bit, 1), aligned)
    filter_grad = jnp.sum(aligned, axis=0, keepdims=True)[:, : LANE - states]
    small_rows[pl.ds(channel, 1), :] = jnp.concatenate([filter_grad, start_grad], 1)
    for index, result in enumerate((response, back_value, back_key)):
        store_rows(out_rows, channel + index * group, sources, out_pad, result)


UNROLL = 4


def sequence_kernel(
    group, in_ref, rows_ref, cols_ref, taps_ref, skip_ref, out_ref, in_rows, out_rows, small_rows,
):
    sources, _, width = in_ref.shape
    parts = width // LANE
    spread(in_ref, in_rows, padded(3 * group))
    small_rows[...] = jnp.zeros_like(small_rows)
    at = iotas(sources)

    def step(index, carry):
        for inner in range(UNROLL):
            channel_body(
                index * UNROLL + inner, sources, parts, group, at, in_rows, out_rows, small_rows,
                rows_ref, cols_ref, taps_ref, skip_ref,
            )
        return carry

    lax.fori_loop(0, group // UNROLL, step, 0)
    out_pad = padded(2 * group) + padded(group)
    extra = out_ref.shape[1] - 3 * group

    def pack(source, carry):
        for part in range(parts):
            row = pl.multiple_of((part * sources + source) * out_pad, 8)
            columns = slice(LANE * part, LANE * (part + 1))
            out_ref[source, : 3 * group, columns] = out_rows[pl.ds(row, 3 * group), :].astype(
                BF16
            )
            out_ref[source, 3 * group :, columns] = small_rows[
                extra * part : extra * (part + 1)
            ].astype(BF16)
        return carry

    lax.fori_loop(0, sources, pack, 0)


def sequence_part(value, rows, cols, taps, skip):
    sources, triple, width = value.shape
    group = triple // 3
    parts = width // LANE
    lines = sources * parts
    extra = -(-group // parts)
    return pl.pallas_call(
        functools.partial(sequence_kernel, group),
        out_shape=jax.ShapeDtypeStruct((sources, triple + extra, width), BF16),
        in_specs=in_vmem(4) + in_smem(1),
        out_specs=in_vmem(1)[0],
        scratch_shapes=[
            pltpu.VMEM((lines * padded(triple), LANE), F32),
            pltpu.VMEM((lines * (padded(2 * group) + padded(group)), LANE), F32),
            pltpu.VMEM((padded(extra * parts), LANE), F32),
        ],
        compiler_params=params(24),
        cost_estimate=call_cost(22_000_000_000, 5_000_000),
    )(value, rows, cols, taps, skip)


def tiles_of(count, body):
    def step(tile, carry):
        body(tile)
        return carry

    lax.fori_loop(0, count, step, 0)


def columns_of(tile, width):
    return pl.ds(pl.multiple_of(tile * width, LANE), width)


def rows_of(tile, height):
    return pl.ds(pl.multiple_of(tile * height, 16), height)


def projected(shards_ref, ids_ref, weight_ref, total_ref):
    count, _, depth = shards_ref.shape
    total_ref[...] = jnp.zeros_like(total_ref)

    def add(tile):
        total_ref[...] += dot_nn(
            shards_ref[tile], weight_ref[rows_of(ids_ref[tile], depth), :]
        )

    tiles_of(count, add)


def key_value_kernel(
    group, shards_ref, key_ref, value_ref, ids_ref, kv_ref, total, across, packed,
):
    pad = padded(2 * group)
    owners = kv_ref.shape[0]
    for index, weight_ref in enumerate((key_ref, value_ref)):
        projected(shards_ref, ids_ref, weight_ref, total)
        across[...] = total[...].T
        for owner in range(owners):
            first = owner * pad + index * group
            packed[first : first + group] = across[owner * group : (owner + 1) * group]
    for owner in range(owners):
        kv_ref[owner] = packed[owner * pad : owner * pad + 2 * group].astype(BF16)


def key_value_part(shards, ids, w_key, w_value, owners):
    count, rows, depth = shards.shape
    channels = w_key.shape[1]
    group = channels // owners
    return pl.pallas_call(
        functools.partial(key_value_kernel, group),
        in_specs=in_vmem(3) + in_smem(1),
        out_specs=in_vmem(1)[0],
        out_shape=jax.ShapeDtypeStruct((owners, 2 * group, rows), BF16),
        scratch_shapes=[
            pltpu.VMEM((rows, channels), F32),
            pltpu.VMEM((channels, rows), F32),
            pltpu.VMEM((owners * padded(2 * group), rows), F32),
        ],
        compiler_params=params(24),
        cost_estimate=call_cost(4 * count * rows * depth * channels, 12_000_000),
    )(shards, w_key, w_value, ids)


def query_kernel(after_ref, shards_ref, weight_ref, ids_ref, query_ref, total):
    projected(shards_ref, ids_ref, weight_ref, total)
    query_ref[...] = total[...].astype(BF16)


def query_part(after, shards, ids, w_query):
    count, rows, depth = shards.shape
    channels = w_query.shape[1]
    return pl.pallas_call(
        query_kernel,
        in_specs=anywhere(1) + in_vmem(2) + in_smem(1),
        out_specs=in_vmem(1)[0],
        out_shape=jax.ShapeDtypeStruct((rows, channels), BF16),
        scratch_shapes=[pltpu.VMEM((rows, channels), F32)],
        compiler_params=params(14),
        cost_estimate=call_cost(2 * count * rows * depth * channels, 6_000_000),
    )(after, shards, w_query, ids)


def gated_grad_kernel(
    group, kv_ref, shards_ref, weight_ref, query_ref, ids_ref, gated_ref, grouped_ref, total, across,
):
    count, _, depth = shards_ref.shape
    total[...] = jnp.zeros_like(total)

    def add(tile):
        first = pl.multiple_of(ids_ref[tile] * depth, LANE)
        total[...] += dot_nt(shards_ref[tile], weight_ref[:, pl.ds(first, depth)])

    tiles_of(count, add)
    gated = total[...].astype(BF16)
    gated_ref[...] = gated
    across[...] = (gated.astype(F32) * query_ref[...].astype(F32)).T
    for owner in range(grouped_ref.shape[0]):
        grouped_ref[owner, : 2 * group] = kv_ref[owner]
        grouped_ref[owner, 2 * group :] = across[owner * group : (owner + 1) * group].astype(BF16)


def gated_grad_part(kv, shards, ids, w_out, query):
    count, rows, depth = shards.shape
    channels = w_out.shape[0]
    owners = kv.shape[0]
    group = channels // owners
    return pl.pallas_call(
        functools.partial(gated_grad_kernel, group),
        in_specs=in_vmem(4) + in_smem(1),
        out_specs=tuple(in_vmem(2)),
        out_shape=(
            jax.ShapeDtypeStruct((rows, channels), BF16),
            jax.ShapeDtypeStruct((owners, 3 * group, rows), BF16),
        ),
        scratch_shapes=[pltpu.VMEM((rows, channels), F32), pltpu.VMEM((channels, rows), F32)],
        compiler_params=params(18),
        cost_estimate=call_cost(2 * count * rows * depth * channels, 9_000_000),
    )(kv, shards, w_out, query, ids)


def unpack_kernel(
    group, returned_ref, query_ref, gated_ref, forward_ref, query_grad_ref, key_ref, value_ref,
    response_rows, value_rows, key_rows,
):
    for owner in range(returned_ref.shape[0]):
        piece = returned_ref[owner].astype(F32)
        at = slice(owner * group, (owner + 1) * group)
        response_rows[at] = piece[:group]
        value_rows[at] = piece[group : 2 * group]
        key_rows[at] = piece[2 * group : 3 * group]
    response = response_rows[...].T
    forward_ref[...] = (query_ref[...].astype(F32) * response).astype(BF16)
    query_grad_ref[...] = (gated_ref[...].astype(F32) * response).astype(BF16)
    value_ref[...] = value_rows[...].T.astype(BF16)
    key_ref[...] = key_rows[...].T.astype(BF16)


def unpack_part(returned, query, gated):
    rows, channels = query.shape
    return pl.pallas_call(
        functools.partial(unpack_kernel, channels // returned.shape[0]),
        in_specs=in_vmem(3),
        out_specs=tuple(in_vmem(4)),
        out_shape=(jax.ShapeDtypeStruct((rows, channels), BF16),) * 4,
        scratch_shapes=[pltpu.VMEM((channels, rows), F32)] * 3,
        compiler_params=params(12),
        cost_estimate=call_cost(4 * rows * channels, 5_000_000),
    )(returned, query, gated)


def turn_kernel(after_ref, first_ref, second_ref, first_out, second_out, first, second, sems):
    count = first.shape[0]

    def copy_out(index, tile):
        held, target = ((first, first_out), (second, second_out))[index]
        return pltpu.make_async_copy(held.at[tile], target.at[tile], sems.at[index, tile])

    def turn(tile):
        first[tile] = first_ref[tile].T
        copy_out(0, tile).start()
        second[tile] = second_ref[tile].T
        copy_out(1, tile).start()

    def finish(tile):
        copy_out(0, tile).wait()
        copy_out(1, tile).wait()

    tiles_of(count, turn)
    tiles_of(count, finish)


def turn_part(after, first, second):
    count, rows, depth = first.shape
    out = jax.ShapeDtypeStruct((count, depth, rows), BF16)
    return pl.pallas_call(
        turn_kernel,
        in_specs=anywhere(1) + in_vmem(2),
        out_specs=tuple(anywhere(2)),
        out_shape=(out, out),
        scratch_shapes=[pltpu.VMEM(out.shape, BF16)] * 2 + [pltpu.SemaphoreType.DMA((2, count))],
        compiler_params=params(16),
        cost_estimate=call_cost(2 * count * depth * rows, 8_000_000),
    )(after, first, second)


def weight_kernel(rows, unread, *refs):
    (
        wide_ref, narrow_ref, ids_ref, core_ref, keep_out, send_out, keep, send, keep_sems,
        send_sems,
    ) = refs[unread:]
    tiles, held = keep.shape[:2]

    def copies(tile):
        at = pl.ds(ids_ref[tile] * held, held)
        return (
            pltpu.make_async_copy(send.at[tile], send_out.at[at], send_sems.at[tile]),
            pltpu.make_async_copy(keep.at[tile], keep_out.at[at], keep_sems.at[tile]),
        )

    def multiply(tile):
        result = dot_nn(wide_ref[tile], narrow_ref[...]).astype(BF16)
        for core in range(2):

            @pl.when(core_ref[0] == core)
            def _():
                for chip in range(held):
                    at = (2 * chip + core) * rows
                    other = (2 * chip + 1 - core) * rows
                    keep[tile, chip] = result[at : at + rows]
                    send[tile, chip] = result[other : other + rows]

        for copy in copies(tile):
            copy.start()

    def finish(tile):
        for copy in copies(tile):
            copy.wait()

    tiles_of(tiles, multiply)
    tiles_of(tiles, finish)


def weight_partial(after, wide, ids, narrow, core, chips):
    tiles, height, depth = wide.shape
    width = narrow.shape[1]
    total = tiles * height
    rows = total // (2 * chips)
    halves = pltpu.VMEM((tiles, chips // tiles, rows, width), BF16)
    return pl.pallas_call(
        functools.partial(weight_kernel, rows, len(after)),
        in_specs=anywhere(len(after)) + in_vmem(2) + in_smem(2),
        out_specs=tuple(anywhere(2)),
        out_shape=(jax.ShapeDtypeStruct((chips, rows, width), BF16),) * 2,
        scratch_shapes=[halves, halves]
        + [pltpu.SemaphoreType.DMA((tiles,)), pltpu.SemaphoreType.DMA((tiles,))],
        compiler_params=params(16),
        cost_estimate=call_cost(2 * total * depth * width, 6_000_000),
    )(*after, wide, narrow, ids, core)


def mixed_kernel(after_ref, gated_ref, weight_ref, out_ref, result, sems):
    count, _, width = out_ref.shape

    def copy_out(tile):
        return pltpu.make_async_copy(result.at[tile], out_ref.at[tile], sems.at[tile])

    def multiply(tile):
        result[tile] = dot_nn(gated_ref[...], weight_ref[:, columns_of(tile, width)]).astype(BF16)
        copy_out(tile).start()

    tiles_of(count, multiply)
    tiles_of(count, lambda tile: copy_out(tile).wait())


def mixed_part(after, gated, w_out, count):
    rows, depth = gated.shape
    width = w_out.shape[1] // count
    return pl.pallas_call(
        mixed_kernel,
        in_specs=anywhere(1) + in_vmem(2),
        out_specs=anywhere(1)[0],
        out_shape=jax.ShapeDtypeStruct((count, rows, width), BF16),
        scratch_shapes=[
            pltpu.VMEM((count, rows, width), BF16), pltpu.SemaphoreType.DMA((count,)),
        ],
        compiler_params=params(14),
        cost_estimate=call_cost(2 * rows * depth * width * count, 6_000_000),
    )(after, gated, w_out)


def input_kernel(unread, *refs):
    *pairs, out_ref, result, sems = refs[unread:]
    half = len(pairs) // 2
    count, _, width = out_ref.shape

    def copy_out(tile):
        return pltpu.make_async_copy(result.at[tile], out_ref.at[tile], sems.at[tile])

    def multiply(tile):
        at = rows_of(tile, width)
        total = dot_nt(pairs[0][...], pairs[half][at, :])
        for index in range(1, half):
            total += dot_nt(pairs[index][...], pairs[half + index][at, :])
        result[tile] = total.astype(BF16)
        copy_out(tile).start()

    tiles_of(count, multiply)
    tiles_of(count, lambda tile: copy_out(tile).wait())


def input_part(after, backs, weights, count):
    rows, depth = backs[0].shape
    width = weights[0].shape[0] // count
    return pl.pallas_call(
        functools.partial(input_kernel, len(after)),
        in_specs=anywhere(len(after)) + in_vmem(len(backs) + len(weights)),
        out_specs=anywhere(1)[0],
        out_shape=jax.ShapeDtypeStruct((count, rows, width), BF16),
        scratch_shapes=[
            pltpu.VMEM((count, rows, width), BF16), pltpu.SemaphoreType.DMA((count,)),
        ],
        compiler_params=params(22),
        cost_estimate=call_cost(6 * rows * depth * width * count, 14_000_000),
    )(*after, *backs, *weights)


def moved(value, axis, steps):
    by_core = steps if isinstance(steps, tuple) else (steps, steps)
    pairs = []
    for x in range(SIDE):
        for y in range(SIDE):
            for core in range(2):
                for z in range(SIDE):
                    goal = [x, y, core, z]
                    if axis == "core":
                        goal[2] = 1 - core
                    else:
                        at = {"x": 0, "y": 1, "z": 3}[axis]
                        goal[at] = (goal[at] + by_core[core]) % SIDE
                    pairs.append(
                        tuple(
                            ((a * SIDE + b) * 2 + c) * SIDE + d
                            for a, b, c, d in ((x, y, core, z), goal)
                        )
                    )
    return lax.ppermute(value, ("seq", "tp"), pairs)


def added(left, right):
    return (left.astype(F32) + right.astype(F32)).astype(BF16)


def picked(value, axis=0):
    return lambda index: lax.dynamic_index_in_dim(value, index, axis, keepdims=False)


def ring_sum(travelling, block, place, up, axis, steps):
    for step in steps:
        travelling = added(moved(travelling, axis, (1, -1)), block((place - step * up) % SIDE))
    return travelling


class SeqSum:
    def __init__(self, halves, first, places, up):
        keep, send = halves
        _, rows, width = keep.shape
        grid = (SIDE, SIDE, rows, width)
        axis = "xy".index(first)
        self.first, self.second = first, "yx"[axis]
        self.places, self.up = places, up
        self.keep = picked(keep.reshape(grid), axis)
        self.came = picked(moved(send, "core", 1).reshape(grid), axis)
        self.start = self.block((places[first] - up) % SIDE)
        self.held = None

    def block(self, index):
        return added(self.keep(index), self.came(index))

    def ring(self, travelling, steps):
        return ring_sum(
            travelling, self.block, self.places[self.first], self.up, self.first, steps
        )

    def step(self):
        if self.held is None:
            self.held = self.ring(self.start, (2,))
        return self.held

    def total(self):
        half = self.ring(self.step(), range(3, SIDE + 1))
        place = self.places[self.second]
        block = picked(half)
        start = block((place - self.up) % SIDE)
        return ring_sum(start, block, place, self.up, self.second, range(2, SIDE + 1)).astype(F32)


def per_device(
    tokens,
    w_query,
    w_key,
    w_value,
    w_out,
    shift_filter,
    log_decay,
    readout,
    skip_gain,
    init_state,
    cotangent,
):
    row_count = tokens.shape[0]
    channels = w_query.shape[1]
    tap_count = shift_filter.shape[0]
    seq_count = lax.axis_size("seq")
    group = channels // seq_count
    position = lax.axis_index("seq")
    core = position % 2
    chip_z = lax.axis_index("tp")
    places = {"x": position // (2 * SIDE), "y": (position // 2) % SIDE}
    core_word = core.reshape(1)

    token_sides = moved(tokens, "z", 1), moved(tokens, "z", -1)
    grad_sides = moved(cotangent, "z", 1), moved(cotangent, "z", -1)

    def all_shards(mine, sides):
        below, above = sides
        far = moved(jnp.where(core == 0, below, above), "z", (1, -1))
        return jnp.stack([mine, below, above, far])

    shards = all_shards(tokens, token_sides)
    grad_shards = all_shards(cotangent, grad_sides)
    ids = (chip_z + jnp.array([0, SIDE - 1, 1, 2], jnp.int32)) % SIDE

    def own(value):
        return lax.dynamic_slice_in_dim(value, position * group, group, value.ndim - 1)

    own_rate, own_read, own_init, own_taps = (
        own(value).T for value in (log_decay, readout, init_state, shift_filter)
    )
    own_taps = jnp.pad(own_taps, ((0, 0), (0, LANE - tap_count)))
    taps = jnp.stack([own_taps, jnp.roll(own_taps[:, ::-1], 1, axis=1)])
    rows = jnp.stack([own_rate, own_init])
    cols = jnp.stack([own_rate, own_read])[..., None]
    skip = own(skip_gain)

    def exchanged(value):
        return lax.all_to_all(value, "seq", 0, 0, tiled=True)

    kv = key_value_part(shards, ids, w_key, w_value, seq_count)
    query = query_part(kv, shards, ids, w_query)
    gated_grad, packed = gated_grad_part(kv, grad_shards, ids, w_out, query)
    results = sequence_part(exchanged(packed), rows, cols, taps, skip)
    shards_turned, grad_turned = turn_part(results, shards, grad_shards)
    returned = exchanged(results)
    gated, back_query, back_key, back_value = unpack_part(returned, query, gated_grad)
    chips = SIDE * SIDE
    up = 1 - 2 * core

    def weight(after, wide, narrow):
        return weight_partial(after, wide, ids, narrow, core_word, chips)

    out_halves = weight((gated,), grad_turned, gated)
    out_sum = SeqSum(out_halves, "x", places, up)
    query_halves = weight((out_halves[1],), shards_turned, back_query)
    query_sum = SeqSum(query_halves, "y", places, up)
    partial_mixed = mixed_part(query_halves[1], gated, w_out, SIDE)
    mixed = lax.psum_scatter(partial_mixed, "tp", scatter_dimension=0, tiled=True)[0]
    key_halves = weight((partial_mixed,), shards_turned, back_key)
    key_sum = SeqSum(key_halves, "x", places, up)
    value_halves = weight((key_halves[1], out_sum.start), shards_turned, back_value)
    value_sum = SeqSum(value_halves, "y", places, up)
    out_first, query_first = out_sum.step(), query_sum.step()
    out_first, value_sum.start = lax.optimization_barrier((out_first, value_sum.start))
    out_sum.held = out_first
    partial_input = input_part(
        (value_halves[1], out_first, query_first, key_sum.start, value_sum.start),
        (back_query, back_key, back_value),
        (w_query, w_key, w_value),
        SIDE,
    )
    returned, query_sum.held, partial_input = lax.optimization_barrier(
        (returned, query_first, partial_input)
    )
    grad_input = lax.psum_scatter(partial_input, "tp", scatter_dimension=0, tiled=True)[0]
    small = returned[:, 3 * group :].reshape(seq_count, -1, row_count // LANE, LANE)
    small = small.transpose(0, 2, 1, 3).reshape(seq_count, -1, LANE)[:, :group]
    small = small.reshape(channels, LANE).T.astype(F32)
    grad_filter, grad_init = small[:tap_count], small[tap_count:]

    grad_out, grad_query, grad_key, grad_value = (
        each.total() for each in (out_sum, query_sum, key_sum, value_sum)
    )
    grad_out = grad_out.T
    return (mixed, grad_input, grad_query, grad_key, grad_value, grad_out, grad_filter, grad_init)


def solution(mesh):
    return jax.shard_map(
        per_device,
        mesh=mesh,
        in_specs=(
            P("seq", "tp"),
            P(None, "tp"),
            P(None, "tp"),
            P(None, "tp"),
            P("tp", None),
            P(None, "tp"),
            P(None, "tp"),
            P(None, "tp"),
            P("tp"),
            P(None, "tp"),
            P("seq", "tp"),
        ),
        out_specs=(
            P("seq", "tp"),
            P("seq", "tp"),
            P("seq", "tp"),
            P("seq", "tp"),
            P("seq", "tp"),
            P("tp", "seq"),
            P(None, "tp"),
            P(None, "tp"),
        ),
        check_vma=False,
    )
```

```python
import functools

import jax
import jax.numpy as jnp
from jax import lax
from jax.experimental import pallas as pl
from jax.experimental.pallas import tpu as pltpu
from jax.sharding import PartitionSpec as P

LANE = 128
F32 = jnp.float32
BF16 = jnp.bfloat16


def dot_nn(left, right):
    return lax.dot_general(left, right, (((1,), (0,)), ((), ())), preferred_element_type=F32)


def dot_nt(left, right):
    return lax.dot_general(left, right, (((1,), (1,)), ((), ())), preferred_element_type=F32)


def dot_tn(left, right):
    return lax.dot_general(left, right, (((0,), (0,)), ((), ())), preferred_element_type=F32)


def dot_tt(left, right):
    return lax.dot_general(left, right, (((0,), (1,)), ((), ())), preferred_element_type=F32)


def split_pair(value):
    high = value.astype(BF16)
    return high, (value - high.astype(F32)).astype(BF16)


SIDE = 4
MIB = 1024 * 1024


def call_cost(flops, bytes_accessed, transcendentals=0):
    return pl.CostEstimate(
        flops=flops, bytes_accessed=bytes_accessed, transcendentals=transcendentals
    )


def params(mebibytes):
    return pltpu.CompilerParams(vmem_limit_bytes=mebibytes * MIB)


def in_vmem(count):
    return [pl.BlockSpec(memory_space=pltpu.VMEM)] * count


def in_smem(count):
    return [pl.BlockSpec(memory_space=pltpu.SMEM)] * count


def in_hbm(count):
    return [pl.BlockSpec(memory_space=pltpu.HBM)] * count


def anywhere(count):
    return [pl.BlockSpec(memory_space=pl.ANY)] * count


def padded(rows):
    return -(-rows // 8) * 8


def later(value, steps, source_at):
    at = source_at[:, : value.shape[1]]
    return jnp.where(at >= steps, pltpu.roll(value, steps, 0), 0.0)


def earlier(value, steps, source_at):
    sources = value.shape[0]
    at = source_at[:, : value.shape[1]]
    return jnp.where(at < sources - steps, pltpu.roll(value, sources - steps, 0), 0.0)


def circulant(row):
    return pltpu.roll(jnp.broadcast_to(row, (LANE, LANE)), 0, 1, stride=1, stride_axis=0)


def iotas(sources):
    lane_at = lax.broadcasted_iota(jnp.int32, (LANE, LANE), 1)
    row_at = lax.broadcasted_iota(jnp.int32, (LANE, LANE), 0)
    source_at = lax.broadcasted_iota(jnp.int32, (sources, LANE), 0)
    return lane_at, row_at, source_at


def decay_tables(cols_ref, channel, lane_at):
    rate = cols_ref[0, channel]
    read = cols_ref[1, channel]
    lanes = lane_at[: rate.shape[0]].astype(F32)
    step_decay = jnp.exp(-rate)
    inflow = 1.0 - step_decay
    rising = jnp.exp(-rate * lanes)
    falling = jnp.exp(-rate * (LANE - 1.0 - lanes))
    reading = (read * step_decay) * rising
    feeding = inflow * falling
    weight = read * inflow
    kernel_row = jnp.sum(weight * rising, axis=0, keepdims=True)
    wrapped = jnp.where(lanes > 0.0, step_decay * falling, 1.0)
    kernel_turned = jnp.sum(weight * wrapped, axis=0, keepdims=True)
    return reading.astype(BF16), feeding.astype(BF16), kernel_row, kernel_turned


def part_rows(value, sources):
    return [value[at : at + sources] for at in range(0, value.shape[0], sources)]


def load_rows(ref, row, sources, pad, parts):
    return [
        ref[pl.ds(row + part * sources * pad, sources, stride=pad), :] for part in range(parts)
    ]


def store_rows(ref, row, sources, pad, value):
    for part, piece in enumerate(part_rows(value, sources)):
        ref[pl.ds(row + part * sources * pad, sources, stride=pad), :] = piece


def spread(block_ref, rows_ref, pad):
    sources, count, width = block_ref.shape

    def step(source, carry):
        for part in range(width // LANE):
            row = pl.multiple_of((part * sources + source) * pad, 8)
            rows_ref[pl.ds(row, count), :] = block_ref[
                source, :, LANE * part : LANE * (part + 1)
            ].astype(F32)
        return carry

    lax.fori_loop(0, sources, step, 0)


def channel_body(
    channel, sources, parts, group, at, in_rows, out_rows, small_rows, rows_ref, cols_ref,
    taps_ref, skip_ref,
):
    lane_at, row_at, source_at = at
    in_pad, out_pad = padded(3 * group), padded(2 * group) + padded(group)
    key = load_rows(in_rows, channel, sources, in_pad, parts)
    value = jnp.concatenate(load_rows(in_rows, channel + group, sources, in_pad, parts), 0)
    grads = jnp.concatenate(load_rows(in_rows, channel + 2 * group, sources, in_pad, parts), 0)
    rate_row = rows_ref[0, pl.ds(channel, 1), :]
    start_row = rows_ref[1, pl.ds(channel, 1), :]
    states = rate_row.shape[1]
    reading, feeding, kernel_row, kernel_turned = decay_tables(cols_ref, channel, lane_at)
    ahead, behind = lane_at >= row_at, lane_at <= row_at
    local = jnp.where(ahead, circulant(kernel_row), 0.0).astype(BF16)
    local_turned = jnp.where(behind, circulant(kernel_turned), 0.0).astype(BF16)
    taps = circulant(taps_ref[0, pl.ds(channel, 1), :])
    taps_turned = circulant(taps_ref[1, pl.ds(channel, 1), :])
    taps_forward = jnp.concatenate(
        [jnp.where(ahead, 0.0, taps), jnp.where(ahead, taps, 0.0)], 0
    ).astype(BF16)
    taps_back = jnp.concatenate(
        [jnp.where(behind, taps_turned, 0.0), jnp.where(behind, 0.0, taps_turned)], 0
    ).astype(BF16)
    skip = skip_ref[channel]
    part_decay = jnp.exp(-rate_row * LANE)
    row_decay = jnp.exp(-rate_row * (LANE * parts))

    key_now = jnp.concatenate(key, 0)
    key_before = jnp.concatenate([later(key[-1], 1, source_at)] + key[:-1], 0)
    key_pair = jnp.concatenate([key_before, key_now], 1).astype(BF16)
    shifted = dot_nn(key_pair, taps_forward)
    drive = shifted * value
    drive_short = drive.astype(BF16)

    fed = part_rows(dot_nt(drive_short, feeding), sources)
    whole = fed[0]
    for part in range(1, parts):
        whole = part_decay * whole + fed[part]
    scan = jnp.where(source_at[:, :states] >= 1, pltpu.roll(whole, 1, 0), start_row)
    step, decay = 1, row_decay
    while step < sources:
        scan = scan + decay * later(scan, step, source_at)
        step, decay = 2 * step, decay * decay
    entering = [scan]
    for part in range(1, parts):
        entering.append(part_decay * entering[-1] + fed[part - 1])
    state_high, state_low = split_pair(jnp.concatenate(entering, 0))
    response = (
        dot_nn(
            jnp.concatenate([drive_short, state_high, state_low], 1),
            jnp.concatenate([local, reading, reading], 0),
        )
        + skip * drive
    )

    grad_short = grads.astype(BF16)
    read = part_rows(dot_nt(grad_short, reading), sources)
    whole = read[-1]
    for part in range(parts - 2, -1, -1):
        whole = part_decay * whole + read[part]
    scan = earlier(whole, 1, source_at)
    step, decay = 1, row_decay
    while step < sources:
        scan = scan + decay * earlier(scan, step, source_at)
        step, decay = 2 * step, decay * decay
    leaving = [scan]
    for part in range(parts - 1, 0, -1):
        leaving.insert(0, part_decay * leaving[0] + read[part])
    start_grad = (part_decay * leaving[0] + read[0])[0:1]
    carry_high, carry_low = split_pair(jnp.concatenate(leaving, 0))
    back_drive = (
        dot_nn(
            jnp.concatenate([grad_short, carry_high, carry_low], 1),
            jnp.concatenate([local_turned, feeding, feeding], 0),
        )
        + skip * grads
    )
    back_value = back_drive * shifted
    back_shifted = back_drive * value
    pieces = part_rows(back_shifted, sources)
    back_after = jnp.concatenate(pieces[1:] + [earlier(pieces[0], 1, source_at)], 0)
    back_short = back_shifted.astype(BF16)
    back_pair = jnp.concatenate([back_short, back_after.astype(BF16)], 1)
    back_key = dot_nn(back_pair, taps_back)

    gram = dot_tn(key_pair, back_short)
    gram = jnp.where(ahead, gram[LANE:], gram[:LANE])
    aligned = gram[:8]
    for first in range(8, LANE, 8):
        aligned = aligned + pltpu.roll(gram[first : first + 8], LANE - first, 1)
    for bit in (1, 2, 4):
        aligned = jnp.where((row_at[:8] & bit) > 0, pltpu.roll(aligned, LANE - bit, 1), aligned)
    filter_grad = jnp.sum(aligned, axis=0, keepdims=True)[:, : LANE - states]
    small_rows[pl.ds(channel, 1), :] = jnp.concatenate([filter_grad, start_grad], 1)
    for index, result in enumerate((response, back_value, back_key)):
        store_rows(out_rows, channel + index * group, sources, out_pad, result)


UNROLL = 4


def sequence_kernel(
    group, in_ref, rows_ref, cols_ref, taps_ref, skip_ref, out_ref, in_rows, out_rows, small_rows,
):
    sources, _, width = in_ref.shape
    parts = width // LANE
    spread(in_ref, in_rows, padded(3 * group))
    small_rows[...] = jnp.zeros_like(small_rows)
    at = iotas(sources)

    def step(index, carry):
        for inner in range(UNROLL):
            channel_body(
                index * UNROLL + inner, sources, parts, group, at, in_rows, out_rows, small_rows,
                rows_ref, cols_ref, taps_ref, skip_ref,
            )
        return carry

    lax.fori_loop(0, group // UNROLL, step, 0)
    out_pad = padded(2 * group) + padded(group)
    extra = out_ref.shape[1] - 3 * group

    def pack(source, carry):
        for part in range(parts):
            row = pl.multiple_of((part * sources + source) * out_pad, 8)
            columns = slice(LANE * part, LANE * (part + 1))
            out_ref[source, : 3 * group, columns] = out_rows[pl.ds(row, 3 * group), :].astype(
                BF16
            )
            out_ref[source, 3 * group :, columns] = small_rows[
                extra * part : extra * (part + 1)
            ].astype(BF16)
        return carry

    lax.fori_loop(0, sources, pack, 0)


def sequence_part(value, rows, cols, taps, skip):
    sources, triple, width = value.shape
    group = triple // 3
    parts = width // LANE
    lines = sources * parts
    extra = -(-group // parts)
    return pl.pallas_call(
        functools.partial(sequence_kernel, group),
        out_shape=jax.ShapeDtypeStruct((sources, triple + extra, width), BF16),
        in_specs=in_vmem(4) + in_smem(1),
        out_specs=in_vmem(1)[0],
        scratch_shapes=[
            pltpu.VMEM((lines * padded(triple), LANE), F32),
            pltpu.VMEM((lines * (padded(2 * group) + padded(group)), LANE), F32),
            pltpu.VMEM((padded(extra * parts), LANE), F32),
        ],
        compiler_params=params(24),
        cost_estimate=call_cost(22_000_000_000, 5_000_000),
    )(value, rows, cols, taps, skip)


def tiles_of(count, body):
    def step(tile, carry):
        body(tile)
        return carry

    lax.fori_loop(0, count, step, 0)


def columns_of(tile, width):
    return pl.ds(pl.multiple_of(tile * width, LANE), width)


def rows_of(tile, height):
    return pl.ds(pl.multiple_of(tile * height, 16), height)


def weight_rows(weight_ref, ids_ref, tile, depth):
    return weight_ref[rows_of(ids_ref[tile], depth), :]


def near_kernel(shard_count, *refs):
    shards, rest = refs[:shard_count], refs[shard_count:]
    half = (len(rest) - 1) // 2
    weights, ids_ref, sums = rest[:half], rest[half], rest[half + 1 :]
    depth = shards[0].shape[1]
    for weight_ref, sum_ref in zip(weights, sums):
        total = dot_nn(shards[0][...], weight_rows(weight_ref, ids_ref, 0, depth))
        for tile in range(1, shard_count):
            total += dot_nn(shards[tile][...], weight_rows(weight_ref, ids_ref, tile, depth))
        sum_ref[...] = total


def near_part(shards, weights, ids):
    rows, depth = shards[0].shape
    channels = weights[0].shape[1]
    return pl.pallas_call(
        functools.partial(near_kernel, len(shards)),
        in_specs=in_vmem(len(shards) + len(weights)) + in_smem(1),
        out_specs=tuple(in_vmem(len(weights))),
        out_shape=(jax.ShapeDtypeStruct((rows, channels), F32),) * len(weights),
        compiler_params=params(24),
        cost_estimate=call_cost(
            2 * len(shards) * len(weights) * rows * depth * channels, 12_000_000
        ),
    )(*shards, *weights, ids)


def far_kernel(
    group, shard_ref, key_ref, value_ref, query_ref, key_sum, value_sum, query_sum, ids_ref,
    kv_ref, query_out, across, packed,
):
    depth = shard_ref.shape[1]
    tile = ids_ref.shape[0] - 1
    pad = padded(2 * group)
    owners = kv_ref.shape[0]
    for index, (weight_ref, sum_ref) in enumerate(((key_ref, key_sum), (value_ref, value_sum))):
        part = dot_nn(shard_ref[...], weight_rows(weight_ref, ids_ref, tile, depth))
        across[...] = (sum_ref[...] + part).T
        for owner in range(owners):
            first = owner * pad + index * group
            packed[first : first + group] = across[owner * group : (owner + 1) * group]
    for owner in range(owners):
        kv_ref[owner] = packed[owner * pad : owner * pad + 2 * group].astype(BF16)
    part = dot_nn(shard_ref[...], weight_rows(query_ref, ids_ref, tile, depth))
    query_out[...] = (query_sum[...] + part).astype(BF16)


def far_part(shard, weights, sums, ids, owners):
    rows, depth = shard.shape
    channels = weights[0].shape[1]
    group = channels // owners
    return pl.pallas_call(
        functools.partial(far_kernel, group),
        in_specs=in_vmem(7) + in_smem(1),
        out_specs=tuple(in_vmem(2)),
        out_shape=(
            jax.ShapeDtypeStruct((owners, 2 * group, rows), BF16),
            jax.ShapeDtypeStruct((rows, channels), BF16),
        ),
        scratch_shapes=[
            pltpu.VMEM((channels, rows), F32),
            pltpu.VMEM((owners * padded(2 * group), rows), F32),
        ],
        compiler_params=params(24),
        cost_estimate=call_cost(6 * rows * depth * channels, 12_000_000),
    )(shard, *weights, *sums, ids)


def grad_near_kernel(after_ref, first_ref, second_ref, third_ref, weight_ref, ids_ref, sum_ref):
    depth = first_ref.shape[1]

    def part(tile, shard_ref):
        first = pl.multiple_of(ids_ref[tile] * depth, LANE)
        return dot_nt(shard_ref[...], weight_ref[:, pl.ds(first, depth)])

    sum_ref[...] = part(0, first_ref) + part(1, second_ref) + part(2, third_ref)


def grad_near_part(after, shards, w_out, ids):
    rows, depth = shards[0].shape
    channels = w_out.shape[0]
    return pl.pallas_call(
        grad_near_kernel,
        in_specs=anywhere(1) + in_vmem(4) + in_smem(1),
        out_specs=in_vmem(1)[0],
        out_shape=jax.ShapeDtypeStruct((rows, channels), F32),
        compiler_params=params(16),
        cost_estimate=call_cost(6 * rows * depth * channels, 6_000_000),
    )(after, *shards, w_out, ids)


def grad_far_kernel(
    group, kv_ref, shard_ref, weight_ref, sum_ref, query_ref, ids_ref, gated_ref, grouped_ref,
    across,
):
    depth = shard_ref.shape[1]
    first = pl.multiple_of(ids_ref[ids_ref.shape[0] - 1] * depth, LANE)
    total = sum_ref[...] + dot_nt(shard_ref[...], weight_ref[:, pl.ds(first, depth)])
    gated = total.astype(BF16)
    gated_ref[...] = gated
    across[...] = (gated.astype(F32) * query_ref[...].astype(F32)).T
    for owner in range(grouped_ref.shape[0]):
        grouped_ref[owner, : 2 * group] = kv_ref[owner]
        grouped_ref[owner, 2 * group :] = across[owner * group : (owner + 1) * group].astype(BF16)


def grad_far_part(kv, shard, w_out, total, query, ids):
    rows, depth = shard.shape
    channels = w_out.shape[0]
    owners = kv.shape[0]
    group = channels // owners
    return pl.pallas_call(
        functools.partial(grad_far_kernel, group),
        in_specs=in_vmem(5) + in_smem(1),
        out_specs=tuple(in_vmem(2)),
        out_shape=(
            jax.ShapeDtypeStruct((rows, channels), BF16),
            jax.ShapeDtypeStruct((owners, 3 * group, rows), BF16),
        ),
        scratch_shapes=[pltpu.VMEM((channels, rows), F32)],
        compiler_params=params(16),
        cost_estimate=call_cost(2 * rows * depth * channels, 6_000_000),
    )(kv, shard, w_out, total, query, ids)


def unpack_kernel(
    group, returned_ref, query_ref, gated_ref, forward_ref, query_grad_ref, key_ref, value_ref,
    filter_ref, init_ref, response_rows, value_rows, key_rows, small_rows,
):
    owners, lines, width = returned_ref.shape
    extra = lines - 3 * group
    for owner in range(owners):
        piece = returned_ref[owner].astype(F32)
        at = slice(owner * group, (owner + 1) * group)
        response_rows[at] = piece[:group]
        value_rows[at] = piece[group : 2 * group]
        key_rows[at] = piece[2 * group : 3 * group]
        for part in range(width // LANE):
            count = min(extra, group - extra * part)
            first = owner * group + extra * part
            small_rows[first : first + count] = piece[
                3 * group : 3 * group + count, LANE * part : LANE * (part + 1)
            ]
    response = response_rows[...].T
    forward_ref[...] = (query_ref[...].astype(F32) * response).astype(BF16)
    query_grad_ref[...] = (gated_ref[...].astype(F32) * response).astype(BF16)
    value_ref[...] = value_rows[...].T.astype(BF16)
    key_ref[...] = key_rows[...].T.astype(BF16)
    small = small_rows[...].T
    taps = filter_ref.shape[0]
    filter_ref[...] = small[:taps]
    init_ref[...] = small[taps:]


def unpack_part(returned, query, gated, taps):
    rows, channels = query.shape
    short = jax.ShapeDtypeStruct((rows, channels), BF16)
    return pl.pallas_call(
        functools.partial(unpack_kernel, channels // returned.shape[0]),
        in_specs=in_vmem(3),
        out_specs=tuple(in_vmem(6)),
        out_shape=(
            short, short, short, short,
            jax.ShapeDtypeStruct((taps, channels), F32),
            jax.ShapeDtypeStruct((LANE - taps, channels), F32),
        ),
        scratch_shapes=[pltpu.VMEM((channels, rows), F32)] * 3
        + [pltpu.VMEM((channels, LANE), F32)],
        compiler_params=params(14),
        cost_estimate=call_cost(4 * rows * channels, 5_000_000),
    )(returned, query, gated)


def turn_kernel(after_ref, *refs):
    count = (len(refs) - 5) // 2
    shards, (first_out, second_out, first, second, sems) = refs[:-5], refs[-5:]
    held = ((first, first_out), (second, second_out))
    sent = []
    for index, ref in enumerate(shards):
        which, tile = index // count, index % count
        source, target = held[which]
        source[tile] = ref[...].T
        sent.append(
            pltpu.make_async_copy(source.at[tile], target.at[tile], sems.at[which, tile])
        )
        sent[-1].start()
    for copy in sent:
        copy.wait()


def turn_part(after, first, second):
    rows, depth = first[0].shape
    count = len(first)
    out = jax.ShapeDtypeStruct((count, depth, rows), BF16)
    return pl.pallas_call(
        turn_kernel,
        in_specs=anywhere(1) + in_vmem(2 * count),
        out_specs=tuple(in_hbm(2)),
        out_shape=(out, out),
        scratch_shapes=[pltpu.VMEM(out.shape, BF16)] * 2 + [pltpu.SemaphoreType.DMA((2, count))],
        compiler_params=params(16),
        cost_estimate=call_cost(2 * count * depth * rows, 8_000_000),
    )(after, *first, *second)


def weight_kernel(rows, count, after_ref, wide_ref, *refs):
    narrows, (ids_ref, core_ref), refs = refs[:count], refs[count : count + 2], refs[count + 2 :]
    outs, (keep, send, sems) = refs[: 2 * count], refs[2 * count :]
    tiles, held = keep.shape[1:3]

    def copies(tile, index):
        at = pl.ds(ids_ref[tile] * held, held)
        return (
            pltpu.make_async_copy(
                keep.at[index, tile], outs[2 * index].at[at], sems.at[0, index, tile]
            ),
            pltpu.make_async_copy(
                send.at[index, tile], outs[2 * index + 1].at[at], sems.at[1, index, tile]
            ),
        )

    def multiply(tile):
        for index in range(count):
            result = dot_nn(wide_ref[tile], narrows[index][...]).astype(BF16)
            for core in range(2):

                @pl.when(core_ref[0] == core)
                def _():
                    for chip in range(held):
                        at = (2 * chip + core) * rows
                        other = (2 * chip + 1 - core) * rows
                        keep[index, tile, chip] = result[at : at + rows]
                        send[index, tile, chip] = result[other : other + rows]

            for copy in copies(tile, index):
                copy.start()

    def finish(tile):
        for index in range(count):
            for copy in copies(tile, index):
                copy.wait()

    tiles_of(tiles, multiply)
    tiles_of(tiles, finish)


def weight_partial(after, wide, ids, narrows, core, chips):
    tiles, height, depth = wide.shape
    width = narrows[0].shape[1]
    total = tiles * height
    rows = total // (2 * chips)
    count = len(narrows)
    halves = pltpu.VMEM((count, tiles, chips // tiles, rows, width), BF16)
    flat = pl.pallas_call(
        functools.partial(weight_kernel, rows, count),
        in_specs=anywhere(1) + in_vmem(1 + count) + in_smem(2),
        out_specs=tuple(in_hbm(2 * count)),
        out_shape=(jax.ShapeDtypeStruct((chips, rows, width), BF16),) * (2 * count),
        scratch_shapes=[halves, halves, pltpu.SemaphoreType.DMA((2, count, tiles))],
        compiler_params=params(12 + 6 * count),
        cost_estimate=call_cost(2 * count * total * depth * width, 6_000_000 * count),
    )(after, wide, *narrows, ids, core)
    return [flat[2 * index : 2 * index + 2] for index in range(count)]


def mixed_kernel(after_ref, gated_ref, weight_ref, out_ref, result, sems):
    count, _, width = out_ref.shape

    def copy_out(tile):
        return pltpu.make_async_copy(result.at[tile], out_ref.at[tile], sems.at[tile])

    def multiply(tile):
        result[tile] = dot_nn(gated_ref[...], weight_ref[:, columns_of(tile, width)]).astype(BF16)
        copy_out(tile).start()

    tiles_of(count, multiply)
    tiles_of(count, lambda tile: copy_out(tile).wait())


def mixed_part(after, gated, w_out, count):
    rows, depth = gated.shape
    width = w_out.shape[1] // count
    return pl.pallas_call(
        mixed_kernel,
        in_specs=anywhere(1) + in_vmem(2),
        out_specs=in_hbm(1)[0],
        out_shape=jax.ShapeDtypeStruct((count, rows, width), BF16),
        scratch_shapes=[
            pltpu.VMEM((count, rows, width), BF16), pltpu.SemaphoreType.DMA((count,)),
        ],
        compiler_params=params(14),
        cost_estimate=call_cost(2 * rows * depth * width * count, 6_000_000),
    )(after, gated, w_out)


def input_kernel(unread, *refs):
    *pairs, out_ref, result, sems = refs[unread:]
    half = len(pairs) // 2
    count, _, width = out_ref.shape

    def copy_out(tile):
        return pltpu.make_async_copy(result.at[tile], out_ref.at[tile], sems.at[tile])

    def multiply(tile):
        at = rows_of(tile, width)
        total = dot_nt(pairs[0][...], pairs[half][at, :])
        for index in range(1, half):
            total += dot_nt(pairs[index][...], pairs[half + index][at, :])
        result[tile] = total.astype(BF16)
        copy_out(tile).start()

    tiles_of(count, multiply)
    tiles_of(count, lambda tile: copy_out(tile).wait())


def input_part(after, backs, weights, count):
    rows, depth = backs[0].shape
    width = weights[0].shape[0] // count
    return pl.pallas_call(
        functools.partial(input_kernel, len(after)),
        in_specs=anywhere(len(after)) + in_vmem(len(backs) + len(weights)),
        out_specs=in_hbm(1)[0],
        out_shape=jax.ShapeDtypeStruct((count, rows, width), BF16),
        scratch_shapes=[
            pltpu.VMEM((count, rows, width), BF16), pltpu.SemaphoreType.DMA((count,)),
        ],
        compiler_params=params(22),
        cost_estimate=call_cost(6 * rows * depth * width * count, 14_000_000),
    )(*after, *backs, *weights)


def moved(value, axis, steps):
    by_core = steps if isinstance(steps, tuple) else (steps, steps)
    pairs = []
    for x in range(SIDE):
        for y in range(SIDE):
            for core in range(2):
                for z in range(SIDE):
                    goal = [x, y, core, z]
                    if axis == "core":
                        goal[2] = 1 - core
                    else:
                        at = {"x": 0, "y": 1, "z": 3}[axis]
                        goal[at] = (goal[at] + by_core[core]) % SIDE
                    pairs.append(
                        tuple(
                            ((a * SIDE + b) * 2 + c) * SIDE + d
                            for a, b, c, d in ((x, y, core, z), goal)
                        )
                    )
    return lax.ppermute(value, ("seq", "tp"), pairs)


def added(left, right):
    return (left.astype(F32) + right.astype(F32)).astype(BF16)


def picked(value, axis=0):
    return lambda index: lax.dynamic_index_in_dim(value, index, axis, keepdims=False)


def ring_sum(travelling, block, place, up, axis, steps):
    for step in steps:
        travelling = added(moved(travelling, axis, (1, -1)), block((place - step * up) % SIDE))
    return travelling


def summed_over_seq(halves, first, places, up):
    keep, came = halves
    _, rows, width = keep.shape
    grid = (SIDE, SIDE, rows, width)
    axis = "xy".index(first)
    second = "yx"[axis]
    keep = picked(keep.reshape(grid), axis)
    came = picked(came.reshape(grid), axis)

    def block(index):
        return added(keep(index), came(index))

    place = places[first]
    half = ring_sum(block((place - up) % SIDE), block, place, up, first, range(2, SIDE + 1))
    place, mine = places[second], picked(half)
    total = mine(place).astype(F32)
    for step in (1, -1, 2):
        steps = (2, -2) if step == 2 else step
        total += moved(mine((place + step) % SIDE), second, steps).astype(F32)
    return total


def per_device(
    tokens,
    w_query,
    w_key,
    w_value,
    w_out,
    shift_filter,
    log_decay,
    readout,
    skip_gain,
    init_state,
    cotangent,
):
    row_count = tokens.shape[0]
    channels = w_query.shape[1]
    tap_count = shift_filter.shape[0]
    seq_count = lax.axis_size("seq")
    group = channels // seq_count
    position = lax.axis_index("seq")
    core = position % 2
    chip_z = lax.axis_index("tp")
    places = {"x": position // (2 * SIDE), "y": (position // 2) % SIDE}
    core_word = core.reshape(1)

    token_sides = moved(tokens, "z", 1), moved(tokens, "z", -1)
    grad_sides = moved(cotangent, "z", 1), moved(cotangent, "z", -1)

    def all_shards(mine, sides):
        below, above = sides
        far = moved(jnp.where(core == 0, below, above), "z", (1, -1))
        return mine, below, above, far

    shards = all_shards(tokens, token_sides)
    grad_shards = all_shards(cotangent, grad_sides)
    ids = (chip_z + jnp.array([0, SIDE - 1, 1, 2], jnp.int32)) % SIDE

    def own(value):
        return lax.dynamic_slice_in_dim(value, position * group, group, value.ndim - 1)

    own_rate, own_read, own_init, own_taps = (
        own(value).T for value in (log_decay, readout, init_state, shift_filter)
    )
    own_taps = jnp.pad(own_taps, ((0, 0), (0, LANE - tap_count)))
    taps = jnp.stack([own_taps, jnp.roll(own_taps[:, ::-1], 1, axis=1)])
    rows = jnp.stack([own_rate, own_init])
    cols = jnp.stack([own_rate, own_read])[..., None]
    skip = own(skip_gain)

    def exchanged(value):
        return lax.all_to_all(value, "seq", 0, 0, tiled=True)

    weights = (w_key, w_value, w_query)
    sums = near_part(shards[:3], weights, ids)
    grad_sum = grad_near_part(sums[2], grad_shards[:3], w_out, ids)
    kv, query = far_part(shards[3], weights, sums, ids, seq_count)
    gated_grad, packed = grad_far_part(kv, grad_shards[3], w_out, grad_sum, query, ids)
    results = sequence_part(exchanged(packed), rows, cols, taps, skip)
    shards_turned, grad_turned = turn_part(results, shards, grad_shards)
    returned = exchanged(results)
    gated, back_query, back_key, back_value, grad_filter, grad_init = unpack_part(
        returned, query, gated_grad, tap_count
    )
    chips = SIDE * SIDE
    up = 1 - 2 * core

    (out_halves,) = weight_partial(gated, grad_turned, ids, (gated,), core_word, chips)
    query_halves, key_halves, value_halves = weight_partial(
        out_halves[1], shards_turned, ids, (back_query, back_key, back_value), core_word, chips
    )
    partial_mixed = mixed_part(query_halves[1], gated, w_out, SIDE)
    mixed = lax.psum_scatter(partial_mixed, "tp", scatter_dimension=0, tiled=True)[0]
    swapped = [
        (keep, moved(send, "core", 1))
        for keep, send in (out_halves, query_halves, key_halves, value_halves)
    ]
    partial_input = input_part(
        (partial_mixed, swapped[0][1], swapped[1][1], swapped[2][1]), (back_query, back_key, back_value), (w_query, w_key, w_value), SIDE
    )
    grad_input = lax.psum_scatter(partial_input, "tp", scatter_dimension=0, tiled=True)[0]
    grad_out, grad_query, grad_key, grad_value = (
        summed_over_seq(halves, first, places, up)
        for halves, first in zip(swapped, "xyxy")
    )
    grad_out = grad_out.T
    return (mixed, grad_input, grad_query, grad_key, grad_value, grad_out, grad_filter, grad_init)


def solution(mesh):
    return jax.shard_map(
        per_device,
        mesh=mesh,
        in_specs=(
            P("seq", "tp"),
            P(None, "tp"),
            P(None, "tp"),
            P(None, "tp"),
            P("tp", None),
            P(None, "tp"),
            P(None, "tp"),
            P(None, "tp"),
            P("tp"),
            P(None, "tp"),
            P("seq", "tp"),
        ),
        out_specs=(
            P("seq", "tp"),
            P("seq", "tp"),
            P("seq", "tp"),
            P("seq", "tp"),
            P("seq", "tp"),
            P("tp", "seq"),
            P(None, "tp"),
            P(None, "tp"),
        ),
        check_vma=False,
    )
```

```python
import functools

import jax
import jax.numpy as jnp
from jax import lax
from jax.experimental import pallas as pl
from jax.experimental.pallas import tpu as pltpu
from jax.sharding import PartitionSpec as P

LANE = 128
F32 = jnp.float32
BF16 = jnp.bfloat16


def dot_nn(left, right):
    return lax.dot_general(left, right, (((1,), (0,)), ((), ())), preferred_element_type=F32)


def dot_nt(left, right):
    return lax.dot_general(left, right, (((1,), (1,)), ((), ())), preferred_element_type=F32)


def dot_tn(left, right):
    return lax.dot_general(left, right, (((0,), (0,)), ((), ())), preferred_element_type=F32)


def dot_tt(left, right):
    return lax.dot_general(left, right, (((0,), (1,)), ((), ())), preferred_element_type=F32)


def split_pair(value):
    high = value.astype(BF16)
    return high, (value - high.astype(F32)).astype(BF16)


SIDE = 4
MIB = 1024 * 1024


def call_cost(flops, bytes_accessed, transcendentals=0):
    return pl.CostEstimate(
        flops=flops, bytes_accessed=bytes_accessed, transcendentals=transcendentals
    )


def params(mebibytes):
    return pltpu.CompilerParams(vmem_limit_bytes=mebibytes * MIB)


def in_vmem(count):
    return [pl.BlockSpec(memory_space=pltpu.VMEM)] * count


def in_smem(count):
    return [pl.BlockSpec(memory_space=pltpu.SMEM)] * count


def in_hbm(count):
    return [pl.BlockSpec(memory_space=pltpu.HBM)] * count


def anywhere(count):
    return [pl.BlockSpec(memory_space=pl.ANY)] * count


TICK = jax.ShapeDtypeStruct((8, LANE), F32)


def padded(rows):
    return -(-rows // 8) * 8


def later(value, steps, source_at):
    at = source_at[:, : value.shape[1]]
    return jnp.where(at >= steps, pltpu.roll(value, steps, 0), 0.0)


def earlier(value, steps, source_at):
    sources = value.shape[0]
    at = source_at[:, : value.shape[1]]
    return jnp.where(at < sources - steps, pltpu.roll(value, sources - steps, 0), 0.0)


def circulant(row):
    return pltpu.roll(jnp.broadcast_to(row, (LANE, LANE)), 0, 1, stride=1, stride_axis=0)


def iotas(sources):
    lane_at = lax.broadcasted_iota(jnp.int32, (LANE, LANE), 1)
    row_at = lax.broadcasted_iota(jnp.int32, (LANE, LANE), 0)
    source_at = lax.broadcasted_iota(jnp.int32, (sources, LANE), 0)
    return lane_at, row_at, source_at


def decay_tables(cols_ref, channel, lane_at):
    rate = cols_ref[0, channel]
    read = cols_ref[1, channel]
    lanes = lane_at[: rate.shape[0]].astype(F32)
    step_decay = jnp.exp(-rate)
    inflow = 1.0 - step_decay
    rising = jnp.exp(-rate * lanes)
    falling = jnp.exp(-rate * (LANE - 1.0 - lanes))
    reading = (read * step_decay) * rising
    feeding = inflow * falling
    weight = read * inflow
    kernel_row = jnp.sum(weight * rising, axis=0, keepdims=True)
    wrapped = jnp.where(lanes > 0.0, step_decay * falling, 1.0)
    kernel_turned = jnp.sum(weight * wrapped, axis=0, keepdims=True)
    return reading.astype(BF16), feeding.astype(BF16), kernel_row, kernel_turned


def part_rows(value, sources):
    return [value[at : at + sources] for at in range(0, value.shape[0], sources)]


def load_rows(ref, row, sources, pad, parts):
    return [
        ref[pl.ds(row + part * sources * pad, sources, stride=pad), :] for part in range(parts)
    ]


def store_rows(ref, row, sources, pad, value):
    for part, piece in enumerate(part_rows(value, sources)):
        ref[pl.ds(row + part * sources * pad, sources, stride=pad), :] = piece


def spread(block_ref, rows_ref, pad):
    sources, count, width = block_ref.shape

    def step(source, carry):
        for part in range(width // LANE):
            row = pl.multiple_of((part * sources + source) * pad, 8)
            rows_ref[pl.ds(row, count), :] = block_ref[
                source, :, LANE * part : LANE * (part + 1)
            ].astype(F32)
        return carry

    lax.fori_loop(0, sources, step, 0)


def channel_body(
    channel, sources, parts, group, at, in_rows, out_rows, small_rows, rows_ref, cols_ref,
    taps_ref, skip_ref,
):
    lane_at, row_at, source_at = at
    in_pad, out_pad = padded(3 * group), padded(2 * group) + padded(group)
    key = load_rows(in_rows, channel, sources, in_pad, parts)
    value = jnp.concatenate(load_rows(in_rows, channel + group, sources, in_pad, parts), 0)
    grads = jnp.concatenate(load_rows(in_rows, channel + 2 * group, sources, in_pad, parts), 0)
    rate_row = rows_ref[0, pl.ds(channel, 1), :]
    start_row = rows_ref[1, pl.ds(channel, 1), :]
    states = rate_row.shape[1]
    reading, feeding, kernel_row, kernel_turned = decay_tables(cols_ref, channel, lane_at)
    ahead, behind = lane_at >= row_at, lane_at <= row_at
    local = jnp.where(ahead, circulant(kernel_row), 0.0).astype(BF16)
    local_turned = jnp.where(behind, circulant(kernel_turned), 0.0).astype(BF16)
    taps = circulant(taps_ref[0, pl.ds(channel, 1), :])
    taps_turned = circulant(taps_ref[1, pl.ds(channel, 1), :])
    taps_forward = jnp.concatenate(
        [jnp.where(ahead, 0.0, taps), jnp.where(ahead, taps, 0.0)], 0
    ).astype(BF16)
    taps_back = jnp.concatenate(
        [jnp.where(behind, taps_turned, 0.0), jnp.where(behind, 0.0, taps_turned)], 0
    ).astype(BF16)
    skip = skip_ref[channel]
    part_decay = jnp.exp(-rate_row * LANE)
    row_decay = jnp.exp(-rate_row * (LANE * parts))

    key_now = jnp.concatenate(key, 0)
    key_before = jnp.concatenate([later(key[-1], 1, source_at)] + key[:-1], 0)
    key_pair = jnp.concatenate([key_before, key_now], 1).astype(BF16)
    shifted = dot_nn(key_pair, taps_forward)
    drive = shifted * value
    drive_short = drive.astype(BF16)

    fed = part_rows(dot_nt(drive_short, feeding), sources)
    whole = fed[0]
    for part in range(1, parts):
        whole = part_decay * whole + fed[part]
    scan = jnp.where(source_at[:, :states] >= 1, pltpu.roll(whole, 1, 0), start_row)
    step, decay = 1, row_decay
    while step < sources:
        scan = scan + decay * later(scan, step, source_at)
        step, decay = 2 * step, decay * decay
    entering = [scan]
    for part in range(1, parts):
        entering.append(part_decay * entering[-1] + fed[part - 1])
    state_high, state_low = split_pair(jnp.concatenate(entering, 0))
    response = (
        dot_nn(
            jnp.concatenate([drive_short, state_high, state_low], 1),
            jnp.concatenate([local, reading, reading], 0),
        )
        + skip * drive
    )

    grad_short = grads.astype(BF16)
    read = part_rows(dot_nt(grad_short, reading), sources)
    whole = read[-1]
    for part in range(parts - 2, -1, -1):
        whole = part_decay * whole + read[part]
    scan = earlier(whole, 1, source_at)
    step, decay = 1, row_decay
    while step < sources:
        scan = scan + decay * earlier(scan, step, source_at)
        step, decay = 2 * step, decay * decay
    leaving = [scan]
    for part in range(parts - 1, 0, -1):
        leaving.insert(0, part_decay * leaving[0] + read[part])
    start_grad = (part_decay * leaving[0] + read[0])[0:1]
    carry_high, carry_low = split_pair(jnp.concatenate(leaving, 0))
    back_drive = (
        dot_nn(
            jnp.concatenate([grad_short, carry_high, carry_low], 1),
            jnp.concatenate([local_turned, feeding, feeding], 0),
        )
        + skip * grads
    )
    back_value = back_drive * shifted
    back_shifted = back_drive * value
    pieces = part_rows(back_shifted, sources)
    back_after = jnp.concatenate(pieces[1:] + [earlier(pieces[0], 1, source_at)], 0)
    back_short = back_shifted.astype(BF16)
    back_pair = jnp.concatenate([back_short, back_after.astype(BF16)], 1)
    back_key = dot_nn(back_pair, taps_back)

    gram = dot_tn(key_pair, back_short)
    gram = jnp.where(ahead, gram[LANE:], gram[:LANE])
    aligned = gram[:8]
    for first in range(8, LANE, 8):
        aligned = aligned + pltpu.roll(gram[first : first + 8], LANE - first, 1)
    for bit in (1, 2, 4):
        aligned = jnp.where((row_at[:8] & bit) > 0, pltpu.roll(aligned, LANE - bit, 1), aligned)
    filter_grad = jnp.sum(aligned, axis=0, keepdims=True)[:, : LANE - states]
    small_rows[pl.ds(channel, 1), :] = jnp.concatenate([filter_grad, start_grad], 1)
    for index, result in enumerate((response, back_value, back_key)):
        store_rows(out_rows, channel + index * group, sources, out_pad, result)


UNROLL = 4


def sequence_kernel(
    group, after_ref, in_ref, rows_ref, cols_ref, taps_ref, skip_ref, out_ref, in_rows, out_rows,
    small_rows,
):
    sources, _, width = in_ref.shape
    parts = width // LANE
    spread(in_ref, in_rows, padded(3 * group))
    small_rows[...] = jnp.zeros_like(small_rows)
    at = iotas(sources)

    def step(index, carry):
        for inner in range(UNROLL):
            channel_body(
                index * UNROLL + inner, sources, parts, group, at, in_rows, out_rows, small_rows,
                rows_ref, cols_ref, taps_ref, skip_ref,
            )
        return carry

    lax.fori_loop(0, group // UNROLL, step, 0)
    out_pad = padded(2 * group) + padded(group)
    extra = out_ref.shape[1] - 3 * group

    def pack(source, carry):
        for part in range(parts):
            row = pl.multiple_of((part * sources + source) * out_pad, 8)
            columns = slice(LANE * part, LANE * (part + 1))
            out_ref[source, : 3 * group, columns] = out_rows[pl.ds(row, 3 * group), :].astype(
                BF16
            )
            out_ref[source, 3 * group :, columns] = small_rows[
                extra * part : extra * (part + 1)
            ].astype(BF16)
        return carry

    lax.fori_loop(0, sources, pack, 0)


def sequence_part(after, value, rows, cols, taps, skip):
    sources, triple, width = value.shape
    group = triple // 3
    parts = width // LANE
    lines = sources * parts
    extra = -(-group // parts)
    return pl.pallas_call(
        functools.partial(sequence_kernel, group),
        out_shape=jax.ShapeDtypeStruct((sources, triple + extra, width), BF16),
        in_specs=anywhere(1) + in_vmem(4) + in_smem(1),
        out_specs=in_vmem(1)[0],
        scratch_shapes=[
            pltpu.VMEM((lines * padded(triple), LANE), F32),
            pltpu.VMEM((lines * (padded(2 * group) + padded(group)), LANE), F32),
            pltpu.VMEM((padded(extra * parts), LANE), F32),
        ],
        compiler_params=params(24),
        cost_estimate=call_cost(22_000_000_000, 5_000_000),
    )(after, value, rows, cols, taps, skip)


def tiles_of(count, body):
    def step(tile, carry):
        body(tile)
        return carry

    lax.fori_loop(0, count, step, 0)


def columns_of(tile, width):
    return pl.ds(pl.multiple_of(tile * width, LANE), width)


def rows_of(tile, height):
    return pl.ds(pl.multiple_of(tile * height, 16), height)


def weight_rows(weight_ref, ids_ref, tile, depth):
    return weight_ref[rows_of(ids_ref[tile], depth), :]


def near_kernel(shard_count, *refs):
    shards, rest = refs[:shard_count], refs[shard_count:]
    half = (len(rest) - 1) // 2
    weights, ids_ref, sums = rest[:half], rest[half], rest[half + 1 :]
    depth = shards[0].shape[1]
    for weight_ref, sum_ref in zip(weights, sums):
        total = dot_nn(shards[0][...], weight_rows(weight_ref, ids_ref, 0, depth))
        for tile in range(1, shard_count):
            total += dot_nn(shards[tile][...], weight_rows(weight_ref, ids_ref, tile, depth))
        sum_ref[...] = total


def near_part(shards, weights, ids):
    rows, depth = shards[0].shape
    channels = weights[0].shape[1]
    return pl.pallas_call(
        functools.partial(near_kernel, len(shards)),
        in_specs=in_vmem(len(shards) + len(weights)) + in_smem(1),
        out_specs=tuple(in_vmem(len(weights))),
        out_shape=(jax.ShapeDtypeStruct((rows, channels), F32),) * len(weights),
        compiler_params=params(24),
        cost_estimate=call_cost(
            2 * len(shards) * len(weights) * rows * depth * channels, 12_000_000
        ),
    )(*shards, *weights, ids)


def far_kernel(
    group, shard_ref, key_ref, value_ref, query_ref, key_sum, value_sum, query_sum, ids_ref,
    kv_ref, query_out, across, packed,
):
    depth = shard_ref.shape[1]
    tile = ids_ref.shape[0] - 1
    pad = padded(2 * group)
    owners = kv_ref.shape[0]
    for index, (weight_ref, sum_ref) in enumerate(((key_ref, key_sum), (value_ref, value_sum))):
        part = dot_nn(shard_ref[...], weight_rows(weight_ref, ids_ref, tile, depth))
        across[...] = (sum_ref[...] + part).T
        for owner in range(owners):
            first = owner * pad + index * group
            packed[first : first + group] = across[owner * group : (owner + 1) * group]
    for owner in range(owners):
        kv_ref[owner] = packed[owner * pad : owner * pad + 2 * group].astype(BF16)
    part = dot_nn(shard_ref[...], weight_rows(query_ref, ids_ref, tile, depth))
    query_out[...] = (query_sum[...] + part).astype(BF16)


def far_part(shard, weights, sums, ids, owners):
    rows, depth = shard.shape
    channels = weights[0].shape[1]
    group = channels // owners
    return pl.pallas_call(
        functools.partial(far_kernel, group),
        in_specs=in_vmem(7) + in_smem(1),
        out_specs=tuple(in_vmem(2)),
        out_shape=(
            jax.ShapeDtypeStruct((owners, 2 * group, rows), BF16),
            jax.ShapeDtypeStruct((rows, channels), BF16),
        ),
        scratch_shapes=[
            pltpu.VMEM((channels, rows), F32),
            pltpu.VMEM((owners * padded(2 * group), rows), F32),
        ],
        compiler_params=params(24),
        cost_estimate=call_cost(6 * rows * depth * channels, 12_000_000),
    )(shard, *weights, *sums, ids)


def grad_near_kernel(after_ref, first_ref, second_ref, third_ref, weight_ref, ids_ref, sum_ref):
    depth = first_ref.shape[1]

    def part(tile, shard_ref):
        first = pl.multiple_of(ids_ref[tile] * depth, LANE)
        return dot_nt(shard_ref[...], weight_ref[:, pl.ds(first, depth)])

    sum_ref[...] = part(0, first_ref) + part(1, second_ref) + part(2, third_ref)


def grad_near_part(after, shards, w_out, ids):
    rows, depth = shards[0].shape
    channels = w_out.shape[0]
    return pl.pallas_call(
        grad_near_kernel,
        in_specs=anywhere(1) + in_vmem(4) + in_smem(1),
        out_specs=in_vmem(1)[0],
        out_shape=jax.ShapeDtypeStruct((rows, channels), F32),
        compiler_params=params(16),
        cost_estimate=call_cost(6 * rows * depth * channels, 6_000_000),
    )(after, *shards, w_out, ids)


def grad_far_kernel(
    group, kv_ref, shard_ref, weight_ref, sum_ref, query_ref, ids_ref, gated_ref, grouped_ref,
    across,
):
    depth = shard_ref.shape[1]
    first = pl.multiple_of(ids_ref[ids_ref.shape[0] - 1] * depth, LANE)
    total = sum_ref[...] + dot_nt(shard_ref[...], weight_ref[:, pl.ds(first, depth)])
    gated = total.astype(BF16)
    gated_ref[...] = gated
    across[...] = (gated.astype(F32) * query_ref[...].astype(F32)).T
    for owner in range(grouped_ref.shape[0]):
        grouped_ref[owner, : 2 * group] = kv_ref[owner]
        grouped_ref[owner, 2 * group :] = across[owner * group : (owner + 1) * group].astype(BF16)


def grad_far_part(kv, shard, w_out, total, query, ids):
    rows, depth = shard.shape
    channels = w_out.shape[0]
    owners = kv.shape[0]
    group = channels // owners
    return pl.pallas_call(
        functools.partial(grad_far_kernel, group),
        in_specs=in_vmem(5) + in_smem(1),
        out_specs=tuple(in_vmem(2)),
        out_shape=(
            jax.ShapeDtypeStruct((rows, channels), BF16),
            jax.ShapeDtypeStruct((owners, 3 * group, rows), BF16),
        ),
        scratch_shapes=[pltpu.VMEM((channels, rows), F32)],
        compiler_params=params(16),
        cost_estimate=call_cost(2 * rows * depth * channels, 6_000_000),
    )(kv, shard, w_out, total, query, ids)


def unpack_kernel(
    group, returned_ref, query_ref, gated_ref, forward_ref, query_grad_ref, key_ref, value_ref,
    filter_ref, init_ref, response_rows, value_rows, key_rows, small_rows,
):
    owners, lines, width = returned_ref.shape
    extra = lines - 3 * group
    for owner in range(owners):
        piece = returned_ref[owner].astype(F32)
        at = slice(owner * group, (owner + 1) * group)
        response_rows[at] = piece[:group]
        value_rows[at] = piece[group : 2 * group]
        key_rows[at] = piece[2 * group : 3 * group]
        for part in range(width // LANE):
            count = min(extra, group - extra * part)
            first = owner * group + extra * part
            small_rows[first : first + count] = piece[
                3 * group : 3 * group + count, LANE * part : LANE * (part + 1)
            ]
    response = response_rows[...].T
    forward_ref[...] = (query_ref[...].astype(F32) * response).astype(BF16)
    query_grad_ref[...] = (gated_ref[...].astype(F32) * response).astype(BF16)
    value_ref[...] = value_rows[...].T.astype(BF16)
    key_ref[...] = key_rows[...].T.astype(BF16)
    small = small_rows[...].T
    taps = filter_ref.shape[0]
    filter_ref[...] = small[:taps]
    init_ref[...] = small[taps:]


def unpack_part(returned, query, gated, taps):
    rows, channels = query.shape
    short = jax.ShapeDtypeStruct((rows, channels), BF16)
    return pl.pallas_call(
        functools.partial(unpack_kernel, channels // returned.shape[0]),
        in_specs=in_vmem(3),
        out_specs=tuple(in_vmem(6)),
        out_shape=(
            short, short, short, short,
            jax.ShapeDtypeStruct((taps, channels), F32),
            jax.ShapeDtypeStruct((LANE - taps, channels), F32),
        ),
        scratch_shapes=[pltpu.VMEM((channels, rows), F32)] * 3
        + [pltpu.VMEM((channels, LANE), F32)],
        compiler_params=params(14),
        cost_estimate=call_cost(4 * rows * channels, 5_000_000),
    )(returned, query, gated)


def turn_kernel(after_ref, *refs):
    count = (len(refs) - 6) // 2
    shards, (first_out, second_out, tick_ref, first, second, sems) = refs[:-6], refs[-6:]
    tick_ref[...] = jnp.zeros_like(tick_ref)
    held = ((first, first_out), (second, second_out))
    sent = []
    for index, ref in enumerate(shards):
        which, tile = index // count, index % count
        source, target = held[which]
        source[tile] = ref[...].T
        sent.append(
            pltpu.make_async_copy(source.at[tile], target.at[tile], sems.at[which, tile])
        )
        sent[-1].start()
    for copy in sent:
        copy.wait()


def turn_part(after, first, second):
    rows, depth = first[0].shape
    count = len(first)
    out = jax.ShapeDtypeStruct((count, depth, rows), BF16)
    return pl.pallas_call(
        turn_kernel,
        in_specs=anywhere(1) + in_vmem(2 * count),
        out_specs=tuple(in_hbm(2) + in_vmem(1)),
        out_shape=(out, out, TICK),
        scratch_shapes=[pltpu.VMEM(out.shape, BF16)] * 2 + [pltpu.SemaphoreType.DMA((2, count))],
        compiler_params=params(16),
        cost_estimate=call_cost(2 * count * depth * rows, 8_000_000),
    )(after, *first, *second)


def hold_kernel(after_ref, *refs):
    count = (len(refs) - 1) // 2
    sources, targets, sems = refs[:count], refs[count:-1], refs[-1]
    copies = [
        pltpu.make_async_copy(source, target, sems.at[index])
        for index, (source, target) in enumerate(zip(sources, targets))
    ]
    for copy in copies:
        copy.start()
    for copy in copies:
        copy.wait()


def held_in_vmem(after, values):
    count = len(values)
    return pl.pallas_call(
        hold_kernel,
        in_specs=anywhere(1) + in_hbm(count),
        out_specs=tuple(in_vmem(count)),
        out_shape=tuple(jax.ShapeDtypeStruct(value.shape, value.dtype) for value in values),
        scratch_shapes=[pltpu.SemaphoreType.DMA((count,))],
        compiler_params=params(16),
        cost_estimate=call_cost(0, 26_000_000),
    )(after, *values)


def weight_kernel(
    rows, after_ref, wide_ref, narrow_ref, ids_ref, core_ref, keep_ref, send_ref, tick_ref
):
    tick_ref[...] = jnp.zeros_like(tick_ref)
    tiles = wide_ref.shape[0]
    held = keep_ref.shape[0] // tiles

    def multiply(tile):
        result = dot_nn(wide_ref[tile], narrow_ref[...]).astype(BF16)
        first = ids_ref[tile] * held
        for core in range(2):

            @pl.when(core_ref[0] == core)
            def _():
                for chip in range(held):
                    at = (2 * chip + core) * rows
                    other = (2 * chip + 1 - core) * rows
                    keep_ref[first + chip] = result[at : at + rows]
                    send_ref[first + chip] = result[other : other + rows]

    tiles_of(tiles, multiply)


def weight_partial(after, wide, ids, narrow, core, chips):
    tiles, height, depth = wide.shape
    width = narrow.shape[1]
    total = tiles * height
    rows = total // (2 * chips)
    return pl.pallas_call(
        functools.partial(weight_kernel, rows),
        in_specs=anywhere(1) + in_vmem(2) + in_smem(2),
        out_specs=tuple(in_vmem(3)),
        out_shape=(jax.ShapeDtypeStruct((chips, rows, width), BF16),) * 2 + (TICK,),
        compiler_params=params(14),
        cost_estimate=call_cost(2 * total * depth * width, 6_000_000),
    )(after, wide, narrow, ids, core)


def outward_kernel(unread, *refs):
    (
        query_ref, key_ref, value_ref, gated_ref, query_weight, key_weight, value_weight,
        out_weight, out_ref, result, sems,
    ) = refs[unread:]
    count, height, width = out_ref.shape
    rows = height // 2

    def copy_out(tile):
        return pltpu.make_async_copy(result.at[tile], out_ref.at[tile], sems.at[tile])

    def multiply(tile):
        result[tile, :rows] = dot_nn(
            gated_ref[...], out_weight[:, columns_of(tile, width)]
        ).astype(BF16)
        at = rows_of(tile, width)
        total = dot_nt(query_ref[...], query_weight[at, :])
        total += dot_nt(key_ref[...], key_weight[at, :])
        total += dot_nt(value_ref[...], value_weight[at, :])
        result[tile, rows:] = total.astype(BF16)
        copy_out(tile).start()

    tiles_of(count, multiply)
    tiles_of(count, lambda tile: copy_out(tile).wait())


def outward_part(after, backs, gated, weights, count):
    rows, depth = gated.shape
    width = weights[0].shape[0] // count
    shape = (count, 2 * rows, width)
    return pl.pallas_call(
        functools.partial(outward_kernel, len(after)),
        in_specs=anywhere(len(after)) + in_vmem(8),
        out_specs=in_hbm(1)[0],
        out_shape=jax.ShapeDtypeStruct(shape, BF16),
        scratch_shapes=[pltpu.VMEM(shape, BF16), pltpu.SemaphoreType.DMA((count,))],
        compiler_params=params(24),
        cost_estimate=call_cost(8 * rows * depth * width * count, 20_000_000),
    )(*after, *backs, gated, *weights)


def moved(value, axis, steps):
    by_core = steps if isinstance(steps, tuple) else (steps, steps)
    pairs = []
    for x in range(SIDE):
        for y in range(SIDE):
            for core in range(2):
                for z in range(SIDE):
                    goal = [x, y, core, z]
                    if axis == "core":
                        goal[2] = 1 - core
                    else:
                        at = {"x": 0, "y": 1, "z": 3}[axis]
                        goal[at] = (goal[at] + by_core[core]) % SIDE
                    pairs.append(
                        tuple(
                            ((a * SIDE + b) * 2 + c) * SIDE + d
                            for a, b, c, d in ((x, y, core, z), goal)
                        )
                    )
    return lax.ppermute(value, ("seq", "tp"), pairs)


def added(left, right):
    return (left.astype(F32) + right.astype(F32)).astype(BF16)


def picked(value, axis=0):
    return lambda index: lax.dynamic_index_in_dim(value, index, axis, keepdims=False)


def ring_sum(travelling, block, place, up, axis, steps):
    for step in steps:
        travelling = added(moved(travelling, axis, (1, -1)), block((place - step * up) % SIDE))
    return travelling


class FirstAxis:
    def __init__(self, halves, first, places, up):
        keep, came = halves
        _, rows, width = keep.shape
        grid = (SIDE, SIDE, rows, width)
        axis = "xy".index(first)
        self.keep, self.came = picked(keep.reshape(grid), axis), picked(came.reshape(grid), axis)
        self.first, self.place, self.up = first, places[first], up
        self.start = self.block((self.place - up) % SIDE)

    def block(self, index):
        return added(self.keep(index), self.came(index))

    def total(self):
        return ring_sum(
            self.start, self.block, self.place, self.up, self.first, range(2, SIDE + 1)
        )


def second_axis_sums(halves, second, places):
    place = places[second]

    def mine(step):
        return jnp.stack([picked(half)((place + step) % SIDE) for half in halves])

    total = mine(0).astype(F32)
    for step in (1, -1, 2):
        steps = (2, -2) if step == 2 else step
        total += moved(mine(step), second, steps).astype(F32)
    return [total[index] for index in range(len(halves))]


def per_device(
    tokens,
    w_query,
    w_key,
    w_value,
    w_out,
    shift_filter,
    log_decay,
    readout,
    skip_gain,
    init_state,
    cotangent,
):
    row_count = tokens.shape[0]
    channels = w_query.shape[1]
    tap_count = shift_filter.shape[0]
    seq_count = lax.axis_size("seq")
    group = channels // seq_count
    position = lax.axis_index("seq")
    core = position % 2
    chip_z = lax.axis_index("tp")
    places = {"x": position // (2 * SIDE), "y": (position // 2) % SIDE}
    core_word = core.reshape(1)

    token_sides = moved(tokens, "z", 1), moved(tokens, "z", -1)
    grad_sides = moved(cotangent, "z", 1), moved(cotangent, "z", -1)

    def passed(sides):
        below, above = sides
        return jnp.where(core == 0, below, above)

    held = held_in_vmem(skip_gain, (w_key, w_value, w_query, w_out))
    tokens_on, _ = lax.optimization_barrier((passed(token_sides), held[0]))
    grad_sides, tokens_on = lax.optimization_barrier((grad_sides, tokens_on))
    grads_on = passed(grad_sides)
    shards = (tokens, *token_sides, moved(tokens_on, "z", (1, -1)))
    grad_shards = (cotangent, *grad_sides, moved(grads_on, "z", (1, -1)))
    ids = (chip_z + jnp.array([0, SIDE - 1, 1, 2], jnp.int32)) % SIDE

    def own(value):
        return lax.dynamic_slice_in_dim(value, position * group, group, value.ndim - 1)

    own_rate, own_read, own_init, own_taps = (
        own(value).T for value in (log_decay, readout, init_state, shift_filter)
    )
    own_taps = jnp.pad(own_taps, ((0, 0), (0, LANE - tap_count)))
    taps = jnp.stack([own_taps, jnp.roll(own_taps[:, ::-1], 1, axis=1)])
    rows = jnp.stack([own_rate, own_init])
    cols = jnp.stack([own_rate, own_read])[..., None]
    skip = own(skip_gain)

    def exchanged(value):
        return lax.all_to_all(value, "seq", 0, 0, tiled=True)

    weights = held[:3]
    sums = near_part(shards[:3], weights, ids)
    grad_sum = grad_near_part(sums[2], grad_shards[:3], held[3], ids)
    kv, query = far_part(shards[3], weights, sums, ids, seq_count)
    gated_grad, packed = grad_far_part(kv, grad_shards[3], held[3], grad_sum, query, ids)
    shards_turned, grad_turned, turned = turn_part(packed, shards, grad_shards)
    results = sequence_part(turned, exchanged(packed), rows, cols, taps, skip)
    returned = exchanged(results)
    gated, back_query, back_key, back_value, grad_filter, grad_init = unpack_part(
        returned, query, gated_grad, tap_count
    )
    chips = SIDE * SIDE
    up = 1 - 2 * core

    after = gated
    swapped = []
    for wide, narrow in (
        (grad_turned, gated), (shards_turned, back_query), (shards_turned, back_key),
        (shards_turned, back_value),
    ):
        keep, send, after = weight_partial(after, wide, ids, narrow, core_word, chips)
        swapped.append((keep, moved(send, "core", 1)))
    sums = [FirstAxis(pair, first, places, up) for pair, first in zip(swapped, "xyxy")]
    outward = outward_part(
        tuple(each.start for each in sums),
        (back_query, back_key, back_value),
        gated,
        (w_query, w_key, w_value, w_out),
        SIDE,
    )
    outward = lax.psum_scatter(outward, "tp", scatter_dimension=0, tiled=True)[0]
    mixed, grad_input = outward[:row_count], outward[row_count:]
    halves = [each.total() for each in sums]
    grad_out, grad_key = second_axis_sums(halves[0::2], "y", places)
    grad_query, grad_value = second_axis_sums(halves[1::2], "x", places)
    grad_out = grad_out.T
    return (mixed, grad_input, grad_query, grad_key, grad_value, grad_out, grad_filter, grad_init)


def solution(mesh):
    return jax.shard_map(
        per_device,
        mesh=mesh,
        in_specs=(
            P("seq", "tp"),
            P(None, "tp"),
            P(None, "tp"),
            P(None, "tp"),
            P("tp", None),
            P(None, "tp"),
            P(None, "tp"),
            P(None, "tp"),
            P("tp"),
            P(None, "tp"),
            P("seq", "tp"),
        ),
        out_specs=(
            P("seq", "tp"),
            P("seq", "tp"),
            P("seq", "tp"),
            P("seq", "tp"),
            P("seq", "tp"),
            P("tp", "seq"),
            P(None, "tp"),
            P(None, "tp"),
        ),
        check_vma=False,
    )
```

```python
import functools

import jax
import jax.numpy as jnp
from jax import lax
from jax.experimental import pallas as pl
from jax.experimental.pallas import tpu as pltpu
from jax.sharding import PartitionSpec as P

LANE = 128
F32 = jnp.float32
BF16 = jnp.bfloat16


def dot_nn(left, right):
    return lax.dot_general(left, right, (((1,), (0,)), ((), ())), preferred_element_type=F32)


def dot_nt(left, right):
    return lax.dot_general(left, right, (((1,), (1,)), ((), ())), preferred_element_type=F32)


def dot_tn(left, right):
    return lax.dot_general(left, right, (((0,), (0,)), ((), ())), preferred_element_type=F32)


def dot_tt(left, right):
    return lax.dot_general(left, right, (((0,), (1,)), ((), ())), preferred_element_type=F32)


def split_pair(value):
    high = value.astype(BF16)
    return high, (value - high.astype(F32)).astype(BF16)


SIDE = 4
MIB = 1024 * 1024


def call_cost(flops, bytes_accessed, transcendentals=0):
    return pl.CostEstimate(
        flops=flops, bytes_accessed=bytes_accessed, transcendentals=transcendentals
    )


def params(mebibytes):
    return pltpu.CompilerParams(vmem_limit_bytes=mebibytes * MIB)


def in_vmem(count):
    return [pl.BlockSpec(memory_space=pltpu.VMEM)] * count


def in_smem(count):
    return [pl.BlockSpec(memory_space=pltpu.SMEM)] * count


def in_hbm(count):
    return [pl.BlockSpec(memory_space=pltpu.HBM)] * count


def anywhere(count):
    return [pl.BlockSpec(memory_space=pl.ANY)] * count


TICK = jax.ShapeDtypeStruct((8, LANE), F32)


def padded(rows):
    return -(-rows // 8) * 8


def later(value, steps, source_at):
    at = source_at[:, : value.shape[1]]
    return jnp.where(at >= steps, pltpu.roll(value, steps, 0), 0.0)


def earlier(value, steps, source_at):
    sources = value.shape[0]
    at = source_at[:, : value.shape[1]]
    return jnp.where(at < sources - steps, pltpu.roll(value, sources - steps, 0), 0.0)


def circulant(row):
    return pltpu.roll(jnp.broadcast_to(row, (LANE, LANE)), 0, 1, stride=1, stride_axis=0)


def iotas(sources):
    lane_at = lax.broadcasted_iota(jnp.int32, (LANE, LANE), 1)
    row_at = lax.broadcasted_iota(jnp.int32, (LANE, LANE), 0)
    source_at = lax.broadcasted_iota(jnp.int32, (sources, LANE), 0)
    return lane_at, row_at, source_at


def decay_tables(cols_ref, channel, lane_at):
    rate = cols_ref[0, channel]
    read = cols_ref[1, channel]
    lanes = lane_at[: rate.shape[0]].astype(F32)
    step_decay = jnp.exp(-rate)
    inflow = 1.0 - step_decay
    rising = jnp.exp(-rate * lanes)
    falling = jnp.exp(-rate * (LANE - 1.0 - lanes))
    reading = (read * step_decay) * rising
    feeding = inflow * falling
    weight = read * inflow
    kernel_row = jnp.sum(weight * rising, axis=0, keepdims=True)
    wrapped = jnp.where(lanes > 0.0, step_decay * falling, 1.0)
    kernel_turned = jnp.sum(weight * wrapped, axis=0, keepdims=True)
    return reading.astype(BF16), feeding.astype(BF16), kernel_row, kernel_turned


def part_rows(value, sources):
    return [value[at : at + sources] for at in range(0, value.shape[0], sources)]


def load_rows(ref, row, sources, pad, parts):
    return [
        ref[pl.ds(row + part * sources * pad, sources, stride=pad), :] for part in range(parts)
    ]


def store_rows(ref, row, sources, pad, value):
    for part, piece in enumerate(part_rows(value, sources)):
        ref[pl.ds(row + part * sources * pad, sources, stride=pad), :] = piece


def spread(block_ref, rows_ref, pad):
    sources, count, width = block_ref.shape

    def step(source, carry):
        for part in range(width // LANE):
            row = pl.multiple_of((part * sources + source) * pad, 8)
            rows_ref[pl.ds(row, count), :] = block_ref[
                source, :, LANE * part : LANE * (part + 1)
            ].astype(F32)
        return carry

    lax.fori_loop(0, sources, step, 0)


def channel_body(
    channel, sources, parts, group, at, in_rows, out_rows, small_rows, rows_ref, cols_ref,
    taps_ref, skip_ref,
):
    lane_at, row_at, source_at = at
    in_pad, out_pad = padded(3 * group), padded(2 * group) + padded(group)
    key = load_rows(in_rows, channel, sources, in_pad, parts)
    value = jnp.concatenate(load_rows(in_rows, channel + group, sources, in_pad, parts), 0)
    grads = jnp.concatenate(load_rows(in_rows, channel + 2 * group, sources, in_pad, parts), 0)
    rate_row = rows_ref[0, pl.ds(channel, 1), :]
    start_row = rows_ref[1, pl.ds(channel, 1), :]
    states = rate_row.shape[1]
    reading, feeding, kernel_row, kernel_turned = decay_tables(cols_ref, channel, lane_at)
    ahead, behind = lane_at >= row_at, lane_at <= row_at
    local = jnp.where(ahead, circulant(kernel_row), 0.0).astype(BF16)
    local_turned = jnp.where(behind, circulant(kernel_turned), 0.0).astype(BF16)
    taps = circulant(taps_ref[0, pl.ds(channel, 1), :])
    taps_turned = circulant(taps_ref[1, pl.ds(channel, 1), :])
    taps_forward = jnp.concatenate(
        [jnp.where(ahead, 0.0, taps), jnp.where(ahead, taps, 0.0)], 0
    ).astype(BF16)
    taps_back = jnp.concatenate(
        [jnp.where(behind, taps_turned, 0.0), jnp.where(behind, 0.0, taps_turned)], 0
    ).astype(BF16)
    skip = skip_ref[channel]
    part_decay = jnp.exp(-rate_row * LANE)
    row_decay = jnp.exp(-rate_row * (LANE * parts))

    key_now = jnp.concatenate(key, 0)
    key_before = jnp.concatenate([later(key[-1], 1, source_at)] + key[:-1], 0)
    key_pair = jnp.concatenate([key_before, key_now], 1).astype(BF16)
    shifted = dot_nn(key_pair, taps_forward)
    drive = shifted * value
    drive_short = drive.astype(BF16)

    fed = part_rows(dot_nt(drive_short, feeding), sources)
    whole = fed[0]
    for part in range(1, parts):
        whole = part_decay * whole + fed[part]
    scan = jnp.where(source_at[:, :states] >= 1, pltpu.roll(whole, 1, 0), start_row)
    step, decay = 1, row_decay
    while step < sources:
        scan = scan + decay * later(scan, step, source_at)
        step, decay = 2 * step, decay * decay
    entering = [scan]
    for part in range(1, parts):
        entering.append(part_decay * entering[-1] + fed[part - 1])
    state_high, state_low = split_pair(jnp.concatenate(entering, 0))
    response = (
        dot_nn(
            jnp.concatenate([drive_short, state_high, state_low], 1),
            jnp.concatenate([local, reading, reading], 0),
        )
        + skip * drive
    )

    grad_short = grads.astype(BF16)
    read = part_rows(dot_nt(grad_short, reading), sources)
    whole = read[-1]
    for part in range(parts - 2, -1, -1):
        whole = part_decay * whole + read[part]
    scan = earlier(whole, 1, source_at)
    step, decay = 1, row_decay
    while step < sources:
        scan = scan + decay * earlier(scan, step, source_at)
        step, decay = 2 * step, decay * decay
    leaving = [scan]
    for part in range(parts - 1, 0, -1):
        leaving.insert(0, part_decay * leaving[0] + read[part])
    start_grad = (part_decay * leaving[0] + read[0])[0:1]
    carry_high, carry_low = split_pair(jnp.concatenate(leaving, 0))
    back_drive = (
        dot_nn(
            jnp.concatenate([grad_short, carry_high, carry_low], 1),
            jnp.concatenate([local_turned, feeding, feeding], 0),
        )
        + skip * grads
    )
    back_value = back_drive * shifted
    back_shifted = back_drive * value
    pieces = part_rows(back_shifted, sources)
    back_after = jnp.concatenate(pieces[1:] + [earlier(pieces[0], 1, source_at)], 0)
    back_short = back_shifted.astype(BF16)
    back_pair = jnp.concatenate([back_short, back_after.astype(BF16)], 1)
    back_key = dot_nn(back_pair, taps_back)

    gram = dot_tn(key_pair, back_short)
    gram = jnp.where(ahead, gram[LANE:], gram[:LANE])
    aligned = gram[:8]
    for first in range(8, LANE, 8):
        aligned = aligned + pltpu.roll(gram[first : first + 8], LANE - first, 1)
    for bit in (1, 2, 4):
        aligned = jnp.where((row_at[:8] & bit) > 0, pltpu.roll(aligned, LANE - bit, 1), aligned)
    filter_grad = jnp.sum(aligned, axis=0, keepdims=True)[:, : LANE - states]
    small_rows[pl.ds(channel, 1), :] = jnp.concatenate([filter_grad, start_grad], 1)
    for index, result in enumerate((response, back_value, back_key)):
        store_rows(out_rows, channel + index * group, sources, out_pad, result)


UNROLL = 4


def sequence_kernel(
    group, after_ref, in_ref, rows_ref, cols_ref, taps_ref, skip_ref, out_ref, in_rows, out_rows,
    small_rows,
):
    sources, _, width = in_ref.shape
    parts = width // LANE
    spread(in_ref, in_rows, padded(3 * group))
    small_rows[...] = jnp.zeros_like(small_rows)
    at = iotas(sources)

    def step(index, carry):
        for inner in range(UNROLL):
            channel_body(
                index * UNROLL + inner, sources, parts, group, at, in_rows, out_rows, small_rows,
                rows_ref, cols_ref, taps_ref, skip_ref,
            )
        return carry

    lax.fori_loop(0, group // UNROLL, step, 0)
    out_pad = padded(2 * group) + padded(group)
    extra = out_ref.shape[1] - 3 * group

    def pack(source, carry):
        for part in range(parts):
            row = pl.multiple_of((part * sources + source) * out_pad, 8)
            columns = slice(LANE * part, LANE * (part + 1))
            out_ref[source, : 3 * group, columns] = out_rows[pl.ds(row, 3 * group), :].astype(
                BF16
            )
            out_ref[source, 3 * group :, columns] = small_rows[
                extra * part : extra * (part + 1)
            ].astype(BF16)
        return carry

    lax.fori_loop(0, sources, pack, 0)


def sequence_part(after, value, rows, cols, taps, skip):
    sources, triple, width = value.shape
    group = triple // 3
    parts = width // LANE
    lines = sources * parts
    extra = -(-group // parts)
    return pl.pallas_call(
        functools.partial(sequence_kernel, group),
        out_shape=jax.ShapeDtypeStruct((sources, triple + extra, width), BF16),
        in_specs=anywhere(1) + in_vmem(4) + in_smem(1),
        out_specs=in_vmem(1)[0],
        scratch_shapes=[
            pltpu.VMEM((lines * padded(triple), LANE), F32),
            pltpu.VMEM((lines * (padded(2 * group) + padded(group)), LANE), F32),
            pltpu.VMEM((padded(extra * parts), LANE), F32),
        ],
        compiler_params=params(24),
        cost_estimate=call_cost(22_000_000_000, 5_000_000),
    )(after, value, rows, cols, taps, skip)


def tiles_of(count, body):
    def step(tile, carry):
        body(tile)
        return carry

    lax.fori_loop(0, count, step, 0)


def columns_of(tile, width):
    return pl.ds(pl.multiple_of(tile * width, LANE), width)


def rows_of(tile, height):
    return pl.ds(pl.multiple_of(tile * height, 16), height)


def weight_rows(weight_ref, ids_ref, tile, depth):
    return weight_ref[rows_of(ids_ref[tile], depth), :]


def near_kernel(shard_count, *refs):
    shards, rest = refs[:shard_count], refs[shard_count:]
    half = (len(rest) - 1) // 2
    weights, ids_ref, sums = rest[:half], rest[half], rest[half + 1 :]
    depth = shards[0].shape[1]
    for weight_ref, sum_ref in zip(weights, sums):
        total = dot_nn(shards[0][...], weight_rows(weight_ref, ids_ref, 0, depth))
        for tile in range(1, shard_count):
            total += dot_nn(shards[tile][...], weight_rows(weight_ref, ids_ref, tile, depth))
        sum_ref[...] = total


def near_part(shards, weights, ids):
    rows, depth = shards[0].shape
    channels = weights[0].shape[1]
    return pl.pallas_call(
        functools.partial(near_kernel, len(shards)),
        in_specs=in_vmem(len(shards) + len(weights)) + in_smem(1),
        out_specs=tuple(in_vmem(len(weights))),
        out_shape=(jax.ShapeDtypeStruct((rows, channels), F32),) * len(weights),
        compiler_params=params(24),
        cost_estimate=call_cost(
            2 * len(shards) * len(weights) * rows * depth * channels, 12_000_000
        ),
    )(*shards, *weights, ids)


def far_kernel(
    group, shard_ref, key_ref, value_ref, query_ref, key_sum, value_sum, query_sum, ids_ref,
    kv_ref, query_out, across, packed,
):
    depth = shard_ref.shape[1]
    tile = ids_ref.shape[0] - 1
    pad = padded(2 * group)
    owners = kv_ref.shape[0]
    for index, (weight_ref, sum_ref) in enumerate(((key_ref, key_sum), (value_ref, value_sum))):
        part = dot_nn(shard_ref[...], weight_rows(weight_ref, ids_ref, tile, depth))
        across[...] = (sum_ref[...] + part).T
        for owner in range(owners):
            first = owner * pad + index * group
            packed[first : first + group] = across[owner * group : (owner + 1) * group]
    for owner in range(owners):
        kv_ref[owner] = packed[owner * pad : owner * pad + 2 * group].astype(BF16)
    part = dot_nn(shard_ref[...], weight_rows(query_ref, ids_ref, tile, depth))
    query_out[...] = (query_sum[...] + part).astype(BF16)


def far_part(shard, weights, sums, ids, owners):
    rows, depth = shard.shape
    channels = weights[0].shape[1]
    group = channels // owners
    return pl.pallas_call(
        functools.partial(far_kernel, group),
        in_specs=in_vmem(7) + in_smem(1),
        out_specs=tuple(in_vmem(2)),
        out_shape=(
            jax.ShapeDtypeStruct((owners, 2 * group, rows), BF16),
            jax.ShapeDtypeStruct((rows, channels), BF16),
        ),
        scratch_shapes=[
            pltpu.VMEM((channels, rows), F32),
            pltpu.VMEM((owners * padded(2 * group), rows), F32),
        ],
        compiler_params=params(24),
        cost_estimate=call_cost(6 * rows * depth * channels, 12_000_000),
    )(shard, *weights, *sums, ids)


def grad_near_kernel(after_ref, first_ref, second_ref, third_ref, weight_ref, ids_ref, sum_ref):
    depth = first_ref.shape[1]

    def part(tile, shard_ref):
        first = pl.multiple_of(ids_ref[tile] * depth, LANE)
        return dot_nt(shard_ref[...], weight_ref[:, pl.ds(first, depth)])

    sum_ref[...] = part(0, first_ref) + part(1, second_ref) + part(2, third_ref)


def grad_near_part(after, shards, w_out, ids):
    rows, depth = shards[0].shape
    channels = w_out.shape[0]
    return pl.pallas_call(
        grad_near_kernel,
        in_specs=anywhere(1) + in_vmem(4) + in_smem(1),
        out_specs=in_vmem(1)[0],
        out_shape=jax.ShapeDtypeStruct((rows, channels), F32),
        compiler_params=params(16),
        cost_estimate=call_cost(6 * rows * depth * channels, 6_000_000),
    )(after, *shards, w_out, ids)


def grad_far_kernel(
    group, kv_ref, shard_ref, weight_ref, sum_ref, query_ref, ids_ref, gated_ref, grouped_ref,
    across,
):
    depth = shard_ref.shape[1]
    first = pl.multiple_of(ids_ref[ids_ref.shape[0] - 1] * depth, LANE)
    total = sum_ref[...] + dot_nt(shard_ref[...], weight_ref[:, pl.ds(first, depth)])
    gated = total.astype(BF16)
    gated_ref[...] = gated
    across[...] = (gated.astype(F32) * query_ref[...].astype(F32)).T
    for owner in range(grouped_ref.shape[0]):
        grouped_ref[owner, : 2 * group] = kv_ref[owner]
        grouped_ref[owner, 2 * group :] = across[owner * group : (owner + 1) * group].astype(BF16)


def grad_far_part(kv, shard, w_out, total, query, ids):
    rows, depth = shard.shape
    channels = w_out.shape[0]
    owners = kv.shape[0]
    group = channels // owners
    return pl.pallas_call(
        functools.partial(grad_far_kernel, group),
        in_specs=in_vmem(5) + in_smem(1),
        out_specs=tuple(in_vmem(2)),
        out_shape=(
            jax.ShapeDtypeStruct((rows, channels), BF16),
            jax.ShapeDtypeStruct((owners, 3 * group, rows), BF16),
        ),
        scratch_shapes=[pltpu.VMEM((channels, rows), F32)],
        compiler_params=params(16),
        cost_estimate=call_cost(2 * rows * depth * channels, 6_000_000),
    )(kv, shard, w_out, total, query, ids)


def unpack_kernel(
    group, returned_ref, query_ref, gated_ref, forward_ref, query_grad_ref, key_ref, value_ref,
    filter_ref, init_ref, response_rows, value_rows, key_rows, small_rows,
):
    owners, lines, width = returned_ref.shape
    extra = lines - 3 * group
    for owner in range(owners):
        piece = returned_ref[owner].astype(F32)
        at = slice(owner * group, (owner + 1) * group)
        response_rows[at] = piece[:group]
        value_rows[at] = piece[group : 2 * group]
        key_rows[at] = piece[2 * group : 3 * group]
        for part in range(width // LANE):
            count = min(extra, group - extra * part)
            first = owner * group + extra * part
            small_rows[first : first + count] = piece[
                3 * group : 3 * group + count, LANE * part : LANE * (part + 1)
            ]
    response = response_rows[...].T
    forward_ref[...] = (query_ref[...].astype(F32) * response).astype(BF16)
    query_grad_ref[...] = (gated_ref[...].astype(F32) * response).astype(BF16)
    value_ref[...] = value_rows[...].T.astype(BF16)
    key_ref[...] = key_rows[...].T.astype(BF16)
    small = small_rows[...].T
    taps = filter_ref.shape[0]
    filter_ref[...] = small[:taps]
    init_ref[...] = small[taps:]


def unpack_part(returned, query, gated, taps):
    rows, channels = query.shape
    short = jax.ShapeDtypeStruct((rows, channels), BF16)
    return pl.pallas_call(
        functools.partial(unpack_kernel, channels // returned.shape[0]),
        in_specs=in_vmem(3),
        out_specs=tuple(in_vmem(6)),
        out_shape=(
            short, short, short, short,
            jax.ShapeDtypeStruct((taps, channels), F32),
            jax.ShapeDtypeStruct((LANE - taps, channels), F32),
        ),
        scratch_shapes=[pltpu.VMEM((channels, rows), F32)] * 3
        + [pltpu.VMEM((channels, LANE), F32)],
        compiler_params=params(14),
        cost_estimate=call_cost(4 * rows * channels, 5_000_000),
    )(returned, query, gated)


def turn_kernel(after_ref, *refs):
    count = (len(refs) - 6) // 2
    shards, (first_out, second_out, tick_ref, first, second, sems) = refs[:-6], refs[-6:]
    tick_ref[...] = jnp.zeros_like(tick_ref)
    held = ((first, first_out), (second, second_out))
    sent = []
    for index, ref in enumerate(shards):
        which, tile = index // count, index % count
        source, target = held[which]
        source[tile] = ref[...].T
        sent.append(
            pltpu.make_async_copy(source.at[tile], target.at[tile], sems.at[which, tile])
        )
        sent[-1].start()
    for copy in sent:
        copy.wait()


def turn_part(after, first, second):
    rows, depth = first[0].shape
    count = len(first)
    out = jax.ShapeDtypeStruct((count, depth, rows), BF16)
    return pl.pallas_call(
        turn_kernel,
        in_specs=anywhere(1) + in_vmem(2 * count),
        out_specs=tuple(in_hbm(2) + in_vmem(1)),
        out_shape=(out, out, TICK),
        scratch_shapes=[pltpu.VMEM(out.shape, BF16)] * 2 + [pltpu.SemaphoreType.DMA((2, count))],
        compiler_params=params(16),
        cost_estimate=call_cost(2 * count * depth * rows, 8_000_000),
    )(after, *first, *second)


def hold_kernel(after_ref, *refs):
    count = (len(refs) - 1) // 2
    sources, targets, sems = refs[:count], refs[count:-1], refs[-1]
    copies = [
        pltpu.make_async_copy(source, target, sems.at[index])
        for index, (source, target) in enumerate(zip(sources, targets))
    ]
    for copy in copies:
        copy.start()
    for copy in copies:
        copy.wait()


def held_in_vmem(after, values):
    count = len(values)
    return pl.pallas_call(
        hold_kernel,
        in_specs=anywhere(1) + in_hbm(count),
        out_specs=tuple(in_vmem(count)),
        out_shape=tuple(jax.ShapeDtypeStruct(value.shape, value.dtype) for value in values),
        scratch_shapes=[pltpu.SemaphoreType.DMA((count,))],
        compiler_params=params(16),
        cost_estimate=call_cost(0, 26_000_000),
    )(after, *values)


def weight_kernel(
    rows, after_ref, wide_ref, narrow_ref, ids_ref, core_ref, keep_ref, send_ref, tick_ref
):
    tick_ref[...] = jnp.zeros_like(tick_ref)
    tiles = wide_ref.shape[0]
    held = keep_ref.shape[0] // tiles

    def multiply(tile):
        result = dot_nn(wide_ref[tile], narrow_ref[...]).astype(BF16)
        first = ids_ref[tile] * held
        for core in range(2):

            @pl.when(core_ref[0] == core)
            def _():
                for chip in range(held):
                    at = (2 * chip + core) * rows
                    other = (2 * chip + 1 - core) * rows
                    keep_ref[first + chip] = result[at : at + rows]
                    send_ref[first + chip] = result[other : other + rows]

    tiles_of(tiles, multiply)


def weight_partial(after, wide, ids, narrow, core, chips):
    tiles, height, depth = wide.shape
    width = narrow.shape[1]
    total = tiles * height
    rows = total // (2 * chips)
    return pl.pallas_call(
        functools.partial(weight_kernel, rows),
        in_specs=anywhere(1) + in_vmem(2) + in_smem(2),
        out_specs=tuple(in_vmem(3)),
        out_shape=(jax.ShapeDtypeStruct((chips, rows, width), BF16),) * 2 + (TICK,),
        compiler_params=params(14),
        cost_estimate=call_cost(2 * total * depth * width, 6_000_000),
    )(after, wide, narrow, ids, core)


def outward_kernel(unread, *refs):
    (
        query_ref, key_ref, value_ref, gated_ref, query_weight, key_weight, value_weight,
        out_weight, out_ref, result, sems,
    ) = refs[unread:]
    count, height, width = out_ref.shape
    rows = height // 2

    def copy_out(tile):
        return pltpu.make_async_copy(result.at[tile], out_ref.at[tile], sems.at[tile])

    def multiply(tile):
        result[tile, :rows] = dot_nn(
            gated_ref[...], out_weight[:, columns_of(tile, width)]
        ).astype(BF16)
        at = rows_of(tile, width)
        total = dot_nt(query_ref[...], query_weight[at, :])
        total += dot_nt(key_ref[...], key_weight[at, :])
        total += dot_nt(value_ref[...], value_weight[at, :])
        result[tile, rows:] = total.astype(BF16)
        copy_out(tile).start()

    tiles_of(count, multiply)
    tiles_of(count, lambda tile: copy_out(tile).wait())


def outward_part(after, backs, gated, weights, count):
    rows, depth = gated.shape
    width = weights[0].shape[0] // count
    shape = (count, 2 * rows, width)
    return pl.pallas_call(
        functools.partial(outward_kernel, len(after)),
        in_specs=anywhere(len(after)) + in_vmem(8),
        out_specs=in_hbm(1)[0],
        out_shape=jax.ShapeDtypeStruct(shape, BF16),
        scratch_shapes=[pltpu.VMEM(shape, BF16), pltpu.SemaphoreType.DMA((count,))],
        compiler_params=params(24),
        cost_estimate=call_cost(8 * rows * depth * width * count, 20_000_000),
    )(*after, *backs, gated, *weights)


def moved(value, axis, steps):
    by_core = steps if isinstance(steps, tuple) else (steps, steps)
    pairs = []
    for x in range(SIDE):
        for y in range(SIDE):
            for core in range(2):
                for z in range(SIDE):
                    goal = [x, y, core, z]
                    if axis == "core":
                        goal[2] = 1 - core
                    else:
                        at = {"x": 0, "y": 1, "z": 3}[axis]
                        goal[at] = (goal[at] + by_core[core]) % SIDE
                    pairs.append(
                        tuple(
                            ((a * SIDE + b) * 2 + c) * SIDE + d
                            for a, b, c, d in ((x, y, core, z), goal)
                        )
                    )
    return lax.ppermute(value, ("seq", "tp"), pairs)


def added(left, right):
    return (left.astype(F32) + right.astype(F32)).astype(BF16)


def picked(value, axis=0):
    return lambda index: lax.dynamic_index_in_dim(value, index, axis, keepdims=False)


def ring_sum(travelling, block, place, up, axis, steps):
    for step in steps:
        travelling = added(moved(travelling, axis, (1, -1)), block((place - step * up) % SIDE))
    return travelling


class FirstAxis:
    def __init__(self, halves, first, places, up):
        keep, came = halves
        _, rows, width = keep.shape
        grid = (SIDE, SIDE, rows, width)
        axis = "xy".index(first)
        self.keep, self.came = picked(keep.reshape(grid), axis), picked(came.reshape(grid), axis)
        self.first, self.place, self.up = first, places[first], up
        self.start = self.block((self.place - up) % SIDE)

    def block(self, index):
        return added(self.keep(index), self.came(index))

    def total(self):
        return ring_sum(
            self.start, self.block, self.place, self.up, self.first, range(2, SIDE + 1)
        )


def second_axis_sums(halves, second, places, ahead=()):
    place = places[second]

    def mine(step):
        return jnp.stack([picked(half)((place + step) % SIDE) for half in halves])

    total, *ahead = lax.optimization_barrier((mine(0).astype(F32), *ahead))
    for step in (1, -1, 2):
        steps = (2, -2) if step == 2 else step
        total += moved(mine(step), second, steps).astype(F32)
    return [total[index] for index in range(len(halves))] + ahead


def per_device(
    tokens,
    w_query,
    w_key,
    w_value,
    w_out,
    shift_filter,
    log_decay,
    readout,
    skip_gain,
    init_state,
    cotangent,
):
    row_count = tokens.shape[0]
    channels = w_query.shape[1]
    tap_count = shift_filter.shape[0]
    seq_count = lax.axis_size("seq")
    group = channels // seq_count
    position = lax.axis_index("seq")
    core = position % 2
    chip_z = lax.axis_index("tp")
    places = {"x": position // (2 * SIDE), "y": (position // 2) % SIDE}
    core_word = core.reshape(1)

    token_sides = moved(tokens, "z", 1), moved(tokens, "z", -1)
    grad_sides = moved(cotangent, "z", 1), moved(cotangent, "z", -1)

    def passed(sides):
        below, above = sides
        return jnp.where(core == 0, below, above)

    held = held_in_vmem(skip_gain, (w_key, w_value, w_query, w_out))
    tokens_on, _ = lax.optimization_barrier((passed(token_sides), held[0]))
    grad_sides, tokens_on = lax.optimization_barrier((grad_sides, tokens_on))
    grads_on = passed(grad_sides)
    shards = (tokens, *token_sides, moved(tokens_on, "z", (1, -1)))
    grad_shards = (cotangent, *grad_sides, moved(grads_on, "z", (1, -1)))
    ids = (chip_z + jnp.array([0, SIDE - 1, 1, 2], jnp.int32)) % SIDE

    def own(value):
        return lax.dynamic_slice_in_dim(value, position * group, group, value.ndim - 1)

    own_rate, own_read, own_init, own_taps = (
        own(value).T for value in (log_decay, readout, init_state, shift_filter)
    )
    own_taps = jnp.pad(own_taps, ((0, 0), (0, LANE - tap_count)))
    taps = jnp.stack([own_taps, jnp.roll(own_taps[:, ::-1], 1, axis=1)])
    rows = jnp.stack([own_rate, own_init])
    cols = jnp.stack([own_rate, own_read])[..., None]
    skip = own(skip_gain)

    def exchanged(value):
        return lax.all_to_all(value, "seq", 0, 0, tiled=True)

    weights = held[:3]
    sums = near_part(shards[:3], weights, ids)
    grad_sum = grad_near_part(sums[2], grad_shards[:3], held[3], ids)
    kv, query = far_part(shards[3], weights, sums, ids, seq_count)
    gated_grad, packed = grad_far_part(kv, grad_shards[3], held[3], grad_sum, query, ids)
    shards_turned, grad_turned, turned = turn_part(packed, shards, grad_shards)
    results = sequence_part(turned, exchanged(packed), rows, cols, taps, skip)
    returned = exchanged(results)
    gated, back_query, back_key, back_value, grad_filter, grad_init = unpack_part(
        returned, query, gated_grad, tap_count
    )
    chips = SIDE * SIDE
    up = 1 - 2 * core

    after = gated
    swapped = []
    for wide, narrow in (
        (grad_turned, gated), (shards_turned, back_query), (shards_turned, back_key),
        (shards_turned, back_value),
    ):
        keep, send, after = weight_partial(after, wide, ids, narrow, core_word, chips)
        swapped.append((keep, moved(send, "core", 1)))
    sums = [FirstAxis(pair, first, places, up) for pair, first in zip(swapped, "xyxy")]
    outward = outward_part(
        (after,),
        (back_query, back_key, back_value),
        gated,
        (w_query, w_key, w_value, w_out),
        SIDE,
    )
    outward = lax.psum_scatter(outward, "tp", scatter_dimension=0, tiled=True)[0]
    mixed, grad_input = outward[:row_count], outward[row_count:]
    halves = [each.total() for each in sums]
    grad_out, grad_key = second_axis_sums(halves[0::2], "y", places)
    grad_query, grad_value, mixed, grad_input = second_axis_sums(
        halves[1::2], "x", places, (mixed, grad_input)
    )
    grad_out = grad_out.T
    return (mixed, grad_input, grad_query, grad_key, grad_value, grad_out, grad_filter, grad_init)


def solution(mesh):
    return jax.shard_map(
        per_device,
        mesh=mesh,
        in_specs=(
            P("seq", "tp"),
            P(None, "tp"),
            P(None, "tp"),
            P(None, "tp"),
            P("tp", None),
            P(None, "tp"),
            P(None, "tp"),
            P(None, "tp"),
            P("tp"),
            P(None, "tp"),
            P("seq", "tp"),
        ),
        out_specs=(
            P("seq", "tp"),
            P("seq", "tp"),
            P("seq", "tp"),
            P("seq", "tp"),
            P("seq", "tp"),
            P("tp", "seq"),
            P(None, "tp"),
            P(None, "tp"),
        ),
        check_vma=False,
    )
```

```python
import functools

import jax
import jax.numpy as jnp
from jax import lax
from jax.experimental import pallas as pl
from jax.experimental.pallas import tpu as pltpu
from jax.sharding import PartitionSpec as P

LANE = 128
F32 = jnp.float32
BF16 = jnp.bfloat16


def dot_nn(left, right):
    return lax.dot_general(left, right, (((1,), (0,)), ((), ())), preferred_element_type=F32)


def dot_nt(left, right):
    return lax.dot_general(left, right, (((1,), (1,)), ((), ())), preferred_element_type=F32)


def dot_tn(left, right):
    return lax.dot_general(left, right, (((0,), (0,)), ((), ())), preferred_element_type=F32)


def dot_tt(left, right):
    return lax.dot_general(left, right, (((0,), (1,)), ((), ())), preferred_element_type=F32)


def split_pair(value):
    high = value.astype(BF16)
    return high, (value - high.astype(F32)).astype(BF16)


SIDE = 4
MIB = 1024 * 1024


def call_cost(flops, bytes_accessed, transcendentals=0):
    return pl.CostEstimate(
        flops=flops, bytes_accessed=bytes_accessed, transcendentals=transcendentals
    )


def params(mebibytes):
    return pltpu.CompilerParams(vmem_limit_bytes=mebibytes * MIB)


def in_vmem(count):
    return [pl.BlockSpec(memory_space=pltpu.VMEM)] * count


def in_smem(count):
    return [pl.BlockSpec(memory_space=pltpu.SMEM)] * count


def in_hbm(count):
    return [pl.BlockSpec(memory_space=pltpu.HBM)] * count


def anywhere(count):
    return [pl.BlockSpec(memory_space=pl.ANY)] * count


TICK = jax.ShapeDtypeStruct((8, LANE), F32)


def padded(rows):
    return -(-rows // 8) * 8


def later(value, steps, source_at):
    at = source_at[:, : value.shape[1]]
    return jnp.where(at >= steps, pltpu.roll(value, steps, 0), 0.0)


def earlier(value, steps, source_at):
    sources = value.shape[0]
    at = source_at[:, : value.shape[1]]
    return jnp.where(at < sources - steps, pltpu.roll(value, sources - steps, 0), 0.0)


def circulant(row):
    return pltpu.roll(jnp.broadcast_to(row, (LANE, LANE)), 0, 1, stride=1, stride_axis=0)


def iotas(sources):
    lane_at = lax.broadcasted_iota(jnp.int32, (LANE, LANE), 1)
    row_at = lax.broadcasted_iota(jnp.int32, (LANE, LANE), 0)
    source_at = lax.broadcasted_iota(jnp.int32, (sources, LANE), 0)
    return lane_at, row_at, source_at


def decay_tables(cols_ref, channel, lane_at):
    rate = cols_ref[0, channel]
    read = cols_ref[1, channel]
    lanes = lane_at[: rate.shape[0]].astype(F32)
    step_decay = jnp.exp(-rate)
    inflow = 1.0 - step_decay
    rising = jnp.exp(-rate * lanes)
    falling = jnp.exp(-rate * (LANE - 1.0 - lanes))
    reading = (read * step_decay) * rising
    feeding = inflow * falling
    weight = read * inflow
    kernel_row = jnp.sum(weight * rising, axis=0, keepdims=True)
    wrapped = jnp.where(lanes > 0.0, step_decay * falling, 1.0)
    kernel_turned = jnp.sum(weight * wrapped, axis=0, keepdims=True)
    return reading.astype(BF16), feeding.astype(BF16), kernel_row, kernel_turned


def part_rows(value, sources):
    return [value[at : at + sources] for at in range(0, value.shape[0], sources)]


def load_rows(ref, row, sources, pad, parts):
    return [
        ref[pl.ds(row + part * sources * pad, sources, stride=pad), :] for part in range(parts)
    ]


def store_rows(ref, row, sources, pad, value):
    for part, piece in enumerate(part_rows(value, sources)):
        ref[pl.ds(row + part * sources * pad, sources, stride=pad), :] = piece


def spread(block_ref, rows_ref, pad):
    sources, count, width = block_ref.shape

    def step(source, carry):
        for part in range(width // LANE):
            row = pl.multiple_of((part * sources + source) * pad, 8)
            rows_ref[pl.ds(row, count), :] = block_ref[
                source, :, LANE * part : LANE * (part + 1)
            ].astype(F32)
        return carry

    lax.fori_loop(0, sources, step, 0)


def channel_body(
    channel, sources, parts, group, at, in_rows, out_rows, small_rows, rows_ref, cols_ref,
    taps_ref, skip_ref,
):
    lane_at, row_at, source_at = at
    in_pad, out_pad = padded(3 * group), padded(2 * group) + padded(group)
    key = load_rows(in_rows, channel, sources, in_pad, parts)
    value = jnp.concatenate(load_rows(in_rows, channel + group, sources, in_pad, parts), 0)
    grads = jnp.concatenate(load_rows(in_rows, channel + 2 * group, sources, in_pad, parts), 0)
    rate_row = rows_ref[0, pl.ds(channel, 1), :]
    start_row = rows_ref[1, pl.ds(channel, 1), :]
    states = rate_row.shape[1]
    reading, feeding, kernel_row, kernel_turned = decay_tables(cols_ref, channel, lane_at)
    ahead, behind = lane_at >= row_at, lane_at <= row_at
    local = jnp.where(ahead, circulant(kernel_row), 0.0).astype(BF16)
    local_turned = jnp.where(behind, circulant(kernel_turned), 0.0).astype(BF16)
    taps = circulant(taps_ref[0, pl.ds(channel, 1), :])
    taps_turned = circulant(taps_ref[1, pl.ds(channel, 1), :])
    taps_forward = jnp.concatenate(
        [jnp.where(ahead, 0.0, taps), jnp.where(ahead, taps, 0.0)], 0
    ).astype(BF16)
    taps_back = jnp.concatenate(
        [jnp.where(behind, taps_turned, 0.0), jnp.where(behind, 0.0, taps_turned)], 0
    ).astype(BF16)
    skip = skip_ref[channel]
    part_decay = jnp.exp(-rate_row * LANE)
    row_decay = jnp.exp(-rate_row * (LANE * parts))

    key_now = jnp.concatenate(key, 0)
    key_before = jnp.concatenate([later(key[-1], 1, source_at)] + key[:-1], 0)
    key_pair = jnp.concatenate([key_before, key_now], 1).astype(BF16)
    shifted = dot_nn(key_pair, taps_forward)
    drive = shifted * value
    drive_short = drive.astype(BF16)

    fed = part_rows(dot_nt(drive_short, feeding), sources)
    whole = fed[0]
    for part in range(1, parts):
        whole = part_decay * whole + fed[part]
    scan = jnp.where(source_at[:, :states] >= 1, pltpu.roll(whole, 1, 0), start_row)
    step, decay = 1, row_decay
    while step < sources:
        scan = scan + decay * later(scan, step, source_at)
        step, decay = 2 * step, decay * decay
    entering = [scan]
    for part in range(1, parts):
        entering.append(part_decay * entering[-1] + fed[part - 1])
    state_high, state_low = split_pair(jnp.concatenate(entering, 0))
    response = (
        dot_nn(
            jnp.concatenate([drive_short, state_high, state_low], 1),
            jnp.concatenate([local, reading, reading], 0),
        )
        + skip * drive
    )

    grad_short = grads.astype(BF16)
    read = part_rows(dot_nt(grad_short, reading), sources)
    whole = read[-1]
    for part in range(parts - 2, -1, -1):
        whole = part_decay * whole + read[part]
    scan = earlier(whole, 1, source_at)
    step, decay = 1, row_decay
    while step < sources:
        scan = scan + decay * earlier(scan, step, source_at)
        step, decay = 2 * step, decay * decay
    leaving = [scan]
    for part in range(parts - 1, 0, -1):
        leaving.insert(0, part_decay * leaving[0] + read[part])
    start_grad = (part_decay * leaving[0] + read[0])[0:1]
    carry_high, carry_low = split_pair(jnp.concatenate(leaving, 0))
    back_drive = (
        dot_nn(
            jnp.concatenate([grad_short, carry_high, carry_low], 1),
            jnp.concatenate([local_turned, feeding, feeding], 0),
        )
        + skip * grads
    )
    back_value = back_drive * shifted
    back_shifted = back_drive * value
    pieces = part_rows(back_shifted, sources)
    back_after = jnp.concatenate(pieces[1:] + [earlier(pieces[0], 1, source_at)], 0)
    back_short = back_shifted.astype(BF16)
    back_pair = jnp.concatenate([back_short, back_after.astype(BF16)], 1)
    back_key = dot_nn(back_pair, taps_back)

    gram = dot_tn(key_pair, back_short)
    gram = jnp.where(ahead, gram[LANE:], gram[:LANE])
    aligned = gram[:8]
    for first in range(8, LANE, 8):
        aligned = aligned + pltpu.roll(gram[first : first + 8], LANE - first, 1)
    for bit in (1, 2, 4):
        aligned = jnp.where((row_at[:8] & bit) > 0, pltpu.roll(aligned, LANE - bit, 1), aligned)
    filter_grad = jnp.sum(aligned, axis=0, keepdims=True)[:, : LANE - states]
    small_rows[pl.ds(channel, 1), :] = jnp.concatenate([filter_grad, start_grad], 1)
    for index, result in enumerate((response, back_value, back_key)):
        store_rows(out_rows, channel + index * group, sources, out_pad, result)


UNROLL = 4


def sequence_kernel(
    group, after_ref, in_ref, rows_ref, cols_ref, taps_ref, skip_ref, out_ref, in_rows, out_rows,
    small_rows,
):
    sources, _, width = in_ref.shape
    parts = width // LANE
    spread(in_ref, in_rows, padded(3 * group))
    small_rows[...] = jnp.zeros_like(small_rows)
    at = iotas(sources)

    def step(index, carry):
        for inner in range(UNROLL):
            channel_body(
                index * UNROLL + inner, sources, parts, group, at, in_rows, out_rows, small_rows,
                rows_ref, cols_ref, taps_ref, skip_ref,
            )
        return carry

    lax.fori_loop(0, group // UNROLL, step, 0)
    out_pad = padded(2 * group) + padded(group)
    extra = out_ref.shape[1] - 3 * group

    def pack(source, carry):
        for part in range(parts):
            row = pl.multiple_of((part * sources + source) * out_pad, 8)
            columns = slice(LANE * part, LANE * (part + 1))
            out_ref[source, : 3 * group, columns] = out_rows[pl.ds(row, 3 * group), :].astype(
                BF16
            )
            out_ref[source, 3 * group :, columns] = small_rows[
                extra * part : extra * (part + 1)
            ].astype(BF16)
        return carry

    lax.fori_loop(0, sources, pack, 0)


def sequence_part(after, value, rows, cols, taps, skip):
    sources, triple, width = value.shape
    group = triple // 3
    parts = width // LANE
    lines = sources * parts
    extra = -(-group // parts)
    return pl.pallas_call(
        functools.partial(sequence_kernel, group),
        out_shape=jax.ShapeDtypeStruct((sources, triple + extra, width), BF16),
        in_specs=anywhere(1) + in_vmem(4) + in_smem(1),
        out_specs=in_vmem(1)[0],
        scratch_shapes=[
            pltpu.VMEM((lines * padded(triple), LANE), F32),
            pltpu.VMEM((lines * (padded(2 * group) + padded(group)), LANE), F32),
            pltpu.VMEM((padded(extra * parts), LANE), F32),
        ],
        compiler_params=params(24),
        cost_estimate=call_cost(22_000_000_000, 5_000_000),
    )(after, value, rows, cols, taps, skip)


def tiles_of(count, body):
    def step(tile, carry):
        body(tile)
        return carry

    lax.fori_loop(0, count, step, 0)


def columns_of(tile, width):
    return pl.ds(pl.multiple_of(tile * width, LANE), width)


def rows_of(tile, height):
    return pl.ds(pl.multiple_of(tile * height, 16), height)


def weight_rows(weight_ref, ids_ref, tile, depth):
    return weight_ref[rows_of(ids_ref[tile], depth), :]


def near_kernel(shard_count, *refs):
    shards, rest = refs[:shard_count], refs[shard_count:]
    half = (len(rest) - 1) // 2
    weights, ids_ref, sums = rest[:half], rest[half], rest[half + 1 :]
    depth = shards[0].shape[1]
    for weight_ref, sum_ref in zip(weights, sums):
        total = dot_nn(shards[0][...], weight_rows(weight_ref, ids_ref, 0, depth))
        for tile in range(1, shard_count):
            total += dot_nn(shards[tile][...], weight_rows(weight_ref, ids_ref, tile, depth))
        sum_ref[...] = total


def near_part(shards, weights, ids):
    rows, depth = shards[0].shape
    channels = weights[0].shape[1]
    return pl.pallas_call(
        functools.partial(near_kernel, len(shards)),
        in_specs=in_vmem(len(shards) + len(weights)) + in_smem(1),
        out_specs=tuple(in_vmem(len(weights))),
        out_shape=(jax.ShapeDtypeStruct((rows, channels), F32),) * len(weights),
        compiler_params=params(24),
        cost_estimate=call_cost(
            2 * len(shards) * len(weights) * rows * depth * channels, 12_000_000
        ),
    )(*shards, *weights, ids)


def far_kernel(
    group, shard_ref, key_ref, value_ref, query_ref, key_sum, value_sum, query_sum, ids_ref,
    kv_ref, query_out, across, packed,
):
    depth = shard_ref.shape[1]
    tile = ids_ref.shape[0] - 1
    pad = padded(2 * group)
    owners = kv_ref.shape[0]
    for index, (weight_ref, sum_ref) in enumerate(((key_ref, key_sum), (value_ref, value_sum))):
        part = dot_nn(shard_ref[...], weight_rows(weight_ref, ids_ref, tile, depth))
        across[...] = (sum_ref[...] + part).T
        for owner in range(owners):
            first = owner * pad + index * group
            packed[first : first + group] = across[owner * group : (owner + 1) * group]
    for owner in range(owners):
        kv_ref[owner] = packed[owner * pad : owner * pad + 2 * group].astype(BF16)
    part = dot_nn(shard_ref[...], weight_rows(query_ref, ids_ref, tile, depth))
    query_out[...] = (query_sum[...] + part).astype(BF16)


def far_part(shard, weights, sums, ids, owners):
    rows, depth = shard.shape
    channels = weights[0].shape[1]
    group = channels // owners
    return pl.pallas_call(
        functools.partial(far_kernel, group),
        in_specs=in_vmem(7) + in_smem(1),
        out_specs=tuple(in_vmem(2)),
        out_shape=(
            jax.ShapeDtypeStruct((owners, 2 * group, rows), BF16),
            jax.ShapeDtypeStruct((rows, channels), BF16),
        ),
        scratch_shapes=[
            pltpu.VMEM((channels, rows), F32),
            pltpu.VMEM((owners * padded(2 * group), rows), F32),
        ],
        compiler_params=params(24),
        cost_estimate=call_cost(6 * rows * depth * channels, 12_000_000),
    )(shard, *weights, *sums, ids)


def grad_near_kernel(after_ref, first_ref, second_ref, third_ref, weight_ref, ids_ref, sum_ref):
    depth = first_ref.shape[1]

    def part(tile, shard_ref):
        first = pl.multiple_of(ids_ref[tile] * depth, LANE)
        return dot_nt(shard_ref[...], weight_ref[:, pl.ds(first, depth)])

    sum_ref[...] = part(0, first_ref) + part(1, second_ref) + part(2, third_ref)


def grad_near_part(after, shards, w_out, ids):
    rows, depth = shards[0].shape
    channels = w_out.shape[0]
    return pl.pallas_call(
        grad_near_kernel,
        in_specs=anywhere(1) + in_vmem(4) + in_smem(1),
        out_specs=in_vmem(1)[0],
        out_shape=jax.ShapeDtypeStruct((rows, channels), F32),
        compiler_params=params(16),
        cost_estimate=call_cost(6 * rows * depth * channels, 6_000_000),
    )(after, *shards, w_out, ids)


def grad_far_kernel(
    group, kv_ref, shard_ref, weight_ref, sum_ref, query_ref, ids_ref, gated_ref, grouped_ref,
    across,
):
    depth = shard_ref.shape[1]
    first = pl.multiple_of(ids_ref[ids_ref.shape[0] - 1] * depth, LANE)
    total = sum_ref[...] + dot_nt(shard_ref[...], weight_ref[:, pl.ds(first, depth)])
    gated = total.astype(BF16)
    gated_ref[...] = gated
    across[...] = (gated.astype(F32) * query_ref[...].astype(F32)).T
    for owner in range(grouped_ref.shape[0]):
        grouped_ref[owner, : 2 * group] = kv_ref[owner]
        grouped_ref[owner, 2 * group :] = across[owner * group : (owner + 1) * group].astype(BF16)


def grad_far_part(kv, shard, w_out, total, query, ids):
    rows, depth = shard.shape
    channels = w_out.shape[0]
    owners = kv.shape[0]
    group = channels // owners
    return pl.pallas_call(
        functools.partial(grad_far_kernel, group),
        in_specs=in_vmem(5) + in_smem(1),
        out_specs=tuple(in_vmem(2)),
        out_shape=(
            jax.ShapeDtypeStruct((rows, channels), BF16),
            jax.ShapeDtypeStruct((owners, 3 * group, rows), BF16),
        ),
        scratch_shapes=[pltpu.VMEM((channels, rows), F32)],
        compiler_params=params(16),
        cost_estimate=call_cost(2 * rows * depth * channels, 6_000_000),
    )(kv, shard, w_out, total, query, ids)


def unpack_kernel(
    group, returned_ref, query_ref, gated_ref, forward_ref, query_grad_ref, key_ref, value_ref,
    filter_ref, init_ref, response_rows, value_rows, key_rows, small_rows,
):
    owners, lines, width = returned_ref.shape
    extra = lines - 3 * group
    for owner in range(owners):
        piece = returned_ref[owner].astype(F32)
        at = slice(owner * group, (owner + 1) * group)
        response_rows[at] = piece[:group]
        value_rows[at] = piece[group : 2 * group]
        key_rows[at] = piece[2 * group : 3 * group]
        for part in range(width // LANE):
            count = min(extra, group - extra * part)
            first = owner * group + extra * part
            small_rows[first : first + count] = piece[
                3 * group : 3 * group + count, LANE * part : LANE * (part + 1)
            ]
    response = response_rows[...].T
    forward_ref[...] = (query_ref[...].astype(F32) * response).astype(BF16)
    query_grad_ref[...] = (gated_ref[...].astype(F32) * response).astype(BF16)
    value_ref[...] = value_rows[...].T.astype(BF16)
    key_ref[...] = key_rows[...].T.astype(BF16)
    small = small_rows[...].T
    taps = filter_ref.shape[0]
    filter_ref[...] = small[:taps]
    init_ref[...] = small[taps:]


def unpack_part(returned, query, gated, taps):
    rows, channels = query.shape
    short = jax.ShapeDtypeStruct((rows, channels), BF16)
    return pl.pallas_call(
        functools.partial(unpack_kernel, channels // returned.shape[0]),
        in_specs=in_vmem(3),
        out_specs=tuple(in_vmem(6)),
        out_shape=(
            short, short, short, short,
            jax.ShapeDtypeStruct((taps, channels), F32),
            jax.ShapeDtypeStruct((LANE - taps, channels), F32),
        ),
        scratch_shapes=[pltpu.VMEM((channels, rows), F32)] * 3
        + [pltpu.VMEM((channels, LANE), F32)],
        compiler_params=params(14),
        cost_estimate=call_cost(4 * rows * channels, 5_000_000),
    )(returned, query, gated)


def turn_kernel(after_ref, *refs):
    count = (len(refs) - 6) // 2
    shards, (first_out, second_out, tick_ref, first, second, sems) = refs[:-6], refs[-6:]
    tick_ref[...] = jnp.zeros_like(tick_ref)
    held = ((first, first_out), (second, second_out))
    sent = []
    for index, ref in enumerate(shards):
        which, tile = index // count, index % count
        source, target = held[which]
        source[tile] = ref[...].T
        sent.append(
            pltpu.make_async_copy(source.at[tile], target.at[tile], sems.at[which, tile])
        )
        sent[-1].start()
    for copy in sent:
        copy.wait()


def turn_part(after, first, second):
    rows, depth = first[0].shape
    count = len(first)
    out = jax.ShapeDtypeStruct((count, depth, rows), BF16)
    return pl.pallas_call(
        turn_kernel,
        in_specs=anywhere(1) + in_vmem(2 * count),
        out_specs=tuple(in_hbm(2) + in_vmem(1)),
        out_shape=(out, out, TICK),
        scratch_shapes=[pltpu.VMEM(out.shape, BF16)] * 2 + [pltpu.SemaphoreType.DMA((2, count))],
        compiler_params=params(16),
        cost_estimate=call_cost(2 * count * depth * rows, 8_000_000),
    )(after, *first, *second)


def hold_kernel(after_ref, *refs):
    count = (len(refs) - 1) // 2
    sources, targets, sems = refs[:count], refs[count:-1], refs[-1]
    copies = [
        pltpu.make_async_copy(source, target, sems.at[index])
        for index, (source, target) in enumerate(zip(sources, targets))
    ]
    for copy in copies:
        copy.start()
    for copy in copies:
        copy.wait()


def held_in_vmem(after, values):
    count = len(values)
    return pl.pallas_call(
        hold_kernel,
        in_specs=anywhere(1) + in_hbm(count),
        out_specs=tuple(in_vmem(count)),
        out_shape=tuple(jax.ShapeDtypeStruct(value.shape, value.dtype) for value in values),
        scratch_shapes=[pltpu.SemaphoreType.DMA((count,))],
        compiler_params=params(16),
        cost_estimate=call_cost(0, 26_000_000),
    )(after, *values)


def weight_kernel(
    rows, after_ref, wide_ref, narrow_ref, ids_ref, core_ref, keep_ref, send_ref, tick_ref
):
    tick_ref[...] = jnp.zeros_like(tick_ref)
    tiles = wide_ref.shape[0]
    held = keep_ref.shape[0] // tiles

    def multiply(tile):
        result = dot_nn(wide_ref[tile], narrow_ref[...]).astype(BF16)
        first = ids_ref[tile] * held
        for core in range(2):

            @pl.when(core_ref[0] == core)
            def _():
                for chip in range(held):
                    at = (2 * chip + core) * rows
                    other = (2 * chip + 1 - core) * rows
                    keep_ref[first + chip] = result[at : at + rows]
                    send_ref[first + chip] = result[other : other + rows]

    tiles_of(tiles, multiply)


def weight_partial(after, wide, ids, narrow, core, chips):
    tiles, height, depth = wide.shape
    width = narrow.shape[1]
    total = tiles * height
    rows = total // (2 * chips)
    return pl.pallas_call(
        functools.partial(weight_kernel, rows),
        in_specs=anywhere(1) + in_vmem(2) + in_smem(2),
        out_specs=tuple(in_vmem(3)),
        out_shape=(jax.ShapeDtypeStruct((chips, rows, width), BF16),) * 2 + (TICK,),
        compiler_params=params(14),
        cost_estimate=call_cost(2 * total * depth * width, 6_000_000),
    )(after, wide, narrow, ids, core)


def outward_kernel(unread, *refs):
    (
        query_ref, key_ref, value_ref, gated_ref, query_weight, key_weight, value_weight,
        out_weight, out_ref, result, sems,
    ) = refs[unread:]
    count, height, width = out_ref.shape
    rows = height // 2

    def copy_out(tile):
        return pltpu.make_async_copy(result.at[tile], out_ref.at[tile], sems.at[tile])

    def multiply(tile):
        result[tile, :rows] = dot_nn(
            gated_ref[...], out_weight[:, columns_of(tile, width)]
        ).astype(BF16)
        at = rows_of(tile, width)
        total = dot_nt(query_ref[...], query_weight[at, :])
        total += dot_nt(key_ref[...], key_weight[at, :])
        total += dot_nt(value_ref[...], value_weight[at, :])
        result[tile, rows:] = total.astype(BF16)
        copy_out(tile).start()

    tiles_of(count, multiply)
    tiles_of(count, lambda tile: copy_out(tile).wait())


def outward_part(after, backs, gated, weights, count):
    rows, depth = gated.shape
    width = weights[0].shape[0] // count
    shape = (count, 2 * rows, width)
    return pl.pallas_call(
        functools.partial(outward_kernel, len(after)),
        in_specs=anywhere(len(after)) + in_vmem(8),
        out_specs=in_hbm(1)[0],
        out_shape=jax.ShapeDtypeStruct(shape, BF16),
        scratch_shapes=[pltpu.VMEM(shape, BF16), pltpu.SemaphoreType.DMA((count,))],
        compiler_params=params(24),
        cost_estimate=call_cost(8 * rows * depth * width * count, 20_000_000),
    )(*after, *backs, gated, *weights)


def moved(value, axis, steps):
    by_core = steps if isinstance(steps, tuple) else (steps, steps)
    pairs = []
    for x in range(SIDE):
        for y in range(SIDE):
            for core in range(2):
                for z in range(SIDE):
                    goal = [x, y, core, z]
                    if axis == "core":
                        goal[2] = 1 - core
                    else:
                        at = {"x": 0, "y": 1, "z": 3}[axis]
                        goal[at] = (goal[at] + by_core[core]) % SIDE
                    pairs.append(
                        tuple(
                            ((a * SIDE + b) * 2 + c) * SIDE + d
                            for a, b, c, d in ((x, y, core, z), goal)
                        )
                    )
    return lax.ppermute(value, ("seq", "tp"), pairs)


def added(left, right):
    return (left.astype(F32) + right.astype(F32)).astype(BF16)


def picked(value, axis=0):
    return lambda index: lax.dynamic_index_in_dim(value, index, axis, keepdims=False)


def ring_sum(travelling, block, place, up, axis, steps):
    for step in steps:
        travelling = added(moved(travelling, axis, (1, -1)), block((place - step * up) % SIDE))
    return travelling


class FirstAxis:
    def __init__(self, halves, first, places, up):
        keep, came = halves
        _, rows, width = keep.shape
        grid = (SIDE, SIDE, rows, width)
        axis = "xy".index(first)
        self.keep, self.came = picked(keep.reshape(grid), axis), picked(came.reshape(grid), axis)
        self.first, self.place, self.up = first, places[first], up
        self.start = self.block((self.place - up) % SIDE)

    def block(self, index):
        return added(self.keep(index), self.came(index))

    def total(self):
        return ring_sum(
            self.start, self.block, self.place, self.up, self.first, range(2, SIDE + 1)
        )


def second_axis_sums(halves, second, places, ahead=()):
    place = places[second]

    def mine(step):
        return jnp.stack([picked(half)((place + step) % SIDE) for half in halves])

    total, *ahead = lax.optimization_barrier((mine(0).astype(F32), *ahead))
    for step in (1, -1, 2):
        steps = (2, -2) if step == 2 else step
        total += moved(mine(step), second, steps).astype(F32)
    return [total[index] for index in range(len(halves))] + ahead


def per_device(
    tokens,
    w_query,
    w_key,
    w_value,
    w_out,
    shift_filter,
    log_decay,
    readout,
    skip_gain,
    init_state,
    cotangent,
):
    row_count = tokens.shape[0]
    channels = w_query.shape[1]
    tap_count = shift_filter.shape[0]
    seq_count = lax.axis_size("seq")
    group = channels // seq_count
    position = lax.axis_index("seq")
    core = position % 2
    chip_z = lax.axis_index("tp")
    places = {"x": position // (2 * SIDE), "y": (position // 2) % SIDE}
    core_word = core.reshape(1)

    token_sides = moved(tokens, "z", 1), moved(tokens, "z", -1)
    grad_sides = moved(cotangent, "z", 1), moved(cotangent, "z", -1)

    def passed(sides):
        below, above = sides
        return jnp.where(core == 0, below, above)

    held = held_in_vmem(skip_gain, (w_key, w_value, w_query, w_out))
    tokens_on, _ = lax.optimization_barrier((passed(token_sides), held[0]))
    tokens_far = moved(tokens_on, "z", (1, -1))
    grad_sides, tokens_far = lax.optimization_barrier((grad_sides, tokens_far))
    grads_on = passed(grad_sides)
    shards = (tokens, *token_sides, tokens_far)
    grad_shards = (cotangent, *grad_sides, moved(grads_on, "z", (1, -1)))
    ids = (chip_z + jnp.array([0, SIDE - 1, 1, 2], jnp.int32)) % SIDE

    def own(value):
        return lax.dynamic_slice_in_dim(value, position * group, group, value.ndim - 1)

    own_rate, own_read, own_init, own_taps = (
        own(value).T for value in (log_decay, readout, init_state, shift_filter)
    )
    own_taps = jnp.pad(own_taps, ((0, 0), (0, LANE - tap_count)))
    taps = jnp.stack([own_taps, jnp.roll(own_taps[:, ::-1], 1, axis=1)])
    rows = jnp.stack([own_rate, own_init])
    cols = jnp.stack([own_rate, own_read])[..., None]
    skip = own(skip_gain)

    def exchanged(value):
        return lax.all_to_all(value, "seq", 0, 0, tiled=True)

    weights = held[:3]
    sums = near_part(shards[:3], weights, ids)
    grad_sum = grad_near_part(sums[2], grad_shards[:3], held[3], ids)
    kv, query = far_part(shards[3], weights, sums, ids, seq_count)
    gated_grad, packed = grad_far_part(kv, grad_shards[3], held[3], grad_sum, query, ids)
    shards_turned, grad_turned, turned = turn_part(packed, shards, grad_shards)
    results = sequence_part(turned, exchanged(packed), rows, cols, taps, skip)
    returned = exchanged(results)
    gated, back_query, back_key, back_value, grad_filter, grad_init = unpack_part(
        returned, query, gated_grad, tap_count
    )
    chips = SIDE * SIDE
    up = 1 - 2 * core

    after = gated
    swapped = []
    for wide, narrow in (
        (grad_turned, gated), (shards_turned, back_query), (shards_turned, back_key),
        (shards_turned, back_value),
    ):
        keep, send, after = weight_partial(after, wide, ids, narrow, core_word, chips)
        swapped.append((keep, moved(send, "core", 1)))
    sums = [FirstAxis(pair, first, places, up) for pair, first in zip(swapped, "xyxy")]
    outward = outward_part(
        (after,),
        (back_query, back_key, back_value),
        gated,
        (w_query, w_key, w_value, w_out),
        SIDE,
    )
    outward = lax.psum_scatter(outward, "tp", scatter_dimension=0, tiled=True)[0]
    mixed, grad_input = outward[:row_count], outward[row_count:]
    halves = [each.total() for each in sums]
    grad_out, grad_key, mixed, grad_input = second_axis_sums(
        halves[0::2], "y", places, (mixed, grad_input)
    )
    grad_query, grad_value = second_axis_sums(halves[1::2], "x", places)
    grad_out = grad_out.T
    return (mixed, grad_input, grad_query, grad_key, grad_value, grad_out, grad_filter, grad_init)


def solution(mesh):
    return jax.shard_map(
        per_device,
        mesh=mesh,
        in_specs=(
            P("seq", "tp"),
            P(None, "tp"),
            P(None, "tp"),
            P(None, "tp"),
            P("tp", None),
            P(None, "tp"),
            P(None, "tp"),
            P(None, "tp"),
            P("tp"),
            P(None, "tp"),
            P("seq", "tp"),
        ),
        out_specs=(
            P("seq", "tp"),
            P("seq", "tp"),
            P("seq", "tp"),
            P("seq", "tp"),
            P("seq", "tp"),
            P("tp", "seq"),
            P(None, "tp"),
            P(None, "tp"),
        ),
        check_vma=False,
    )
```
